32 devices in a mesh: groups: 2 (over y), seq: 4 (over z), head: 2 (over x), rep: 2 (over core).
Axes of the slice: x: 2, y: 2, z: 4, core: 2. Of those that a mesh axis runs over, the one named last changes fastest.
Arguments:
- prefix_x: bfloat16 [1024, 8192], P(('groups', 'seq'), ('head', 'rep')), parts along dimension 0, may hold values from -6 to 6
- prefix_b: bfloat16 [1024, 8, 256], P(('groups', 'seq'), ('head', 'rep')), parts along dimension 0, may hold values from -0.09375 to 0.09375
- prefix_c: bfloat16 [1024, 8, 256], P(('groups', 'seq'), ('head', 'rep')), parts along dimension 0, may hold values from -0.375 to 0.375
- prefix_decay: float32 [1024, 128], P(('groups', 'seq'), ('head', 'rep')), parts along dimension 0, may hold values from 0 to 1.5, as said below
- bypass_weight: float32 [128], replicated, may hold values from 0.1 to 1.9
- prefix_key_rows: bfloat16 [1024, 4, 128], P(('groups', 'seq'), 'head'), parts along dimension 0, may hold values from -8 to 8
- prefix_values: bfloat16 [1024, 4, 128], P(('groups', 'seq'), 'head'), parts along dimension 0, may hold values from -6 to 6
- cand_x: bfloat16 [16, 32, 8192], P(('groups', 'seq', 'rep'), None, 'head'), parts along dimension 0, may hold values from -6 to 6
- cand_b: bfloat16 [16, 32, 8, 256], P(('groups', 'seq', 'rep'), None, 'head'), parts along dimension 0, may hold values from -0.09375 to 0.09375
- cand_c: bfloat16 [16, 32, 8, 256], P(('groups', 'seq', 'rep'), None, 'head'), parts along dimension 0, may hold values from -0.375 to 0.375
- cand_decay: float32 [16, 32, 128], P(('groups', 'seq', 'rep'), None, 'head'), parts along dimension 0, may hold values from 0 to 1.5, as said below
- cand_queries: bfloat16 [16, 32, 32, 128], P(('groups', 'seq', 'rep'), None, 'head'), parts along dimension 0, may hold values from -8 to 8
- cand_keys: bfloat16 [16, 32, 4, 128], P(('groups', 'seq', 'rep'), None, 'head'), parts along dimension 0, may hold values from -16 to 16
- cand_values: bfloat16 [16, 32, 4, 128], P(('groups', 'seq', 'rep'), None, 'head'), parts along dimension 0, may hold values from -6 to 6
- cand_length: int32 [16], P(('groups', 'seq', 'rep')), parts along dimension 0, may hold values from 16 to 32
Outputs:
- prefix_out: bfloat16 [1024, 8192], P(('groups', 'seq'), ('head', 'rep')), parts along dimension 0
- cand_ssm: bfloat16 [16, 32, 8192], P(('groups', 'seq', 'rep'), None, 'head'), parts along dimension 0
- cand_attn: bfloat16 [16, 32, 32, 128], P(('groups', 'seq', 'rep'), None, 'head'), parts along dimension 0
The draws below stay inside these ranges and needn't reach their ends.
There are 2 independent parts, one for each index of `groups`. The reference program is written for one: setup_inputs(seed, part) draws one part's arguments, and reference() takes and returns one part's arrays. A program takes and returns all parts, laid end to end along the dimension named above; an argument that names none is the same for every part. Nothing has to cross between parts.
Inputs may be any that keep to these rules, and one draw needn't show every extreme that they name: `prefix_decay`: positive. `cand_decay`: positive.
All inputs are finite; a program needn't handle non-finite values.
Results may differ from the reference program's by a relative error of at most 0.008.
Values may be sent and summed in bfloat16 or wider, within the bound.
No kernel may reach another device: no remote copies, remote signals or barrier semaphores. Data moves between devices by JAX's collectives and lax.ppermute only.
A program may use at most 128 MiB of HBM per device.

```python
import jax
import jax.numpy as jnp
from jax import lax

GROUPS = 8
HEAD_DIM = 64
STATE = 256
KV_HEADS = 4
ATT_DIM = 128
TOK_DEV = 128
CT = 32
HEADS = 128
QHEADS = 32
PREFIX = 512
CANDS = 8


def decay_law(key, steps, heads, chain, lead):
    keys = jax.random.split(key, 6)
    slow = jax.random.bernoulli(keys[0], 0.5, (heads,))
    approximate_guess = jnp.exp(jax.random.uniform(keys[1], lead + (steps, heads), minval=-0.69, maxval=0.69))
    slow_rate = jnp.exp(jax.random.uniform(keys[2], (heads,), minval=jnp.log(0.05), maxval=jnp.log(0.6))) / chain
    fast_rate = jnp.exp(jax.random.uniform(keys[3], (heads,), minval=jnp.log(1.0 / 50.0), maxval=jnp.log(1.0 / 30.0)))
    forgetting_speed = jnp.where(slow, slow_rate, fast_rate)
    proposal_locations = jax.random.randint(keys[4], (2, heads), 0, steps)
    symbol_quantities = jax.random.uniform(keys[5], (2, heads), minval=0.22, maxval=0.69)
    symbol_locations = jnp.arange(steps, dtype=jnp.int32)[:, None]
    driving_signals = (symbol_locations == proposal_locations[0][None, :]) * symbol_quantities[0][None, :] + (symbol_locations == proposal_locations[1][None, :]) * symbol_quantities[1][None, :]
    return (forgetting_speed * approximate_guess + driving_signals).astype(jnp.float32)


def draw_prefix_decay(key, part):
    return decay_law(jax.random.fold_in(key, 11), PREFIX, HEADS, PREFIX, ())


def draw_cand_decay(key, part):
    return decay_law(jax.random.fold_in(key, 13), CT, HEADS, PREFIX, (CANDS,))


def draw_prefix_key_rows(key, part):
    keys = jnp.clip(jax.random.normal(jax.random.fold_in(key, 31), (PREFIX, KV_HEADS, ATT_DIM)), -8.0, 8.0)
    return keys.astype(jnp.bfloat16)


def draw_cand_queries(key, part):
    queries = jnp.clip(jax.random.normal(jax.random.fold_in(key, 37), (CANDS, CT, QHEADS, ATT_DIM)), -8.0, 8.0)
    return queries.astype(jnp.bfloat16)


def touch_ends(values, own_key, least, top_value):
    longest = values.shape.index(max(values.shape))
    spots = []
    for shift in (0, 1):
        where = [jax.random.randint(jax.random.fold_in(own_key, axis), (), 0, length) for axis, length in enumerate(values.shape)]
        where[longest] = (where[longest] + shift) % values.shape[longest]
        spots.append(tuple(where))
    return values.at[spots[0]].set(least).at[spots[1]].set(top_value)


def steps_of(key, dims, shards, low, largest):
    level, own = 1.0, jax.random.fold_in(key, 6)
    for dim, parts in shards:
        draws = jnp.exp(jax.random.uniform(jax.random.fold_in(own, dim), (parts,), jnp.float32, low / len(shards), largest / len(shards)))
        level = level * jnp.repeat(draws, dims[dim] // parts).reshape([-1 if axis == dim else 1 for axis in range(len(dims))])
    return level


def centred(key, shape, scale, reach, shards=(), kind=jnp.bfloat16):
    values = scale * jax.random.normal(key, shape, jnp.float32)
    if shards:
        values = values * steps_of(key, shape, shards, -0.22, 0.18)
    return jnp.clip(values, -reach, reach).astype(kind)


def setup_inputs(seed: int = 0, part: int = 0) -> dict:
    streams_of = jax.random.split(jax.random.key(seed), 16)
    part_keys = jax.random.split(jax.random.fold_in(streams_of[15], part), 16)
    return {
        "prefix_x": centred(part_keys[0], (PREFIX, HEADS * HEAD_DIM), 1.0, 6.0, ((0, 4), (1, 4))),
        "prefix_b": centred(part_keys[1], (PREFIX, GROUPS, STATE), (4.0 / STATE), 0.09375, ((0, 4), (1, 4))),
        "prefix_c": centred(part_keys[2], (PREFIX, GROUPS, STATE), (1.0 / STATE ** 0.5), 0.375, ((0, 4), (1, 4))),
        "prefix_decay": draw_prefix_decay(jax.random.fold_in(jax.random.fold_in(streams_of[15], part), 71), part),
        "bypass_weight": jnp.clip(1.0 + 0.18 * jax.random.normal(streams_of[4], (HEADS,), jnp.float32), 0.1, 1.9),
        "prefix_key_rows": draw_prefix_key_rows(jax.random.fold_in(jax.random.fold_in(streams_of[15], part), 71), part),
        "prefix_values": centred(part_keys[6], (PREFIX, KV_HEADS, ATT_DIM), 1.0, 6.0, ((0, 4), (1, 2))),
        "cand_x": centred(part_keys[7], (CANDS, CT, HEADS * HEAD_DIM), 1.0, 6.0, ((0, 8), (2, 2))),
        "cand_b": centred(part_keys[8], (CANDS, CT, GROUPS, STATE), (4.0 / STATE), 0.09375, ((0, 8), (2, 2))),
        "cand_c": centred(part_keys[9], (CANDS, CT, GROUPS, STATE), (1.0 / STATE ** 0.5), 0.375, ((0, 8), (2, 2))),
        "cand_decay": draw_cand_decay(jax.random.fold_in(jax.random.fold_in(streams_of[15], part), 71), part),
        "cand_queries": draw_cand_queries(jax.random.fold_in(jax.random.fold_in(streams_of[15], part), 71), part),
        "cand_keys": centred(part_keys[12], (CANDS, CT, KV_HEADS, ATT_DIM), 2.5, 16.0, ((0, 8), (2, 2))),
        "cand_values": centred(part_keys[13], (CANDS, CT, KV_HEADS, ATT_DIM), 1.0, 6.0, ((0, 8), (2, 2))),
        "cand_length": touch_ends(jax.random.randint(part_keys[14], (CANDS,), CT // 2, CT + 1), jax.random.fold_in(part_keys[14], 1), CT // 2, CT).astype(jnp.int32),
    }


EPSILON = 1e-06
HIGH = lax.Precision.HIGHEST

def summarize(x, bmat, decay):
    length, groups, state = bmat.shape
    heads = decay.shape[1]
    per_group = heads // groups
    width = x.shape[1] // heads
    cum = jnp.cumsum(decay, axis=0)
    total = jnp.exp(-cum[-1])
    weights = jnp.exp(cum[-1][None, :] - cum)
    inputs = x.reshape(length, heads, width).astype(jnp.float32)
    weighted = (inputs * weights[:, :, None]).astype(jnp.bfloat16)
    weighted = lax.optimization_barrier(weighted).astype(jnp.float32)
    weighted = weighted.reshape(length, groups, per_group, width)
    local = jnp.einsum('sgn,sgkp->gknp', bmat.astype(jnp.float32), weighted, precision=HIGH)
    return (cum, total, local.reshape(heads, state, width))

def emit(x, bmat, cmat, cum, skip, start):
    length, groups, state = bmat.shape
    heads = cum.shape[1]
    per_group = heads // groups
    width = x.shape[1] // heads
    inputs = x.reshape(length, heads, width).astype(jnp.float32)
    gram = jnp.einsum('tgn,sgn->gts', cmat.astype(jnp.float32), bmat.astype(jnp.float32), precision=HIGH)
    gram = jnp.repeat(gram, per_group, axis=0)
    causal = jnp.arange(length)[:, None] >= jnp.arange(length)[None, :]
    gap = cum.T[:, :, None] - cum.T[:, None, :]
    state_mixing = jnp.where(causal, jnp.exp(-jnp.where(causal, gap, 0.0)), 0.0) * gram
    state_mixing = lax.optimization_barrier(state_mixing.astype(jnp.bfloat16)).astype(jnp.float32)
    intra = jnp.einsum('hts,shp->thp', state_mixing, inputs, precision=HIGH)
    start_set = start.astype(jnp.float32).reshape(groups, per_group, state, width)
    carried = jnp.einsum('tgn,gknp->tgkp', cmat.astype(jnp.float32), start_set, precision=HIGH)
    carried = carried.reshape(length, heads, width)
    result = intra + jnp.exp(-cum)[:, :, None] * carried + skip[None, :, None] * inputs
    return result.reshape(length, heads * width).astype(jnp.bfloat16)

def attend(query, keys, values, own_keys, own_values):
    steps, per_kv, dim = query.shape
    rows = query.reshape(steps * per_kv, dim)
    scale = dim ** (-0.5)
    far = jnp.dot(rows, keys.T, preferred_element_type=jnp.float32) * scale
    near = jnp.dot(rows, own_keys.T, preferred_element_type=jnp.float32) * scale
    position = jnp.arange(steps * per_kv) // per_kv
    near = jnp.where(position[:, None] >= jnp.arange(steps)[None, :], near, -jnp.inf)
    top = jnp.maximum(far.max(1), near.max(1))
    far_w = jnp.exp(far - top[:, None])
    near_w = jnp.exp(near - top[:, None])
    mass = far_w.sum(1) + near_w.sum(1)
    mixed = jnp.dot(far_w.astype(jnp.bfloat16), values, preferred_element_type=jnp.float32)
    mixed = mixed + jnp.dot(near_w.astype(jnp.bfloat16), own_values, preferred_element_type=jnp.float32)
    mixed = mixed / mass[:, None]
    mixed = mixed * lax.rsqrt(lax.optimization_barrier(jnp.mean(mixed * mixed, axis=-1, keepdims=True)) + EPSILON)
    return mixed.reshape(steps, per_kv, dim)

def reference(prefix_x, prefix_b, prefix_c, prefix_decay, bypass_weight, prefix_key_rows, prefix_values, cand_x, cand_b, cand_c, cand_decay, cand_queries, cand_keys, cand_values, cand_length):
    heads = prefix_decay.shape[1]
    groups = prefix_b.shape[1]
    state = prefix_b.shape[2]
    width = prefix_x.shape[1] // heads
    count = prefix_x.shape[0] // TOK_DEV
    pieces = (prefix_x.reshape(count, TOK_DEV, heads * width), prefix_b.reshape(count, TOK_DEV, groups, state), prefix_c.reshape(count, TOK_DEV, groups, state), prefix_decay.reshape(count, TOK_DEV, heads))

    def advance(start, piece):
        xb, bb, cb, db = piece
        cum, total, local = summarize(xb, bb, db)
        out = emit(xb, bb, cb, cum, bypass_weight, start)
        return (total[:, None, None] * start + local, out)
    final, outs = lax.scan(advance, jnp.zeros((heads, state, width), jnp.float32), pieces)
    prefix_out = outs.reshape(prefix_x.shape)
    steps = cand_x.shape[1]
    valid = jnp.arange(steps)[None, :] < cand_length[:, None]

    def candidate(piece):
        xb, bb, cb, db = piece
        cum = jnp.cumsum(db, axis=0)
        return emit(xb, bb, cb, cum, bypass_weight, final)
    cand_ssm = lax.map(candidate, (cand_x, cand_b, cand_c, cand_decay))
    cand_ssm = jnp.where(valid[:, :, None], cand_ssm, jnp.zeros((), jnp.bfloat16))
    kv_heads = prefix_key_rows.shape[1]
    dim = prefix_key_rows.shape[2]
    qheads = cand_queries.shape[2]
    per_kv = qheads // kv_heads
    keys_t = prefix_key_rows.transpose(1, 0, 2)
    values_t = prefix_values.transpose(1, 0, 2)

    def one_candidate(piece):
        query, own_keys, own_values = piece
        query = query.reshape(steps, kv_heads, per_kv, dim).transpose(1, 0, 2, 3)
        heads_out = lax.map(lambda args: attend(*args), (query, keys_t, values_t, own_keys.transpose(1, 0, 2), own_values.transpose(1, 0, 2)))
        return heads_out.transpose(1, 0, 2, 3).reshape(steps, qheads, dim)
    cand_attn = lax.map(one_candidate, (cand_queries, cand_keys, cand_values))
    cand_attn = jnp.where(valid[:, :, None, None], cand_attn, 0.0).astype(jnp.bfloat16)
    return (prefix_out, cand_ssm, cand_attn)
```

```python
import functools

import jax
import jax.numpy as jnp
from jax import lax
from jax.experimental import pallas as pl
from jax.experimental.pallas import tpu as pltpu
from jax.sharding import PartitionSpec as P

EPSILON = 1e-06
NEG = -1e30
CHUNKS = 4
F32 = jnp.float32
BF16 = jnp.bfloat16


def mm(a, b):
    return lax.dot_general(a, b, (((1,), (0,)), ((), ())), preferred_element_type=F32)


def mm_nt(a, b):
    return lax.dot_general(a, b, (((1,), (1,)), ((), ())), preferred_element_type=F32)


def mm_tn(a, b):
    return lax.dot_general(a, b, (((0,), (0,)), ((), ())), preferred_element_type=F32)


def exact_nt(a, b):
    return lax.dot_general(
        a, b, (((1,), (1,)), ((), ())), preferred_element_type=F32, precision=lax.Precision.HIGHEST
    )


def exact(a, b):
    return lax.dot_general(
        a, b, (((1,), (0,)), ((), ())), preferred_element_type=F32, precision=lax.Precision.HIGHEST
    )


def iota(shape, dim):
    return lax.broadcasted_iota(jnp.int32, shape, dim)


def split3(a):
    hi = a.astype(BF16)
    rest = a - hi.astype(F32)
    mid = rest.astype(BF16)
    return hi, mid, (rest - mid.astype(F32)).astype(BF16)


def spread(a, width, first=0, count=None):
    rows, cols = a.shape
    count = cols if count is None else count
    parts = jnp.concatenate(split3(a), axis=1)
    shape = (3 * cols, count * width)
    source = iota(shape, 0)
    source = jnp.where(source >= 2 * cols, source - 2 * cols, jnp.where(source >= cols, source - cols, source))
    unit = (source == first + iota(shape, 1) // width).astype(F32).astype(BF16)
    return mm(parts, unit)


def group_of(array, g):
    return array.astype(F32)[:, g, :].astype(BF16)


def pack_kernel(c_ref, k_ref, v_ref, out_ref):
    rep = lax.axis_index("rep")
    steps, groups, state = c_ref.shape[1:]
    c = c_ref[0].astype(F32)
    for g in range(groups):
        out_ref[:steps, g * state : (g + 1) * state] = c[:, g, :].astype(BF16)
    k = k_ref[...].astype(F32)
    v = v_ref[...].astype(F32)
    tokens, heads, dim = k.shape
    kv = jnp.where(rep == 0, k, v)
    parts = groups * state // (heads * dim)
    rows = tokens // parts
    for i in range(parts):
        for j in range(heads):
            at = (i * heads + j) * dim
            out_ref[steps : steps + rows, at : at + dim] = kv[i * rows : (i + 1) * rows, j, :].astype(BF16)


def local_kernel(x_ref, b_ref, decay_t_ref, b2_ref, cum_ref, total_ref, *outs):
    local_refs, send_refs = outs[:CHUNKS], outs[CHUNKS:]
    tokens, groups, state = b_ref.shape
    heads = decay_t_ref.shape[0]
    width = x_ref.shape[1] // heads
    lower = (iota((tokens, tokens), 0) >= iota((tokens, tokens), 1)).astype(F32)
    cum = exact_nt(lower, decay_t_ref[...])
    cum_ref[...] = cum
    last = cum[tokens - 1 : tokens, :]
    total = jnp.exp(-last)
    total_ref[...] = spread(jnp.broadcast_to(total, (8, heads)), width)
    weights = spread(jnp.exp(last - cum), width)
    b = b_ref[...].astype(F32)
    for g in range(groups):
        b2_ref[:, g * state : (g + 1) * state] = b[:, g, :].astype(BF16)
    cols = x_ref.shape[1] // CHUNKS
    for q in range(CHUNKS):
        g = q * groups // CHUNKS
        at = slice(q * cols, (q + 1) * cols)
        weighted = (x_ref[:, at].astype(F32) * weights[:, at]).astype(BF16)
        local = mm_tn(b2_ref[:, g * state : (g + 1) * state], weighted)
        local_refs[q][...] = local
        send_refs[q][...] = local.astype(BF16)


def intra_kernel(x_ref, b2_ref, c_ref, cum_ref, skip_ref, c2_ref, base_ref):
    tokens, groups, state = c_ref.shape
    heads = cum_ref.shape[1]
    width = x_ref.shape[1] // heads
    per_group = heads // groups
    first = (lax.axis_index("head") * lax.axis_size("rep") + lax.axis_index("rep")) * heads
    c = c_ref[...].astype(F32)
    for g in range(groups):
        c2_ref[:, g * state : (g + 1) * state] = c[:, g, :].astype(BF16)
    skip = spread(jnp.broadcast_to(skip_ref[...], (8, skip_ref.shape[1])), width, first, heads)[:1]
    cum = cum_ref[...]
    cum_t = cum.T
    shape = (tokens, tokens)
    hidden = jnp.where(iota(shape, 0) >= iota(shape, 1), 0.0, NEG)
    pair = 2 * width
    lane = iota((tokens, pair), 1)
    for g in range(groups):
        here = slice(g * state, (g + 1) * state)
        gram = mm_nt(c2_ref[:, here], b2_ref[:, here])
        for h in range(g * per_group, (g + 1) * per_group, 2):
            mixing = []
            for i in (h, h + 1):
                gap = cum_t[i : i + 1, :] - jnp.broadcast_to(cum[:, i : i + 1], shape)
                mixing.append((jnp.exp(gap + hidden) * gram).astype(BF16))
            at = slice(h * width, (h + 2) * width)
            x = x_ref[:, at]
            zero = jnp.zeros_like(x)
            inputs = jnp.concatenate(
                [jnp.where(lane < width, x, zero), jnp.where(lane < width, zero, x)], axis=0
            )
            base_ref[:, at] = mm(jnp.concatenate(mixing, axis=1), inputs) + skip[:, at] * x.astype(F32)


def cand_kernel(x_ref, b_ref, c_ref, decay_ref, skip_ref, base_ref, fade_ref):
    steps, groups, state = b_ref.shape[1:]
    heads = decay_ref.shape[2]
    width = x_ref.shape[2] // heads
    per_group = heads // groups
    first = lax.axis_index("head") * heads
    skip = spread(jnp.broadcast_to(skip_ref[...], (8, skip_ref.shape[1])), width, first, heads)[:1]
    lower = (iota((steps, steps), 0) >= iota((steps, steps), 1)).astype(F32)
    cum = exact(lower, decay_ref[0])
    fade_ref[...] = spread(jnp.exp(-cum), width)
    wide = (steps, heads * steps)
    cum_t = spread(cum, steps)
    place = iota(wide, 1) % steps
    row = iota(wide, 0)
    cum_s = jnp.sum(jnp.where(row == place, cum_t, 0.0), axis=0, keepdims=True)
    fall = jnp.exp(jnp.where(row >= place, cum_s - cum_t, NEG))
    b = b_ref[0].astype(F32)
    c = c_ref[0].astype(F32)
    quad = 128 // steps
    shape = (quad * steps, quad * width)
    mine = iota(shape, 0) // steps == iota(shape, 1) // width
    for g in range(groups):
        b_g = b[:, g, :].astype(BF16)
        gram = mm_nt(c[:, g, :].astype(BF16), jnp.concatenate([b_g] * quad, axis=0))
        for h in range(g * per_group, (g + 1) * per_group, quad):
            mixing = (fall[:, h * steps : (h + quad) * steps] * gram).astype(BF16)
            at = slice(h * width, (h + quad) * width)
            x = x_ref[0, :, at]
            tall = jnp.concatenate([x] * quad, axis=0)
            inputs = jnp.where(mine, tall, jnp.zeros_like(tall))
            base_ref[:, at] = mm(mixing, inputs) + skip[:, at] * x.astype(F32)


def attend_kernel(length_ref, q_ref, own_k_ref, own_v_ref, *refs):
    packets, out_ref = refs[:-1], refs[-1]
    count = len(packets) // 2
    rep = lax.axis_index("rep")
    steps, heads, dim = q_ref.shape[1:]
    kv_heads = own_k_ref.shape[2]
    per_kv = heads // kv_heads
    rows = steps * per_kv
    keys, values = [], []
    for d in range(count):
        mine, other = packets[d][steps:, :], packets[count + d][steps:, :]
        keys.append(jnp.where(rep == 0, mine, other))
        values.append(jnp.where(rep == 0, other, mine))
    parts = packets[0].shape[1] // (kv_heads * dim)
    q = q_ref[0].astype(F32)
    own_k = own_k_ref[0].astype(F32)
    own_v = own_v_ref[0].astype(F32)
    scale = dim ** (-0.5)
    step_of = iota((rows, steps), 0) // per_kv
    visible = step_of >= iota((rows, steps), 1)
    live = iota((rows, dim), 0) // per_kv < length_ref[0]
    mixed_of = []
    for j in range(kv_heads):
        query = q[:, j * per_kv : (j + 1) * per_kv, :].reshape(rows, dim).astype(BF16)

        def gather(arrays):
            return jnp.concatenate(
                [a[:, (i * kv_heads + j) * dim : (i * kv_heads + j + 1) * dim] for a in arrays for i in range(parts)],
                axis=0,
            )

        far = mm_nt(query, gather(keys)) * scale
        near = jnp.where(visible, mm_nt(query, own_k[:, j, :].astype(BF16)) * scale, NEG)
        top = jnp.maximum(jnp.max(far, axis=1, keepdims=True), jnp.max(near, axis=1, keepdims=True))
        far = jnp.exp(far - top)
        near = jnp.exp(near - top)
        mass = jnp.sum(far, axis=1, keepdims=True) + jnp.sum(near, axis=1, keepdims=True)
        mixed = mm(far.astype(BF16), gather(values)) + mm(near.astype(BF16), own_v[:, j, :].astype(BF16))
        mixed = mixed / mass
        mixed = mixed * lax.rsqrt(jnp.mean(mixed * mixed, axis=1, keepdims=True) + EPSILON)
        mixed = jnp.where(live, mixed, 0.0)
        mixed_of.append(mixed.reshape(steps, per_kv, dim))
    out_ref[0] = (jnp.concatenate(mixed_of, axis=1) if kv_heads > 1 else mixed_of[0]).astype(BF16)


def both_candidates(mine_ref, other_ref, groups, state):
    rep = lax.axis_index("rep")
    steps = mine_ref.shape[0] // 2
    mine, other = mine_ref[:steps, :], other_ref[:steps, :]
    zero, one = jnp.where(rep == 0, mine, other), jnp.where(rep == 0, other, mine)
    half = groups * state
    pick = [jnp.where(rep == 0, a[:, :half], a[:, half : 2 * half]) for a in (zero, one)]
    return jnp.concatenate(pick, axis=0)


def share_kernel(total_ref, *refs, groups):
    count = (len(refs) - CHUNKS) // 3
    send_refs = refs[:CHUNKS]
    mine_refs, other_refs = refs[CHUNKS : CHUNKS + count], refs[CHUNKS + count : CHUNKS + 2 * count]
    out_refs = refs[CHUNKS + 2 * count :]
    state, cols = send_refs[0].shape
    projections = [both_candidates(m, o, groups, state) for m, o in zip(mine_refs, other_refs)]
    rows = projections[0].shape[0]
    for q in range(CHUNKS):
        g = q * groups // CHUNKS
        at = slice(q * cols, (q + 1) * cols)
        stacked = jnp.concatenate([p[:, g * state : (g + 1) * state] for p in projections], axis=0)
        result = mm(stacked, send_refs[q][...])
        out_refs[0][:, at] = result[:rows]
        for d in range(1, count):
            out_refs[d][:rows, at] = result[d * rows : (d + 1) * rows].astype(BF16)
    hi, mid, lo = [a.astype(F32) for a in split3(total_ref[...])]
    line = iota(hi.shape, 0)
    tail = jnp.where(line == 0, hi, jnp.where(line == 1, mid, jnp.where(line == 2, lo, 0.0)))
    tail = jnp.concatenate([tail, jnp.zeros_like(tail)], axis=0).astype(BF16)
    for d in range(1, count):
        out_refs[d][rows:, :] = tail


def carry_kernel(cum_ref, base_ref, c2_ref, total_ref, mine_ref, other_ref, own_ref, *refs, groups, hops):
    size = lax.axis_size("seq")
    place = lax.axis_index("seq")
    rep = lax.axis_index("rep")
    received, refs = refs[: CHUNKS * hops], refs[CHUNKS * hops :]
    shares, (out_ref, keep_ref, give_ref) = refs[:-3], refs[-3:]
    state, cols = received[0].shape
    heads = cum_ref.shape[1]
    width = base_ref.shape[1] // heads
    fade = spread(jnp.exp(-cum_ref[...]), width)
    projections = both_candidates(mine_ref, other_ref, groups, state)
    rows = projections.shape[0]
    tokens = c2_ref.shape[0]
    for q in range(CHUNKS):
        g = q * groups // CHUNKS
        at = slice(q * cols, (q + 1) * cols)
        here = slice(g * state, (g + 1) * state)
        start = received[q][...]
        for i in range(1, hops):
            start = start + received[i * CHUNKS + q][...]
        carried = mm(jnp.concatenate([c2_ref[:, here], projections[:, here]], axis=0), start)
        out_ref[:, at] = (base_ref[:, at] + fade[:, at] * carried[:tokens]).astype(BF16)
        acc = total_ref[:1, at] * carried[tokens:] + own_ref[:, at]
        for d in range(1, size):
            share = shares[d - 1]
            tail = share[rows:, at].astype(F32)
            total = tail[0:1] + tail[1:2] + tail[2:3]
            total = jnp.where(place + d < size, total, 1.0)
            acc = acc * total + share[:rows, at].astype(F32)
        half = rows // 2
        keep_ref[:, at] = jnp.where(rep == 0, acc[:half], acc[half:])
        give_ref[:, at] = jnp.where(rep == 0, acc[half:], acc[:half]).astype(BF16)


def close_kernel(length_ref, base_ref, fade_ref, keep_ref, got_ref, out_ref):
    rep = lax.axis_index("rep")
    keep, got = keep_ref[...], got_ref[...].astype(F32)
    cols = keep.shape[1]
    live = iota(keep.shape, 0) < length_ref[0]
    for i in range(2):
        at = slice(i * cols, (i + 1) * cols)
        carried = jnp.where(rep == i, keep, got)
        result = base_ref[:, at] + fade_ref[:, at] * carried
        out_ref[0, :, at] = jnp.where(live, result, 0.0).astype(BF16)


def call(kernel, name, outs, *args, flops=1e8, scalars=0):
    shapes = [jax.ShapeDtypeStruct(shape, dtype) for shape, dtype in outs]
    moved = sum(a.size * a.dtype.itemsize for a in args) + sum(s.size * s.dtype.itemsize for s in shapes)
    vmem = pl.BlockSpec(memory_space=pltpu.VMEM)
    smem = pl.BlockSpec(memory_space=pltpu.SMEM)
    return pl.pallas_call(
        kernel,
        out_shape=shapes,
        in_specs=[smem] * scalars + [vmem] * (len(args) - scalars),
        out_specs=[vmem] * len(shapes),
        compiler_params=pltpu.CompilerParams(vmem_limit_bytes=32 * 2**20),
        cost_estimate=pl.CostEstimate(flops=int(flops), bytes_accessed=int(moved), transcendentals=0),
        name=name,
    )(*args)


def on_device(
    prefix_x,
    prefix_b,
    prefix_c,
    prefix_decay,
    bypass_weight,
    prefix_key_rows,
    prefix_values,
    cand_x,
    cand_b,
    cand_c,
    cand_decay,
    cand_queries,
    cand_keys,
    cand_values,
    cand_length,
):
    size = lax.axis_size("seq")
    hops = size - 1
    tokens, groups, state = prefix_b.shape
    heads = prefix_decay.shape[1]
    wide = prefix_x.shape[1]
    steps = cand_x.shape[1]
    cand_wide = cand_x.shape[2]
    cand_groups = cand_b.shape[2]
    cols = wide // CHUNKS
    swap = [(0, 1), (1, 0)]
    skip = bypass_weight.reshape(1, -1)

    (packet,) = call(
        pack_kernel, "pack", [((2 * steps, cand_groups * state), BF16)], cand_c, prefix_key_rows, prefix_values
    )
    mine = [packet] + [
        lax.ppermute(packet, "seq", [(i, (i + d) % size) for i in range(size)]) for d in range(1, size)
    ]
    b2, cum, total, *parts = call(
        local_kernel,
        "local_state",
        [((tokens, groups * state), BF16), ((tokens, heads), F32), ((8, wide), F32)]
        + [((state, cols), F32)] * CHUNKS
        + [((state, cols), BF16)] * CHUNKS,
        prefix_x,
        prefix_b,
        prefix_decay.T,
    )
    local, send = parts[:CHUNKS], parts[CHUNKS:]
    received = []
    sent = send
    for hop in range(hops):
        got = [lax.ppermute(a, "seq", [(hop, hop + 1)]) for a in sent]
        received += got
        sent = [
            (total[:1, q * cols : (q + 1) * cols] * got[q].astype(F32) + local[q]).astype(BF16)
            for q in range(CHUNKS)
        ]
    other = [lax.ppermute(p, "rep", swap) for p in mine]
    own, *shares = call(
        functools.partial(share_kernel, groups=groups),
        "shares",
        [((2 * steps, wide), F32)] + [((2 * steps + 16, wide), BF16)] * hops,
        total,
        *send,
        *mine,
        *other,
    )
    back = [
        lax.ppermute(shares[d - 1], "seq", [(i, i - d) for i in range(d, size)]) for d in range(1, size)
    ]
    c2, base = call(
        intra_kernel,
        "intra",
        [((tokens, groups * state), BF16), ((tokens, wide), F32)],
        prefix_x,
        b2,
        prefix_c,
        cum,
        skip,
    )
    cand_base, cand_fade = call(
        cand_kernel,
        "candidates",
        [((steps, cand_wide), F32), ((steps, cand_wide), F32)],
        cand_x,
        cand_b,
        cand_c,
        cand_decay,
        skip,
    )
    (cand_attn,) = call(
        attend_kernel,
        "attend",
        [(cand_queries.shape, BF16)],
        cand_length,
        cand_queries,
        cand_keys,
        cand_values,
        *mine,
        *other,
        scalars=1,
    )
    prefix_out, keep, give = call(
        functools.partial(carry_kernel, groups=groups, hops=hops),
        "carried",
        [((tokens, wide), BF16), ((steps, wide), F32), ((steps, wide), BF16)],
        cum,
        base,
        c2,
        total,
        mine[0],
        other[0],
        own,
        *received,
        *back,
    )
    (cand_ssm,) = call(
        close_kernel,
        "close",
        [((1, steps, cand_wide), BF16)],
        cand_length,
        cand_base,
        cand_fade,
        keep,
        lax.ppermute(give, "rep", swap),
        scalars=1,
    )
    return (prefix_out, cand_ssm, cand_attn)


def solution(mesh):
    placed = (
        P(("groups", "seq"), ("head", "rep")),
        P(("groups", "seq"), ("head", "rep"), None),
        P(("groups", "seq"), ("head", "rep"), None),
        P(("groups", "seq"), ("head", "rep")),
        P(),
        P(("groups", "seq"), "head", None),
        P(("groups", "seq"), "head", None),
        P(("groups", "seq", "rep"), None, "head"),
        P(("groups", "seq", "rep"), None, "head", None),
        P(("groups", "seq", "rep"), None, "head", None),
        P(("groups", "seq", "rep"), None, "head"),
        P(("groups", "seq", "rep"), None, "head", None),
        P(("groups", "seq", "rep"), None, "head", None),
        P(("groups", "seq", "rep"), None, "head", None),
        P(("groups", "seq", "rep")),
    )
    return jax.shard_map(
        on_device,
        mesh=mesh,
        in_specs=placed,
        out_specs=(
            P(("groups", "seq"), ("head", "rep")),
            P(("groups", "seq", "rep"), None, "head"),
            P(("groups", "seq", "rep"), None, "head", None),
        ),
        check_vma=False,
    )
```

```python
import functools

import jax
import jax.numpy as jnp
from jax import lax
from jax.experimental import pallas as pl
from jax.experimental.pallas import tpu as pltpu
from jax.sharding import PartitionSpec as P

EPSILON = 1e-06
NEG = -1e30
CHUNKS = 4
F32 = jnp.float32
BF16 = jnp.bfloat16


def mm(a, b):
    return lax.dot_general(a, b, (((1,), (0,)), ((), ())), preferred_element_type=F32)


def mm_nt(a, b):
    return lax.dot_general(a, b, (((1,), (1,)), ((), ())), preferred_element_type=F32)


def mm_tn(a, b):
    return lax.dot_general(a, b, (((0,), (0,)), ((), ())), preferred_element_type=F32)


def exact_nt(a, b):
    return lax.dot_general(
        a, b, (((1,), (1,)), ((), ())), preferred_element_type=F32, precision=lax.Precision.HIGHEST
    )


def exact(a, b):
    return lax.dot_general(
        a, b, (((1,), (0,)), ((), ())), preferred_element_type=F32, precision=lax.Precision.HIGHEST
    )


def iota(shape, dim):
    return lax.broadcasted_iota(jnp.int32, shape, dim)


def split3(a):
    hi = a.astype(BF16)
    rest = a - hi.astype(F32)
    mid = rest.astype(BF16)
    return hi, mid, (rest - mid.astype(F32)).astype(BF16)


def spread(a, width, first=0, count=None):
    rows, cols = a.shape
    count = cols if count is None else count
    parts = jnp.concatenate(split3(a), axis=1)
    shape = (3 * cols, count * width)
    source = iota(shape, 0)
    source = jnp.where(source >= 2 * cols, source - 2 * cols, jnp.where(source >= cols, source - cols, source))
    unit = (source == first + iota(shape, 1) // width).astype(F32).astype(BF16)
    return mm(parts, unit)


def group_of(array, g):
    return array.astype(F32)[:, g, :].astype(BF16)


def payload_plan(groups):
    of = [q * groups // CHUNKS for q in range(CHUNKS)]
    plan, seen = [], set()
    for chunks in ([0], [1], list(range(2, CHUNKS))):
        fresh = [g for g in sorted({of[q] for q in chunks}) if g not in seen]
        seen |= set(fresh)
        plan.append((chunks, fresh))
    return plan


def totals_to_lines(total):
    hi, mid, lo = [a.astype(F32) for a in split3(jnp.broadcast_to(total, (16, total.shape[1])))]
    line = iota(hi.shape, 0)
    return jnp.where(line == 0, hi, jnp.where(line == 1, mid, jnp.where(line == 2, lo, 0.0))).astype(BF16)


def lines_to_totals(lines):
    lines = lines.astype(F32)
    return lines[0:1] + lines[1:2] + lines[2:3]


def as_row(total, width):
    return spread(jnp.broadcast_to(total, (8, total.shape[1])), width)


def local_kernel(x_ref, b_ref, decay_t_ref, b2_ref, cum_ref, total_ref, *outs):
    local_refs, load_refs = outs[:CHUNKS], outs[CHUNKS:]
    tokens, groups, state = b_ref.shape
    heads = decay_t_ref.shape[0]
    width = x_ref.shape[1] // heads
    lower = (iota((tokens, tokens), 0) >= iota((tokens, tokens), 1)).astype(F32)
    cum = exact_nt(lower, decay_t_ref[...])
    cum_ref[...] = cum
    last = cum[tokens - 1 : tokens, :]
    weights = spread(jnp.exp(last - cum), width)
    b = b_ref[...].astype(F32)
    for g in range(groups):
        b2_ref[:, g * state : (g + 1) * state] = b[:, g, :].astype(BF16)
    cols = x_ref.shape[1] // CHUNKS
    for (chunks, fresh), load in zip(payload_plan(groups), load_refs):
        for i, q in enumerate(chunks):
            g = q * groups // CHUNKS
            at = slice(q * cols, (q + 1) * cols)
            weighted = (x_ref[:, at].astype(F32) * weights[:, at]).astype(BF16)
            load[:tokens, i * cols : (i + 1) * cols] = weighted
            local_refs[q][...] = mm_tn(b2_ref[:, g * state : (g + 1) * state], weighted)
        for i, g in enumerate(fresh):
            at = len(chunks) * cols + i * state
            load[:tokens, at : at + state] = b2_ref[:, g * state : (g + 1) * state]
    load = load_refs[0]
    load[tokens:, :] = jnp.zeros((16, load.shape[1]), BF16)
    total = jnp.exp(-last)
    total_ref[...] = jnp.broadcast_to(total, (8, heads))
    load[tokens:, :heads] = totals_to_lines(total)


def pack_kernel(k_ref, v_ref, out_ref):
    rep = lax.axis_index("rep")
    tokens, heads, dim = k_ref.shape
    kv = jnp.where(rep == 0, k_ref[...].astype(F32), v_ref[...].astype(F32))
    rows, wide = out_ref.shape
    for i in range(wide // (heads * dim)):
        for j in range(heads):
            at = (i * heads + j) * dim
            out_ref[:, at : at + dim] = kv[i * rows : (i + 1) * rows, j, :].astype(BF16)


def collect_kernel(*refs):
    out_ref = refs[-1]
    at = 0
    for ref in refs[:-1]:
        out_ref[at : at + ref.shape[0], :] = ref[...]
        at += ref.shape[0]


def half_of(place, level):
    odd = lax.rem(place, 2)
    return jnp.where(lax.rem(lax.div(place, 2**level), 2) == 0, 1 - odd, odd)


def merge_kernel(*refs, level, last, chunks, cols, groups, heads, tokens, carry):
    refs = list(refs)

    def take(count):
        taken = refs[:count]
        del refs[:count]
        return taken

    place = lax.axis_index("seq")
    right = lax.rem(lax.div(place, 2**level), 2) == 1
    width = cols * CHUNKS // heads
    first = 0 in chunks
    outs = []
    others = []
    if level == 0:
        for q in chunks:
            w_ref, b_ref = take(2)
            at_w, at_b = carry[q]
            others.append(mm_tn(b_ref[:tokens, at_b], w_ref[:tokens, at_w]))
    else:
        half = half_of(place, level)
        for q in chunks:
            near_ref, far_ref = take(2)
            rows = near_ref.shape[0] - 16 if q == 0 else near_ref.shape[0]
            near, far = near_ref[:rows, :], far_ref[:rows, :]
            pieces = [jnp.where(half == 0, near, far), jnp.where(half == 0, far, near)]
            others.append(jnp.concatenate(pieces, axis=1).astype(F32))
    if first:
        mine_ref, lines_ref = take(2)
        mine = mine_ref[:1, :]
        theirs = lines_to_totals(lines_ref[lines_ref.shape[0] - 16 :, :heads])
        later = as_row(jnp.where(right, mine, theirs), width)
        pair = mine * theirs
        if level == 0:
            before = jnp.ones_like(mine)
        else:
            before = take(1)[0][:1, :]
        before_row = as_row(before, width)
        before = jnp.where(right, before * theirs, before)
        outs += [later, before_row, jnp.broadcast_to(pair, (8, heads)), jnp.broadcast_to(before, (8, heads))]
    else:
        later_ref, before_ref = take(2)
        later, before_row = later_ref[...], before_ref[...]
    for q, other in zip(chunks, others, strict=True):
        at = slice(q * cols, (q + 1) * cols)
        own = take(1)[0][...]
        earlier, following = jnp.where(right, other, own), jnp.where(right, own, other)
        joined = later[:1, at] * earlier + following
        if level == 0:
            start = jnp.where(right, other, 0.0)
        else:
            start = take(1)[0][...]
            start = jnp.where(right, before_row[:1, at] * other + start, start)
        if not last:
            send = jnp.where(half_of(place, level + 1) == 0, joined[:, : cols // 2], joined[:, cols // 2 :]).astype(BF16)
            if q == 0:
                tail = jnp.zeros((16, cols // 2 - heads), BF16)
                lines = jnp.concatenate([totals_to_lines(pair), tail], axis=1)
                send = jnp.concatenate([send, lines], axis=0)
            outs += [joined, start, send]
        else:
            c2_ref, mine_c_ref, base_ref, cum_ref = take(4)
            state = own.shape[0]
            g = q * groups // CHUNKS
            here = slice(g * state, (g + 1) * state)
            fade = spread(jnp.exp(-cum_ref[...]), width, q * heads // CHUNKS, heads // CHUNKS)
            carried = mm(c2_ref[:, here], start.astype(BF16))
            outs.append((base_ref[:, at] + fade * carried).astype(BF16))
            outs.append(mm(mine_c_ref[:, here], joined.astype(BF16)))
    if last and CHUNKS - 1 in chunks:
        parts = take(2 * (CHUNKS - 1))
        out_parts = [ref[...] for ref in parts[: CHUNKS - 1]] + [outs[-2]]
        raws = [ref[...] for ref in parts[CHUNKS - 1 :]] + [outs[-1]]
        rep = lax.axis_index("rep")
        out_ref, keep_ref, give_ref = refs
        rows = keep_ref.shape[0]
        for q in range(CHUNKS):
            at = slice(q * cols, (q + 1) * cols)
            out_ref[:, at] = out_parts[q]
            keep_ref[:, at] = jnp.where(rep == 0, raws[q][:rows], raws[q][rows:])
            give_ref[:, at] = jnp.where(rep == 0, raws[q][rows:], raws[q][:rows]).astype(BF16)
    else:
        for ref, value in zip(refs, outs, strict=True):
            ref[...] = value


def projections_kernel(mine_ref, other_ref, out_ref):
    rep = lax.axis_index("rep")
    steps, all_groups, state = mine_ref.shape[1:]
    groups = all_groups // 2
    mine, other = mine_ref[0].astype(F32), other_ref[0].astype(F32)
    zero, one = jnp.where(rep == 0, mine, other), jnp.where(rep == 0, other, mine)
    for i, c in enumerate((zero, one)):
        for g in range(groups):
            part = jnp.where(rep == 0, c[:, g, :], c[:, groups + g, :])
            out_ref[i * steps : (i + 1) * steps, g * state : (g + 1) * state] = part.astype(BF16)


def intra_kernel(x_ref, b2_ref, c_ref, cum_ref, skip_ref, c2_ref, base_ref):
    tokens, groups, state = c_ref.shape
    heads = cum_ref.shape[1]
    width = x_ref.shape[1] // heads
    per_group = heads // groups
    first = (lax.axis_index("head") * lax.axis_size("rep") + lax.axis_index("rep")) * heads
    c = c_ref[...].astype(F32)
    for g in range(groups):
        c2_ref[:, g * state : (g + 1) * state] = c[:, g, :].astype(BF16)
    skip = spread(jnp.broadcast_to(skip_ref[...], (8, skip_ref.shape[1])), width, first, heads)[:1]
    cum = cum_ref[...]
    cum_t = cum.T
    shape = (tokens, tokens)
    hidden = jnp.where(iota(shape, 0) >= iota(shape, 1), 0.0, NEG)
    pair = 2 * width
    lane = iota((tokens, pair), 1)
    for g in range(groups):
        here = slice(g * state, (g + 1) * state)
        gram = mm_nt(c2_ref[:, here], b2_ref[:, here])
        for h in range(g * per_group, (g + 1) * per_group, 2):
            mixing = []
            for i in (h, h + 1):
                gap = cum_t[i : i + 1, :] - jnp.broadcast_to(cum[:, i : i + 1], shape)
                mixing.append((jnp.exp(gap + hidden) * gram).astype(BF16))
            at = slice(h * width, (h + 2) * width)
            x = x_ref[:, at]
            zero = jnp.zeros_like(x)
            inputs = jnp.concatenate(
                [jnp.where(lane < width, x, zero), jnp.where(lane < width, zero, x)], axis=0
            )
            base_ref[:, at] = mm(jnp.concatenate(mixing, axis=1), inputs) + skip[:, at] * x.astype(F32)


def cand_kernel(x_ref, b_ref, c_ref, decay_ref, skip_ref, base_ref, fade_ref):
    steps, groups, state = b_ref.shape[1:]
    heads = decay_ref.shape[2]
    width = x_ref.shape[2] // heads
    per_group = heads // groups
    first = lax.axis_index("head") * heads
    skip = spread(jnp.broadcast_to(skip_ref[...], (8, skip_ref.shape[1])), width, first, heads)[:1]
    lower = (iota((steps, steps), 0) >= iota((steps, steps), 1)).astype(F32)
    cum = exact(lower, decay_ref[0])
    fade_ref[...] = spread(jnp.exp(-cum), width)
    wide = (steps, heads * steps)
    cum_t = spread(cum, steps)
    place = iota(wide, 1) % steps
    row = iota(wide, 0)
    cum_s = jnp.sum(jnp.where(row == place, cum_t, 0.0), axis=0, keepdims=True)
    fall = jnp.exp(jnp.where(row >= place, cum_s - cum_t, NEG))
    b = b_ref[0].astype(F32)
    c = c_ref[0].astype(F32)
    quad = 128 // steps
    shape = (quad * steps, quad * width)
    mine = iota(shape, 0) // steps == iota(shape, 1) // width
    for g in range(groups):
        b_g = b[:, g, :].astype(BF16)
        gram = mm_nt(c[:, g, :].astype(BF16), jnp.concatenate([b_g] * quad, axis=0))
        for h in range(g * per_group, (g + 1) * per_group, quad):
            mixing = (fall[:, h * steps : (h + quad) * steps] * gram).astype(BF16)
            at = slice(h * width, (h + quad) * width)
            x = x_ref[0, :, at]
            tall = jnp.concatenate([x] * quad, axis=0)
            inputs = jnp.where(mine, tall, jnp.zeros_like(tall))
            base_ref[:, at] = mm(mixing, inputs) + skip[:, at] * x.astype(F32)


def attend_kernel(length_ref, q_ref, own_k_ref, own_v_ref, k_ref, v_ref, mine_ref, other_ref, *refs):
    out_ref = refs[-1]
    rep = lax.axis_index("rep")
    steps, heads, dim = q_ref.shape[1:]
    kv_heads = own_k_ref.shape[2]
    per_kv = heads // kv_heads
    rows = steps * per_kv
    mine, other = mine_ref[...], other_ref[...]
    keys, values = jnp.where(rep == 0, mine, other), jnp.where(rep == 0, other, mine)
    parts = mine.shape[1] // (kv_heads * dim)
    q = q_ref[0].astype(F32)
    own_k = own_k_ref[0].astype(F32)
    own_v = own_v_ref[0].astype(F32)
    block_k = k_ref[...].astype(F32)
    block_v = v_ref[...].astype(F32)
    scale = dim ** (-0.5)
    step_of = iota((rows, steps), 0) // per_kv
    visible = step_of >= iota((rows, steps), 1)
    live = iota((rows, dim), 0) // per_kv < length_ref[0]
    mixed_of = []
    for j in range(kv_heads):
        query = q[:, j * per_kv : (j + 1) * per_kv, :].reshape(rows, dim).astype(BF16)

        def gather(far, block):
            pieces = [far[:, (i * kv_heads + j) * dim : (i * kv_heads + j + 1) * dim] for i in range(parts)]
            return jnp.concatenate([*pieces, block[:, j, :].astype(BF16)], axis=0)

        far = mm_nt(query, gather(keys, block_k)) * scale
        near = jnp.where(visible, mm_nt(query, own_k[:, j, :].astype(BF16)) * scale, NEG)
        top = jnp.maximum(jnp.max(far, axis=1, keepdims=True), jnp.max(near, axis=1, keepdims=True))
        far = jnp.exp(far - top)
        near = jnp.exp(near - top)
        mass = jnp.sum(far, axis=1, keepdims=True) + jnp.sum(near, axis=1, keepdims=True)
        mixed = mm(far.astype(BF16), gather(values, block_v)) + mm(near.astype(BF16), own_v[:, j, :].astype(BF16))
        mixed = mixed / mass
        mixed = mixed * lax.rsqrt(jnp.mean(mixed * mixed, axis=1, keepdims=True) + EPSILON)
        mixed = jnp.where(live, mixed, 0.0)
        mixed_of.append(mixed.reshape(steps, per_kv, dim))
    out_ref[0] = (jnp.concatenate(mixed_of, axis=1) if kv_heads > 1 else mixed_of[0]).astype(BF16)


def close_kernel(length_ref, base_ref, fade_ref, keep_ref, got_ref, out_ref):
    rep = lax.axis_index("rep")
    keep, got = keep_ref[...], got_ref[...].astype(F32)
    cols = keep.shape[1]
    live = iota(keep.shape, 0) < length_ref[0]
    for i in range(2):
        at = slice(i * cols, (i + 1) * cols)
        carried = jnp.where(rep == i, keep, got)
        result = base_ref[:, at] + fade_ref[:, at] * carried
        out_ref[0, :, at] = jnp.where(live, result, 0.0).astype(BF16)


def call(kernel, name, outs, *args, scalars=0, after=()):
    shapes = [jax.ShapeDtypeStruct(shape, dtype) for shape, dtype in outs]
    moved = sum(a.size * a.dtype.itemsize for a in args) + sum(s.size * s.dtype.itemsize for s in shapes)
    vmem = pl.BlockSpec(memory_space=pltpu.VMEM)
    smem = pl.BlockSpec(memory_space=pltpu.SMEM)
    count, rest = len(args), len(args) + len(after)

    def body(*refs):
        kernel(*refs[:count], *refs[rest:])

    return pl.pallas_call(
        body,
        out_shape=shapes,
        in_specs=[smem] * scalars + [vmem] * (count - scalars) + [pl.BlockSpec(memory_space=pl.ANY)] * len(after),
        out_specs=[vmem] * len(shapes),
        compiler_params=pltpu.CompilerParams(vmem_limit_bytes=32 * 2**20),
        cost_estimate=pl.CostEstimate(flops=10**8, bytes_accessed=int(moved), transcendentals=0),
        name=name,
    )(*args, *after)


def on_device(
    prefix_x,
    prefix_b,
    prefix_c,
    prefix_decay,
    bypass_weight,
    prefix_key_rows,
    prefix_values,
    cand_x,
    cand_b,
    cand_c,
    cand_decay,
    cand_queries,
    cand_keys,
    cand_values,
    cand_length,
):
    size = lax.axis_size("seq")
    levels = size.bit_length() - 1
    assert size == 2**levels and lax.axis_size("rep") == 2
    tokens, groups, state = prefix_b.shape
    heads = prefix_decay.shape[1]
    wide = prefix_x.shape[1]
    steps = cand_x.shape[1]
    cand_wide = cand_x.shape[2]
    cols = wide // CHUNKS
    skip = bypass_weight.reshape(1, -1)
    plan = payload_plan(groups)

    def to_core(array):
        return lax.ppermute(array, "rep", [(0, 1), (1, 0)])

    def to_neighbour(array):
        return lax.ppermute(array, "seq", [(i, i ^ 1) for i in range(size)])

    def to_mirror(array, level):
        return lax.ppermute(array, "seq", [(i, i ^ (2 ** (level + 1) - 1)) for i in range(size)])

    other_c = to_core(cand_c)
    b2, cum, total, *parts = call(
        local_kernel,
        "local_state",
        [((tokens, groups * state), BF16), ((tokens, heads), F32), ((8, heads), F32)]
        + [((state, cols), F32)] * CHUNKS
        + [
            ((tokens + (16 if p == 0 else 0), len(chunks) * cols + len(fresh) * state), BF16)
            for p, (chunks, fresh) in enumerate(plan)
        ],
        prefix_x,
        prefix_b,
        prefix_decay.T,
    )
    local, loads = parts[:CHUNKS], parts[CHUNKS:]
    got = [to_neighbour(a) for a in loads]
    kv_rows = prefix_key_rows.size // (groups * state)
    (kv,) = call(
        pack_kernel, "pack", [((kv_rows, groups * state), BF16)], prefix_key_rows, prefix_values, after=(loads[0],)
    )
    halves = [kv, to_neighbour(kv)]
    for level in range(1, levels):
        mirrored = to_mirror(halves[0], level)
        halves = [halves[0], halves[1], mirrored, to_neighbour(mirrored)]
        if level < levels - 1:
            halves = [jnp.concatenate([halves[0], halves[2]]), jnp.concatenate([halves[1], halves[3]])]
    c2, base = call(
        intra_kernel,
        "intra",
        [((tokens, groups * state), BF16), ((tokens, wide), F32)],
        prefix_x,
        b2,
        prefix_c,
        cum,
        skip,
        after=(kv,),
    )
    (both_c,) = call(
        projections_kernel, "projections", [((2 * steps, groups * state), BF16)], cand_c, other_c, after=(base,)
    )
    where = {}
    spot = {}
    for p, (chunks, fresh) in enumerate(plan):
        for i, g in enumerate(fresh):
            at = len(chunks) * cols + i * state
            where[g] = (p, slice(at, at + state))
        for i, q in enumerate(chunks):
            spot[q] = (p, slice(i * cols, (i + 1) * cols))
    mark = both_c
    own, start = dict(enumerate(local)), {}
    before = None
    near, far = {}, {}
    cand_base = cand_attn = None
    out_parts, raws = [], []

    def attend(mark):
        (mine,) = call(
            collect_kernel,
            "collect",
            [((kv_rows * (size - 1), groups * state), BF16)],
            *halves[1:],
            after=(mark,),
        )
        return call(
            attend_kernel,
            "attend",
            [(cand_queries.shape, BF16)],
            cand_length,
            cand_queries,
            cand_keys,
            cand_values,
            prefix_key_rows,
            prefix_values,
            mine,
            to_core(mine),
            scalars=1,
        )[0]

    for level in range(levels):
        last = level == levels - 1
        rows = None
        for batch in [chunks for chunks, _ in plan] if level == 0 else [[q] for q in range(CHUNKS)]:
            args, outs = [], []
            if level == 0:
                for q in batch:
                    args += [got[spot[q][0]], got[where[q * groups // CHUNKS][0]]]
                lines = got[0]
            else:
                for q in batch:
                    args += [near[q], far[q]]
                lines = near.get(0)
            if 0 in batch:
                args += [total, lines] + ([] if level == 0 else [before])
                outs += [((8, wide), F32)] * 2 + [((8, heads), F32)] * 2
            else:
                args += rows
            for q in batch:
                args += [own[q]] + ([] if level == 0 else [start[q]])
                if last:
                    args += [c2, both_c, base, cum]
                    outs += [((tokens, cols), BF16), ((2 * steps, cols), F32)]
                else:
                    outs += [((state, cols), F32)] * 2
                    outs += [((state + (16 if q == 0 else 0), cols // 2), BF16)]
            if last and batch == [CHUNKS - 1]:
                args += out_parts + raws
                outs = [((tokens, wide), BF16), ((steps, wide), F32), ((steps, wide), BF16)]
            results = list(
                call(
                    functools.partial(
                        merge_kernel,
                        level=level,
                        last=last,
                        chunks=batch,
                        cols=cols,
                        groups=groups,
                        heads=heads,
                        tokens=tokens,
                        carry={q: (spot[q][1], where[q * groups // CHUNKS][1]) for q in batch},
                    ),
                    "merge",
                    outs,
                    *args,
                    after=(mark,),
                )
            )
            mark = results[0]
            if last and batch == [CHUNKS - 1]:
                prefix_out, keep, give = results
                continue
            if 0 in batch:
                rows, results = results[:2], results[2:]
                total, before = results[:2]
                results = results[2:]
            for q in batch:
                if last:
                    out_parts.append(results.pop(0))
                    raws.append(results.pop(0))
                else:
                    own[q], start[q], sent = results[:3]
                    results = results[3:]
                    near[q] = to_mirror(sent, level + 1)
                    far[q] = to_neighbour(near[q])
            if level == 0 and 0 in batch:
                cand_base, cand_fade = call(
                    cand_kernel,
                    "candidates",
                    [((steps, cand_wide), F32), ((steps, cand_wide), F32)],
                    cand_x,
                    cand_b,
                    cand_c,
                    cand_decay,
                    skip,
                    after=(mark,),
                )
                mark = cand_base
        if level == 0:
            cand_attn = attend(mark)
            mark = cand_attn
    (cand_ssm,) = call(
        close_kernel,
        "close",
        [((1, steps, cand_wide), BF16)],
        cand_length,
        cand_base,
        cand_fade,
        keep,
        to_core(give),
        scalars=1,
    )
    return (prefix_out, cand_ssm, cand_attn)


def solution(mesh):
    placed = (
        P(("groups", "seq"), ("head", "rep")),
        P(("groups", "seq"), ("head", "rep"), None),
        P(("groups", "seq"), ("head", "rep"), None),
        P(("groups", "seq"), ("head", "rep")),
        P(),
        P(("groups", "seq"), "head", None),
        P(("groups", "seq"), "head", None),
        P(("groups", "seq", "rep"), None, "head"),
        P(("groups", "seq", "rep"), None, "head", None),
        P(("groups", "seq", "rep"), None, "head", None),
        P(("groups", "seq", "rep"), None, "head"),
        P(("groups", "seq", "rep"), None, "head", None),
        P(("groups", "seq", "rep"), None, "head", None),
        P(("groups", "seq", "rep"), None, "head", None),
        P(("groups", "seq", "rep")),
    )
    return jax.shard_map(
        on_device,
        mesh=mesh,
        in_specs=placed,
        out_specs=(
            P(("groups", "seq"), ("head", "rep")),
            P(("groups", "seq", "rep"), None, "head"),
            P(("groups", "seq", "rep"), None, "head", None),
        ),
        check_vma=False,
    )
```

```python
import functools

import jax
import jax.numpy as jnp
from jax import lax
from jax.experimental import pallas as pl
from jax.experimental.pallas import tpu as pltpu
from jax.sharding import PartitionSpec as P

EPSILON = 1e-06
NEG = -1e30
CHUNKS = 4
SECOND_COST = 1.0
FIRST_COST = 2.0
F32 = jnp.float32
BF16 = jnp.bfloat16


def mm(a, b):
    return lax.dot_general(a, b, (((1,), (0,)), ((), ())), preferred_element_type=F32)


def mm_nt(a, b):
    return lax.dot_general(a, b, (((1,), (1,)), ((), ())), preferred_element_type=F32)


def mm_tn(a, b):
    return lax.dot_general(a, b, (((0,), (0,)), ((), ())), preferred_element_type=F32)


def exact_nt(a, b):
    return lax.dot_general(
        a, b, (((1,), (1,)), ((), ())), preferred_element_type=F32, precision=lax.Precision.HIGHEST
    )


def exact(a, b):
    return lax.dot_general(
        a, b, (((1,), (0,)), ((), ())), preferred_element_type=F32, precision=lax.Precision.HIGHEST
    )


def iota(shape, dim):
    return lax.broadcasted_iota(jnp.int32, shape, dim)


def split3(a):
    hi = a.astype(BF16)
    rest = a - hi.astype(F32)
    mid = rest.astype(BF16)
    return hi, mid, (rest - mid.astype(F32)).astype(BF16)


def spread(a, width, first=0, count=None):
    rows, cols = a.shape
    count = cols if count is None else count
    parts = jnp.concatenate(split3(a), axis=1)
    shape = (3 * cols, count * width)
    source = iota(shape, 0)
    source = jnp.where(source >= 2 * cols, source - 2 * cols, jnp.where(source >= cols, source - cols, source))
    unit = (source == first + iota(shape, 1) // width).astype(F32).astype(BF16)
    return mm(parts, unit)


def group_of(array, g):
    return array.astype(F32)[:, g, :].astype(BF16)


def payload_plan(groups):
    of = [q * groups // CHUNKS for q in range(CHUNKS)]
    return [([g] if g not in of[:q] else []) for q, g in enumerate(of)]


def totals_to_lines(total):
    hi, mid, lo = [a.astype(F32) for a in split3(jnp.broadcast_to(total, (16, total.shape[1])))]
    line = iota(hi.shape, 0)
    return jnp.where(line == 0, hi, jnp.where(line == 1, mid, jnp.where(line == 2, lo, 0.0))).astype(BF16)


def lines_to_totals(lines):
    lines = lines.astype(F32)
    return lines[0:1] + lines[1:2] + lines[2:3]


def as_row(total, width):
    return spread(jnp.broadcast_to(total, (8, total.shape[1])), width)


def pack(k_ref, v_ref):
    rep = lax.axis_index("rep")
    kv = jnp.where(rep == 0, k_ref[...].astype(F32), v_ref[...].astype(F32))
    return jnp.concatenate([kv[:, j, :] for j in range(kv.shape[1])], axis=1).astype(BF16)


def head_kernel(x_any, b_any, decay_t_any, cum_ref, total_ref, load_ref, x_ref, b_ref, decay_t_ref, sems):
    tokens, groups, state = b_ref.shape
    heads = decay_t_ref.shape[0]
    cols = x_ref.shape[1]
    width = cols * CHUNKS // heads
    copies = [
        pltpu.make_async_copy(source, target, sems.at[i])
        for i, (source, target) in enumerate(
            ((decay_t_any, decay_t_ref), (x_any.at[:, pl.ds(0, cols)], x_ref), (b_any, b_ref))
        )
    ]
    for copy in copies:
        copy.start()
    copies[0].wait()
    lower = (iota((tokens, tokens), 0) >= iota((tokens, tokens), 1)).astype(F32)
    cum = exact_nt(lower, decay_t_ref[...])
    cum_ref[...] = cum
    last = cum[tokens - 1 : tokens, :]
    total = jnp.exp(-last)
    total_ref[...] = jnp.broadcast_to(total, (8, heads))
    load_ref[tokens:, :] = jnp.zeros((16, load_ref.shape[1]), BF16)
    load_ref[tokens:, :heads] = totals_to_lines(total)
    weights = spread(jnp.exp(last - cum), width, 0, heads // CHUNKS)
    copies[1].wait()
    load_ref[:tokens, :cols] = (x_ref[...].astype(F32) * weights).astype(BF16)
    copies[2].wait()
    load_ref[:tokens, cols:] = b_ref[...].astype(F32)[:, 0, :].astype(BF16)


def local_kernel(x_ref, b_ref, cum_ref, first_ref, k_ref, v_ref, b2_ref, kv_ref, *outs):
    local_refs, load_refs = outs[:CHUNKS], outs[CHUNKS:]
    tokens, groups, state = b_ref.shape
    heads = cum_ref.shape[1]
    width = x_ref.shape[1] // heads
    cols = x_ref.shape[1] // CHUNKS
    cum = cum_ref[...]
    weights = spread(jnp.exp(cum[tokens - 1 : tokens, :] - cum), width)
    b = b_ref[...].astype(F32)
    for g in range(groups):
        b2_ref[:, g * state : (g + 1) * state] = b[:, g, :].astype(BF16)
    kv = pack(k_ref, v_ref)
    kv_ref[...] = kv
    for q, fresh in enumerate(payload_plan(groups)):
        g = q * groups // CHUNKS
        at = slice(q * cols, (q + 1) * cols)
        if q == 0:
            weighted = first_ref[:tokens, :cols]
        else:
            weighted = (x_ref[:, at].astype(F32) * weights[:, at]).astype(BF16)
            load = load_refs[q - 1]
            load[:, :cols] = weighted
            if fresh:
                load[:, cols : cols + state] = b2_ref[:, g * state : (g + 1) * state]
            if q == 1:
                load[:, load.shape[1] - kv.shape[1] :] = kv
        local_refs[q][...] = mm_tn(b2_ref[:, g * state : (g + 1) * state], weighted)


def collect_kernel(*refs, inner):
    refs, out_ref = list(refs[:-1]), refs[-1]
    place = lax.axis_index("seq")
    pieces = [ref[...] for ref in refs]
    if inner:
        second = pieces.pop()
        pieces[-1] = jnp.where((place == 1) | (place == 2), pieces[-1], second)
        pieces[0] = pieces[0][pieces[0].shape[0] // 2 :]
    at = 0
    for piece in pieces:
        out_ref[at : at + piece.shape[0], :] = piece
        at += piece.shape[0]


def half_of(place, level):
    odd = lax.rem(place, 2)
    return jnp.where(lax.rem(lax.div(place, 2**level), 2) == 0, 1 - odd, odd)


def merge_kernel(*refs, level, last, chunks, cols, groups, heads, tokens, state):
    refs = list(refs)

    def take(count):
        taken = refs[:count]
        del refs[:count]
        return taken

    place = lax.axis_index("seq")
    right = lax.rem(lax.div(place, 2**level), 2) == 1
    width = cols * CHUNKS // heads
    first = 0 in chunks
    outs = []
    others = []
    if level == 0:
        for q in chunks:
            w_ref, b_ref = take(2)
            others.append(mm_tn(b_ref[:tokens, cols : cols + state], w_ref[:tokens, :cols]))
    else:
        half = half_of(place, level)
        for q in chunks:
            near_ref, far_ref = take(2)
            rows = near_ref.shape[0] - 16 if q == 0 else near_ref.shape[0]
            near, far = near_ref[:rows, :], far_ref[:rows, :]
            pieces = [jnp.where(half == 0, near, far), jnp.where(half == 0, far, near)]
            others.append(jnp.concatenate(pieces, axis=1).astype(F32))
    if first:
        mine_ref, lines_ref = take(2)
        mine = mine_ref[:1, :]
        theirs = lines_to_totals(lines_ref[lines_ref.shape[0] - 16 :, :heads])
        later = as_row(jnp.where(right, mine, theirs), width)
        pair = mine * theirs
        if level == 0:
            before = jnp.ones_like(mine)
        else:
            before = take(1)[0][:1, :]
        before_row = as_row(before, width)
        before = jnp.where(right, before * theirs, before)
        outs += [later, before_row, jnp.broadcast_to(pair, (8, heads)), jnp.broadcast_to(before, (8, heads))]
    else:
        later_ref, before_ref = take(2)
        later, before_row = later_ref[...], before_ref[...]
    for q, other in zip(chunks, others, strict=True):
        at = slice(q * cols, (q + 1) * cols)
        own = take(1)[0][...]
        earlier, following = jnp.where(right, other, own), jnp.where(right, own, other)
        joined = later[:1, at] * earlier + following
        if level == 0:
            start = jnp.where(right, other, 0.0)
        else:
            start = take(1)[0][...]
            start = jnp.where(right, before_row[:1, at] * other + start, start)
        if not last:
            send = jnp.where(half_of(place, level + 1) == 0, joined[:, : cols // 2], joined[:, cols // 2 :]).astype(BF16)
            if q == 0:
                tail = jnp.zeros((16, cols // 2 - heads), BF16)
                lines = jnp.concatenate([totals_to_lines(pair), tail], axis=1)
                send = jnp.concatenate([send, lines], axis=0)
            outs += [joined, start, send]
        else:
            cc_ref, base_ref, cum_ref = take(3)
            g = q * groups // CHUNKS
            here = slice(g * state, (g + 1) * state)
            fade = spread(jnp.exp(-cum_ref[...]), width, q * heads // CHUNKS, heads // CHUNKS)
            carried = mm(cc_ref[:tokens, here], start.astype(BF16))
            outs.append((base_ref[:, at] + fade * carried).astype(BF16))
            outs.append(mm(cc_ref[tokens:, here], joined.astype(BF16)))
    if last and CHUNKS - 1 in chunks:
        parts = take(2 * (CHUNKS - 1))
        out_parts = [ref[...] for ref in parts[: CHUNKS - 1]] + [outs[-2]]
        raws = [ref[...] for ref in parts[CHUNKS - 1 :]] + [outs[-1]]
        rep = lax.axis_index("rep")
        out_ref, keep_ref, give_ref = refs
        rows = keep_ref.shape[0]
        for q in range(CHUNKS):
            at = slice(q * cols, (q + 1) * cols)
            out_ref[:, at] = out_parts[q]
            keep_ref[:, at] = jnp.where(rep == 0, raws[q][:rows], raws[q][rows:])
            give_ref[:, at] = jnp.where(rep == 0, raws[q][rows:], raws[q][:rows]).astype(BF16)
    else:
        for ref, value in zip(refs, outs, strict=True):
            ref[...] = value


def projections_kernel(c_ref, mine_ref, other_ref, out_ref):
    rep = lax.axis_index("rep")
    tokens, groups, state = c_ref.shape
    steps = mine_ref.shape[1]
    mine, other = mine_ref[0].astype(F32), other_ref[0].astype(F32)
    zero, one = jnp.where(rep == 0, mine, other), jnp.where(rep == 0, other, mine)
    prefix = c_ref[...].astype(F32)
    for g in range(groups):
        at = slice(g * state, (g + 1) * state)
        out_ref[:tokens, at] = prefix[:, g, :].astype(BF16)
        for i, c in enumerate((zero, one)):
            part = jnp.where(rep == 0, c[:, g, :], c[:, groups + g, :])
            out_ref[tokens + i * steps : tokens + (i + 1) * steps, at] = part.astype(BF16)


def first_kernel(*refs, q, cols, groups, heads, tokens, state):
    refs = list(refs)
    w_ref, b_ref, local_ref = refs[:3]
    left = lax.axis_index("seq") < 2
    width = cols * CHUNKS // heads
    other = mm_tn(b_ref[:tokens, cols : cols + state], w_ref[:tokens, :cols])
    if q == 0:
        mine_ref, own_row_ref, near_row_ref, near_ref, other_ref, send_ref = refs[3:]
        mine = mine_ref[:1, :]
        near = lines_to_totals(w_ref[tokens:, :heads])
        own_row, near_row = as_row(mine, width), as_row(near, width)
        own_row_ref[...] = own_row
        near_row_ref[...] = near_row
        near_ref[...] = jnp.broadcast_to(near, (8, heads))
        send_ref[state:, :] = jnp.zeros((16, cols), BF16)
        send_ref[state:, :heads] = totals_to_lines(mine * near)
    else:
        own_row_ref, near_row_ref = refs[3:5]
        refs = refs[5:]
        if q == 1:
            kv_ref, pair_ref = refs[0], refs.pop()
            refs = refs[1:]
            pair_ref[:tokens, :] = kv_ref[...]
            pair_ref[tokens:, :] = w_ref[:, w_ref.shape[1] - kv_ref.shape[1] :]
        other_ref, send_ref = refs
        own_row, near_row = own_row_ref[...], near_row_ref[...]
    at = slice(q * cols, (q + 1) * cols)
    local = local_ref[...]
    after = own_row[:1, at] * other + local
    beyond = other + near_row[:1, at] * local
    send_ref[:state, :] = jnp.where(left, after, beyond).astype(BF16)
    other_ref[...] = other


def second_kernel(*refs, q, cols, groups, heads, tokens, state):
    refs = list(refs)
    got_ref, other_ref, local_ref, own_row_ref, cc_ref, near_cc_ref = refs[:6]
    place = lax.axis_index("seq")
    left, inner = place < 2, (place == 1) | (place == 2)
    width = cols * CHUNKS // heads
    at = slice(q * cols, (q + 1) * cols)
    g = q * groups // CHUNKS
    here = slice(g * state, (g + 1) * state)
    rows = cc_ref.shape[0]
    if q == 0:
        mine_ref, near_ref, later_row_ref, carried_ref, cand_ref, send_ref = refs[6:]
        later = jnp.where(left, lines_to_totals(got_ref[state:, :heads]), near_ref[:1, :])
        later_row = as_row(later, width)
        later_row_ref[...] = later_row
        send_ref[rows:, :] = jnp.zeros((16, cols), BF16)
        send_ref[rows:, :heads] = totals_to_lines(later * mine_ref[:1, :])
    else:
        later_row_ref, carried_ref, cand_ref, send_ref = refs[6:]
        later_row = later_row_ref[...]
    got, other, local = got_ref[:state, :].astype(F32), other_ref[...], local_ref[...]
    start, beyond = jnp.where(left, other, got), jnp.where(left, got, other)
    start = jnp.where(inner, start, 0.0)
    after = own_row_ref[:1, at] * start + local
    lasting = later_row[:1, at]
    state_out = jnp.where(left, beyond + lasting * local, after)
    send_ref[:rows, :] = mm(near_cc_ref[:, here], state_out.astype(BF16)).astype(BF16)
    final = jnp.where(inner, lasting * after + beyond, local)
    carried_ref[...] = mm(cc_ref[:tokens, here], start.astype(BF16))
    cand_ref[...] = mm(cc_ref[tokens:, here], final.astype(BF16))


def third_kernel(*refs, q, cols, heads, tokens):
    refs = list(refs)
    got_ref, carried_ref, cand_ref, base_ref, cum_ref, own_row_ref = refs[:6]
    place = lax.axis_index("seq")
    width = cols * CHUNKS // heads
    at = slice(q * cols, (q + 1) * cols)
    rows = cand_ref.shape[0]
    refs = refs[6:]
    if q == 0:
        later_row_ref = refs[0]
        later_row = as_row(lines_to_totals(got_ref[tokens + rows :, :heads]), width)
        later_row_ref[...] = later_row
    else:
        later_row = refs[0][...]
    refs = refs[1:]
    fade = spread(jnp.exp(-cum_ref[...]), width, q * heads // CHUNKS, heads // CHUNKS)
    got = got_ref[: tokens + rows, :].astype(F32)
    carried = jnp.where(place == 3, got[:tokens], carried_ref[...])
    cand = cand_ref[...]
    cand = jnp.where(
        place == 3,
        own_row_ref[:1, at] * got[tokens:] + cand,
        jnp.where(place == 0, later_row[:1, at] * cand + got[tokens:], cand),
    )
    out = (base_ref[:, at] + fade * carried).astype(BF16)
    if q < CHUNKS - 1:
        out_ref, raw_ref = refs
        out_ref[...] = out
        raw_ref[...] = cand
        return
    outs, raws, (out_ref, keep_ref, give_ref) = refs[: CHUNKS - 1], refs[CHUNKS - 1 : 2 * CHUNKS - 2], refs[-3:]
    rep = lax.axis_index("rep")
    half = rows // 2
    for i in range(CHUNKS):
        at = slice(i * cols, (i + 1) * cols)
        out_ref[:, at] = out if i == q else outs[i][...]
        raw = cand if i == q else raws[i][...]
        keep_ref[:, at] = jnp.where(rep == 0, raw[:half], raw[half:])
        give_ref[:, at] = jnp.where(rep == 0, raw[half:], raw[:half]).astype(BF16)


def intra_kernel(x_ref, b2_ref, c2_ref, cum_ref, skip_ref, base_ref, *, groups):
    tokens, heads = cum_ref.shape
    width = x_ref.shape[1] // heads
    state = c2_ref.shape[1] // groups
    per_group = heads // groups
    first = (lax.axis_index("head") * lax.axis_size("rep") + lax.axis_index("rep")) * heads
    skip = spread(jnp.broadcast_to(skip_ref[...], (8, skip_ref.shape[1])), width, first, heads)[:1]
    cum = cum_ref[...]
    cum_t = cum.T
    shape = (tokens, tokens)
    hidden = jnp.where(iota(shape, 0) >= iota(shape, 1), 0.0, NEG)
    pair = 2 * width
    lane = iota((tokens, pair), 1)
    for g in range(groups):
        here = slice(g * state, (g + 1) * state)
        gram = mm_nt(c2_ref[:tokens, here], b2_ref[:, here])
        for h in range(g * per_group, (g + 1) * per_group, 2):
            mixing = []
            for i in (h, h + 1):
                gap = cum_t[i : i + 1, :] - jnp.broadcast_to(cum[:, i : i + 1], shape)
                mixing.append((jnp.exp(gap + hidden) * gram).astype(BF16))
            at = slice(h * width, (h + 2) * width)
            x = x_ref[:, at]
            zero = jnp.zeros_like(x)
            inputs = jnp.concatenate(
                [jnp.where(lane < width, x, zero), jnp.where(lane < width, zero, x)], axis=0
            )
            base_ref[:, at] = mm(jnp.concatenate(mixing, axis=1), inputs) + skip[:, at] * x.astype(F32)


def cand_kernel(x_ref, b_ref, c_ref, decay_ref, skip_ref, base_ref, fade_ref):
    steps, groups, state = b_ref.shape[1:]
    heads = decay_ref.shape[2]
    width = x_ref.shape[2] // heads
    per_group = heads // groups
    first = lax.axis_index("head") * heads
    skip = spread(jnp.broadcast_to(skip_ref[...], (8, skip_ref.shape[1])), width, first, heads)[:1]
    lower = (iota((steps, steps), 0) >= iota((steps, steps), 1)).astype(F32)
    cum = exact(lower, decay_ref[0])
    fade_ref[...] = spread(jnp.exp(-cum), width)
    wide = (steps, heads * steps)
    cum_t = spread(cum, steps)
    place = iota(wide, 1) % steps
    row = iota(wide, 0)
    cum_s = jnp.sum(jnp.where(row == place, cum_t, 0.0), axis=0, keepdims=True)
    fall = jnp.exp(jnp.where(row >= place, cum_s - cum_t, NEG))
    b = b_ref[0].astype(F32)
    c = c_ref[0].astype(F32)
    quad = 128 // steps
    shape = (quad * steps, quad * width)
    mine = iota(shape, 0) // steps == iota(shape, 1) // width
    for g in range(groups):
        b_g = b[:, g, :].astype(BF16)
        gram = mm_nt(c[:, g, :].astype(BF16), jnp.concatenate([b_g] * quad, axis=0))
        for h in range(g * per_group, (g + 1) * per_group, quad):
            mixing = (fall[:, h * steps : (h + quad) * steps] * gram).astype(BF16)
            at = slice(h * width, (h + quad) * width)
            x = x_ref[0, :, at]
            tall = jnp.concatenate([x] * quad, axis=0)
            inputs = jnp.where(mine, tall, jnp.zeros_like(tall))
            base_ref[:, at] = mm(mixing, inputs) + skip[:, at] * x.astype(F32)


def attend_kernel(length_ref, q_ref, own_k_ref, own_v_ref, k_ref, v_ref, mine_ref, other_ref, *refs):
    out_ref = refs[-1]
    rep = lax.axis_index("rep")
    steps, heads, dim = q_ref.shape[1:]
    kv_heads = own_k_ref.shape[2]
    per_kv = heads // kv_heads
    rows = steps * per_kv
    mine, other = mine_ref[...], other_ref[...]
    keys, values = jnp.where(rep == 0, mine, other), jnp.where(rep == 0, other, mine)
    q = q_ref[0].astype(F32)
    own_k = own_k_ref[0].astype(F32)
    own_v = own_v_ref[0].astype(F32)
    block_k = k_ref[...].astype(F32)
    block_v = v_ref[...].astype(F32)
    scale = dim ** (-0.5)
    step_of = iota((rows, steps), 0) // per_kv
    visible = step_of >= iota((rows, steps), 1)
    live = iota((rows, dim), 0) // per_kv < length_ref[0]
    mixed_of = []
    for j in range(kv_heads):
        query = q[:, j * per_kv : (j + 1) * per_kv, :].reshape(rows, dim).astype(BF16)

        def gather(far, block):
            return jnp.concatenate([far[:, j * dim : (j + 1) * dim], block[:, j, :].astype(BF16)], axis=0)

        far = mm_nt(query, gather(keys, block_k)) * scale
        near = jnp.where(visible, mm_nt(query, own_k[:, j, :].astype(BF16)) * scale, NEG)
        top = jnp.maximum(jnp.max(far, axis=1, keepdims=True), jnp.max(near, axis=1, keepdims=True))
        far = jnp.exp(far - top)
        near = jnp.exp(near - top)
        mass = jnp.sum(far, axis=1, keepdims=True) + jnp.sum(near, axis=1, keepdims=True)
        mixed = mm(far.astype(BF16), gather(values, block_v)) + mm(near.astype(BF16), own_v[:, j, :].astype(BF16))
        mixed = mixed / mass
        mixed = mixed * lax.rsqrt(jnp.mean(mixed * mixed, axis=1, keepdims=True) + EPSILON)
        mixed = jnp.where(live, mixed, 0.0)
        mixed_of.append(mixed.reshape(steps, per_kv, dim))
    out_ref[0] = (jnp.concatenate(mixed_of, axis=1) if kv_heads > 1 else mixed_of[0]).astype(BF16)


def close_kernel(length_ref, base_ref, fade_ref, keep_ref, got_ref, out_ref):
    rep = lax.axis_index("rep")
    keep, got = keep_ref[...], got_ref[...].astype(F32)
    cols = keep.shape[1]
    live = iota(keep.shape, 0) < length_ref[0]
    for i in range(2):
        at = slice(i * cols, (i + 1) * cols)
        carried = jnp.where(rep == i, keep, got)
        result = base_ref[:, at] + fade_ref[:, at] * carried
        out_ref[0, :, at] = jnp.where(live, result, 0.0).astype(BF16)


def call(kernel, name, outs, *args, scalars=0, after=(), cost=0.0, scratch=(), limit=32):
    shapes = [jax.ShapeDtypeStruct(shape, dtype) for shape, dtype in outs]
    vmem = pl.BlockSpec(memory_space=pltpu.VMEM)
    smem = pl.BlockSpec(memory_space=pltpu.SMEM)
    count, rest = len(args), len(args) + len(after)
    out_spec = vmem
    if scratch:
        vmem = pl.BlockSpec(memory_space=pl.ANY)

    def body(*refs):
        kernel(*refs[:count], *refs[rest:])

    return pl.pallas_call(
        body,
        out_shape=shapes,
        in_specs=[smem] * scalars + [vmem] * (count - scalars) + [pl.BlockSpec(memory_space=pl.ANY)] * len(after),
        out_specs=[out_spec] * len(shapes),
        scratch_shapes=list(scratch),
        compiler_params=pltpu.CompilerParams(vmem_limit_bytes=limit * 2**20),
        cost_estimate=pl.CostEstimate(flops=int(cost * 10**9), bytes_accessed=0, transcendentals=0),
        name=name,
    )(*args, *after)


def on_device(
    prefix_x,
    prefix_b,
    prefix_c,
    prefix_decay,
    bypass_weight,
    prefix_key_rows,
    prefix_values,
    cand_x,
    cand_b,
    cand_c,
    cand_decay,
    cand_queries,
    cand_keys,
    cand_values,
    cand_length,
):
    size = lax.axis_size("seq")
    levels = size.bit_length() - 1
    assert size == 2**levels and lax.axis_size("rep") == 2
    tokens, groups, state = prefix_b.shape
    heads = prefix_decay.shape[1]
    wide = prefix_x.shape[1]
    steps = cand_x.shape[1]
    cand_wide = cand_x.shape[2]
    cols = wide // CHUNKS
    skip = bypass_weight.reshape(1, -1)
    plan = payload_plan(groups)

    def to_core(array):
        return lax.ppermute(array, "rep", [(0, 1), (1, 0)])

    def to_neighbour(array):
        return lax.ppermute(array, "seq", [(i, i ^ 1) for i in range(size)])

    def to_mirror(array, level):
        return lax.ppermute(array, "seq", [(i, i ^ (2 ** (level + 1) - 1)) for i in range(size)])

    def between_inner(array):
        far = {1: 2, 2: 1}
        pairs = [(2 * i + r, 2 * far[i] + r if i in far else 2 * i + 1 - r) for i in range(size) for r in range(2)]
        return lax.ppermute(array, ("seq", "rep"), pairs)

    other_c = to_core(cand_c)
    kv_shape = (tokens, prefix_key_rows.shape[1] * prefix_key_rows.shape[2])
    cum, total, load = call(
        head_kernel,
        "head",
        [((tokens, heads), F32), ((8, heads), F32), ((tokens + 16, cols + state), BF16)],
        prefix_x,
        prefix_b,
        prefix_decay.T,
        scratch=[
            pltpu.VMEM((tokens, cols), BF16),
            pltpu.VMEM(prefix_b.shape, BF16),
            pltpu.VMEM((heads, tokens), F32),
            pltpu.SemaphoreType.DMA((3,)),
        ],
        limit=60,
    )
    b2, kv, *parts = call(
        local_kernel,
        "local_state",
        [((tokens, groups * state), BF16), (kv_shape, BF16)]
        + [((state, cols), F32)] * CHUNKS
        + [
            ((tokens, cols + len(fresh) * state + (kv_shape[1] if q == 1 else 0)), BF16)
            for q, fresh in enumerate(plan)
            if q
        ],
        prefix_x,
        prefix_b,
        cum,
        load,
        prefix_key_rows,
        prefix_values,
    )
    local, loads = parts[:CHUNKS], [load] + parts[CHUNKS:]
    got = [to_neighbour(a) for a in loads]
    first_of = {g: q for q, fresh in enumerate(plan) for g in fresh}
    (cc,) = call(
        projections_kernel,
        "projections",
        [((tokens + 2 * steps, groups * state), BF16)],
        prefix_c,
        cand_c,
        other_c,
        after=(kv,),
    )

    def intra(mark):
        return call(
            functools.partial(intra_kernel, groups=groups),
            "intra",
            [((tokens, wide), F32)],
            prefix_x,
            b2,
            cc,
            cum,
            skip,
            after=(mark,),
        )[0]

    def candidates(mark):
        return call(
            cand_kernel,
            "candidates",
            [((steps, cand_wide), F32), ((steps, cand_wide), F32)],
            cand_x,
            cand_b,
            cand_c,
            cand_decay,
            skip,
            after=(mark,),
        )

    def attend(mark, pieces, inner):
        (mine,) = call(
            functools.partial(collect_kernel, inner=inner),
            "collect",
            [((tokens * (size - 1), kv_shape[1]), BF16)],
            *pieces,
            after=(mark,),
        )
        theirs = to_core(mine)

        def finish(mark):
            return call(
                attend_kernel,
                "attend",
                [(cand_queries.shape, BF16)],
                cand_length,
                cand_queries,
                cand_keys,
                cand_values,
                prefix_key_rows,
                prefix_values,
                mine,
                theirs,
                scalars=1,
                after=(mark,),
            )[0]

        return mine, finish

    shared = dict(cols=cols, heads=heads, tokens=tokens)
    if size == 4:
        near_cc = to_neighbour(cc)
        other, middle, carried, cands, outer, outs, raws = {}, {}, {}, {}, {}, [], []
        rows = {}

        def first(q, mark):
            extra = [((8, wide), F32), ((8, wide), F32), ((8, heads), F32)] if q == 0 else []
            results = call(
                functools.partial(first_kernel, q=q, groups=groups, state=state, **shared),
                "first",
                extra
                + [((state, cols), F32), ((state + (16 if q == 0 else 0), cols), BF16)]
                + ([((2 * tokens, kv_shape[1]), BF16)] if q == 1 else []),
                got[q],
                got[first_of[q * groups // CHUNKS]],
                local[q],
                *([total] if q == 0 else [rows["own"], rows["near"]]),
                *([kv] if q == 1 else []),
                after=(mark,),
                cost=FIRST_COST if q == 1 else 0.0,
            )
            if q == 0:
                rows["own"], rows["near"], rows["near_total"], *results = results
            other[q] = results[0]
            middle[q] = between_inner(results[1])
            if q == 1:
                rows["kv"] = results[2]
            return results[0]

        def second(q, mark):
            results = call(
                functools.partial(second_kernel, q=q, groups=groups, state=state, **shared),
                "second",
                ([((8, wide), F32)] if q == 0 else [])
                + [
                    ((tokens, cols), F32),
                    ((2 * steps, cols), F32),
                    ((tokens + 2 * steps + (16 if q == 0 else 0), cols), BF16),
                ],
                middle[q],
                other[q],
                local[q],
                rows["own"],
                cc,
                near_cc,
                *([total, rows["near_total"]] if q == 0 else [rows["later"]]),
                after=(mark,),
                cost=SECOND_COST,
            )
            if q == 0:
                rows["later"], *results = results
            carried[q], cands[q] = results[:2]
            outer[q] = to_neighbour(results[2])
            return results[0]

        def third(q, mark):
            final = q == CHUNKS - 1
            results = call(
                functools.partial(third_kernel, q=q, **shared),
                "third",
                [((tokens, wide), BF16), ((steps, wide), F32), ((steps, wide), BF16)]
                if final
                else ([((8, wide), F32)] if q == 0 else []) + [((tokens, cols), BF16), ((2 * steps, cols), F32)],
                outer[q],
                carried[q],
                cands[q],
                base,
                cum,
                rows["own"],
                *([] if q == 0 else [rows["outer"]]),
                *(outs + raws if final else []),
                after=(mark,),
                cost=0.3,
            )
            if final:
                return results
            if q == 0:
                rows["outer"], *results = results
            outs.append(results[0])
            raws.append(results[1])
            return results[0]

        mark = first(0, cc)
        mark = first(1, mark)
        far_kv = between_inner(rows["kv"])
        outer_kv = to_neighbour(far_kv)
        mark = base = intra(mark)
        mark = first(2, mark)
        cand_base, cand_fade = candidates(mark)
        mark = second(0, cand_base)
        mark = first(3, mark)
        mark = second(1, mark)
        mark = third(0, mark)
        mark, finish_attend = attend(mark, [rows["kv"], far_kv, outer_kv], True)
        mark = second(2, mark)
        mark = cand_attn = finish_attend(mark)
        mark = third(1, mark)
        mark = second(3, mark)
        mark = third(2, mark)
        results = third(3, mark)
        prefix_out, keep, give = results
    else:
        halves = [kv, got[1][:, -kv_shape[1] :]]
        for level in range(1, levels):
            mirrored = to_mirror(halves[0], level)
            halves = [halves[0], halves[1], mirrored, to_neighbour(mirrored)]
            if level < levels - 1:
                halves = [jnp.concatenate([halves[0], halves[2]]), jnp.concatenate([halves[1], halves[3]])]
        mark = base = intra(cc)
        own, start = dict(enumerate(local)), {}
        before = None
        near, far = {}, {}
        outs, raws = [], []
        for level in range(levels):
            last = level == levels - 1
            rows = None
            for q in range(CHUNKS):
                final = last and q == CHUNKS - 1
                if level == 0:
                    args, lines = [got[q], got[first_of[q * groups // CHUNKS]]], got[0]
                else:
                    args, lines = [near[q], far[q]], near[0]
                shapes = []
                if q == 0:
                    args += [total, lines] + ([] if level == 0 else [before])
                    shapes += [((8, wide), F32)] * 2 + [((8, heads), F32)] * 2
                else:
                    args += rows
                args += [own[q]] + ([] if level == 0 else [start[q]])
                if final:
                    args += [cc, base, cum] + outs + raws
                    shapes = [((tokens, wide), BF16), ((steps, wide), F32), ((steps, wide), BF16)]
                elif last:
                    args += [cc, base, cum]
                    shapes += [((tokens, cols), BF16), ((2 * steps, cols), F32)]
                else:
                    shapes += [((state, cols), F32)] * 2 + [((state + (16 if q == 0 else 0), cols // 2), BF16)]
                results = call(
                    functools.partial(
                        merge_kernel, level=level, last=last, chunks=[q], groups=groups, state=state, **shared
                    ),
                    "merge",
                    shapes,
                    *args,
                    after=(mark,),
                )
                mark = results[0]
                if final:
                    prefix_out, keep, give = results
                    continue
                if q == 0:
                    rows, (total, before) = list(results[:2]), results[2:4]
                if last:
                    outs.append(results[-2])
                    raws.append(results[-1])
                else:
                    own[q], start[q] = results[-3], results[-2]
                    near[q] = to_mirror(results[-1], level + 1)
                    far[q] = to_neighbour(near[q])
            if level == 0:
                cand_base, cand_fade = candidates(mark)
                pieces = ([halves[0][tokens:]] if levels > 2 else []) + halves[1:]
                mark, finish_attend = attend(cand_base, pieces, False)
                mark = cand_attn = finish_attend(mark)
    (cand_ssm,) = call(
        close_kernel,
        "close",
        [((1, steps, cand_wide), BF16)],
        cand_length,
        cand_base,
        cand_fade,
        keep,
        to_core(give),
        scalars=1,
    )
    return (prefix_out, cand_ssm, cand_attn)


def solution(mesh):
    placed = (
        P(("groups", "seq"), ("head", "rep")),
        P(("groups", "seq"), ("head", "rep"), None),
        P(("groups", "seq"), ("head", "rep"), None),
        P(("groups", "seq"), ("head", "rep")),
        P(),
        P(("groups", "seq"), "head", None),
        P(("groups", "seq"), "head", None),
        P(("groups", "seq", "rep"), None, "head"),
        P(("groups", "seq", "rep"), None, "head", None),
        P(("groups", "seq", "rep"), None, "head", None),
        P(("groups", "seq", "rep"), None, "head"),
        P(("groups", "seq", "rep"), None, "head", None),
        P(("groups", "seq", "rep"), None, "head", None),
        P(("groups", "seq", "rep"), None, "head", None),
        P(("groups", "seq", "rep")),
    )
    return jax.shard_map(
        on_device,
        mesh=mesh,
        in_specs=placed,
        out_specs=(
            P(("groups", "seq"), ("head", "rep")),
            P(("groups", "seq", "rep"), None, "head"),
            P(("groups", "seq", "rep"), None, "head", None),
        ),
        check_vma=False,
    )
```

```python
import functools

import jax
import jax.numpy as jnp
from jax import lax
from jax.experimental import pallas as pl
from jax.experimental.pallas import tpu as pltpu
from jax.sharding import PartitionSpec as P

EPSILON = 1e-06
NEG = -1e30
CHUNKS = 4
SECOND_COST = 1.0
FIRST_COST = 0.0
THIRD_COST = 0.3
F32 = jnp.float32
BF16 = jnp.bfloat16


def mm(a, b):
    return lax.dot_general(a, b, (((1,), (0,)), ((), ())), preferred_element_type=F32)


def mm_nt(a, b):
    return lax.dot_general(a, b, (((1,), (1,)), ((), ())), preferred_element_type=F32)


def mm_tn(a, b):
    return lax.dot_general(a, b, (((0,), (0,)), ((), ())), preferred_element_type=F32)


def exact_nt(a, b):
    return lax.dot_general(
        a, b, (((1,), (1,)), ((), ())), preferred_element_type=F32, precision=lax.Precision.HIGHEST
    )


def exact(a, b):
    return lax.dot_general(
        a, b, (((1,), (0,)), ((), ())), preferred_element_type=F32, precision=lax.Precision.HIGHEST
    )


def iota(shape, dim):
    return lax.broadcasted_iota(jnp.int32, shape, dim)


def split3(a):
    hi = a.astype(BF16)
    rest = a - hi.astype(F32)
    mid = rest.astype(BF16)
    return hi, mid, (rest - mid.astype(F32)).astype(BF16)


def spread(a, width, first=0, count=None):
    rows, cols = a.shape
    count = cols if count is None else count
    parts = jnp.concatenate(split3(a), axis=1)
    shape = (3 * cols, count * width)
    source = iota(shape, 0)
    source = jnp.where(source >= 2 * cols, source - 2 * cols, jnp.where(source >= cols, source - cols, source))
    unit = (source == first + iota(shape, 1) // width).astype(F32).astype(BF16)
    return mm(parts, unit)


def group_of(array, g):
    return array.astype(F32)[:, g, :].astype(BF16)


def payload_plan(groups):
    of = [q * groups // CHUNKS for q in range(CHUNKS)]
    return [([g] if g not in of[:q] else []) for q, g in enumerate(of)]


def totals_to_lines(total):
    hi, mid, lo = [a.astype(F32) for a in split3(jnp.broadcast_to(total, (16, total.shape[1])))]
    line = iota(hi.shape, 0)
    return jnp.where(line == 0, hi, jnp.where(line == 1, mid, jnp.where(line == 2, lo, 0.0))).astype(BF16)


def lines_to_totals(lines):
    lines = lines.astype(F32)
    return lines[0:1] + lines[1:2] + lines[2:3]


def as_row(total, width):
    return spread(jnp.broadcast_to(total, (8, total.shape[1])), width)


def pack(k_ref, v_ref):
    rep = lax.axis_index("rep")
    kv = jnp.where(rep == 0, k_ref[...].astype(F32), v_ref[...].astype(F32))
    return jnp.concatenate([kv[:, j, :] for j in range(kv.shape[1])], axis=1).astype(BF16)


def inputs_kernel(x_any, b_any, decay_t_any, k_any, v_any, cum_ref, total_ref, b2_ref, kv_ref, *refs):
    load_refs, (x_ref, b_ref, decay_t_ref, k_ref, v_ref, sems) = refs[:-6], refs[-6:]
    pairs = ((decay_t_any, decay_t_ref), (b_any, b_ref), (x_any, x_ref), (k_any, k_ref), (v_any, v_ref))
    copies = [pltpu.make_async_copy(source, target, sems.at[i]) for i, (source, target) in enumerate(pairs)]
    for copy in copies:
        copy.start()
    tokens, groups, state = b_ref.shape
    heads = decay_t_ref.shape[0]
    cols = x_ref.shape[1] // CHUNKS
    copies[0].wait()
    lower = (iota((tokens, tokens), 0) >= iota((tokens, tokens), 1)).astype(F32)
    cum = exact_nt(lower, decay_t_ref[...])
    cum_ref[...] = cum
    last = cum[tokens - 1 : tokens, :]
    total = jnp.exp(-last)
    total_ref[...] = jnp.broadcast_to(total, (8, heads))
    load_refs[0][tokens:, :] = jnp.zeros((16, cols + state), BF16)
    load_refs[0][tokens:, :heads] = totals_to_lines(total)
    weights = spread(jnp.exp(last - cum), x_ref.shape[1] // heads)
    for copy in copies[1:]:
        copy.wait()
    b = b_ref[...].astype(F32)
    for g in range(groups):
        b2_ref[:, g * state : (g + 1) * state] = b[:, g, :].astype(BF16)
    kv = pack(k_ref, v_ref)
    kv_ref[...] = kv
    for q, (fresh, load) in enumerate(zip(payload_plan(groups), load_refs)):
        at = slice(q * cols, (q + 1) * cols)
        load[:tokens, :cols] = (x_ref[:, at].astype(F32) * weights[:, at]).astype(BF16)
        if fresh:
            load[:tokens, cols : cols + state] = b2_ref[:, fresh[0] * state : (fresh[0] + 1) * state]
        if q == 1:
            load[:, load.shape[1] - kv.shape[1] :] = kv


def own_kernel(*refs, cols, groups, state):
    load_refs, out_refs = refs[:CHUNKS], refs[CHUNKS:]
    tokens = load_refs[1].shape[0]
    first_of = {g: q for q, fresh in enumerate(payload_plan(groups)) for g in fresh}
    for q in range(CHUNKS):
        b_ref = load_refs[first_of[q * groups // CHUNKS]]
        out_refs[q][...] = mm_tn(b_ref[:tokens, cols : cols + state], load_refs[q][:tokens, :cols])


def collect_kernel(*refs, inner):
    refs, out_ref = list(refs[:-1]), refs[-1]
    place = lax.axis_index("seq")
    pieces = [ref[...] for ref in refs]
    if inner:
        pair, far, outer = pieces
        rows, wide = far.shape
        count = outer.shape[1] // wide
        first = outer.shape[0] - rows // count
        outer = jnp.concatenate([outer[first:, i * wide : (i + 1) * wide] for i in range(count)], axis=0)
        pieces = [pair[pair.shape[0] // 2 :], jnp.where((place == 1) | (place == 2), far, outer)]
    at = 0
    for piece in pieces:
        out_ref[at : at + piece.shape[0], :] = piece
        at += piece.shape[0]


def half_of(place, level):
    odd = lax.rem(place, 2)
    return jnp.where(lax.rem(lax.div(place, 2**level), 2) == 0, 1 - odd, odd)


def merge_kernel(*refs, level, last, chunks, cols, groups, heads, tokens, state):
    refs = list(refs)

    def take(count):
        taken = refs[:count]
        del refs[:count]
        return taken

    place = lax.axis_index("seq")
    right = lax.rem(lax.div(place, 2**level), 2) == 1
    width = cols * CHUNKS // heads
    first = 0 in chunks
    outs = []
    others = []
    if level == 0:
        for q in chunks:
            w_ref, b_ref = take(2)
            others.append(mm_tn(b_ref[:tokens, cols : cols + state], w_ref[:tokens, :cols]))
    else:
        half = half_of(place, level)
        for q in chunks:
            near_ref, far_ref = take(2)
            rows = near_ref.shape[0] - 16 if q == 0 else near_ref.shape[0]
            near, far = near_ref[:rows, :], far_ref[:rows, :]
            pieces = [jnp.where(half == 0, near, far), jnp.where(half == 0, far, near)]
            others.append(jnp.concatenate(pieces, axis=1).astype(F32))
    if first:
        mine_ref, lines_ref = take(2)
        mine = mine_ref[:1, :]
        theirs = lines_to_totals(lines_ref[lines_ref.shape[0] - 16 :, :heads])
        later = as_row(jnp.where(right, mine, theirs), width)
        pair = mine * theirs
        if level == 0:
            before = jnp.ones_like(mine)
        else:
            before = take(1)[0][:1, :]
        before_row = as_row(before, width)
        before = jnp.where(right, before * theirs, before)
        outs += [later, before_row, jnp.broadcast_to(pair, (8, heads)), jnp.broadcast_to(before, (8, heads))]
    else:
        later_ref, before_ref = take(2)
        later, before_row = later_ref[...], before_ref[...]
    for q, other in zip(chunks, others, strict=True):
        at = slice(q * cols, (q + 1) * cols)
        own = take(1)[0][...]
        earlier, following = jnp.where(right, other, own), jnp.where(right, own, other)
        joined = later[:1, at] * earlier + following
        if level == 0:
            start = jnp.where(right, other, 0.0)
        else:
            start = take(1)[0][...]
            start = jnp.where(right, before_row[:1, at] * other + start, start)
        if not last:
            send = jnp.where(half_of(place, level + 1) == 0, joined[:, : cols // 2], joined[:, cols // 2 :]).astype(BF16)
            if q == 0:
                tail = jnp.zeros((16, cols // 2 - heads), BF16)
                lines = jnp.concatenate([totals_to_lines(pair), tail], axis=1)
                send = jnp.concatenate([send, lines], axis=0)
            outs += [joined, start, send]
        else:
            cc_ref, base_ref, cum_ref = take(3)
            g = q * groups // CHUNKS
            here = slice(g * state, (g + 1) * state)
            fade = spread(jnp.exp(-cum_ref[...]), width, q * heads // CHUNKS, heads // CHUNKS)
            carried = mm(cc_ref[:tokens, here], start.astype(BF16))
            outs.append((base_ref[:, at] + fade * carried).astype(BF16))
            outs.append(mm(cc_ref[tokens:, here], joined.astype(BF16)))
    if last and CHUNKS - 1 in chunks:
        parts = take(2 * (CHUNKS - 1))
        out_parts = [ref[...] for ref in parts[: CHUNKS - 1]] + [outs[-2]]
        raws = [ref[...] for ref in parts[CHUNKS - 1 :]] + [outs[-1]]
        rep = lax.axis_index("rep")
        out_ref, keep_ref, give_ref = refs
        rows = keep_ref.shape[0]
        for q in range(CHUNKS):
            at = slice(q * cols, (q + 1) * cols)
            out_ref[:, at] = out_parts[q]
            keep_ref[:, at] = jnp.where(rep == 0, raws[q][:rows], raws[q][rows:])
            give_ref[:, at] = jnp.where(rep == 0, raws[q][rows:], raws[q][:rows]).astype(BF16)
    else:
        for ref, value in zip(refs, outs, strict=True):
            ref[...] = value


def projections_kernel(c_ref, mine_ref, other_ref, out_ref):
    rep = lax.axis_index("rep")
    tokens, groups, state = c_ref.shape
    steps = mine_ref.shape[1]
    mine, other = mine_ref[0].astype(F32), other_ref[0].astype(F32)
    zero, one = jnp.where(rep == 0, mine, other), jnp.where(rep == 0, other, mine)
    prefix = c_ref[...].astype(F32)
    for g in range(groups):
        at = slice(g * state, (g + 1) * state)
        out_ref[:tokens, at] = prefix[:, g, :].astype(BF16)
        for i, c in enumerate((zero, one)):
            part = jnp.where(rep == 0, c[:, g, :], c[:, groups + g, :])
            out_ref[tokens + i * steps : tokens + (i + 1) * steps, at] = part.astype(BF16)


def first_kernel(*refs, q, cols, groups, heads, tokens, state):
    refs = list(refs)
    w_ref, b_ref, own_w_ref, own_b_ref = refs[:4]
    refs = refs[4:]
    left = lax.axis_index("seq") < 2
    width = cols * CHUNKS // heads
    other = mm_tn(b_ref[:tokens, cols : cols + state], w_ref[:tokens, :cols])
    if q == 0:
        mine_ref, own_row_ref, near_row_ref, near_ref, send_ref = refs
        mine = mine_ref[:1, :]
        near = lines_to_totals(w_ref[tokens:, :heads])
        own_row, near_row = as_row(mine, width), as_row(near, width)
        own_row_ref[...] = own_row
        near_row_ref[...] = near_row
        near_ref[...] = jnp.broadcast_to(near, (8, heads))
        send_ref[state:, :] = jnp.zeros((16, cols), BF16)
        send_ref[state:, :heads] = totals_to_lines(mine * near)
    else:
        own_row_ref, near_row_ref = refs[:2]
        refs = refs[2:]
        if q == 1:
            kv_ref, pair_ref = refs[0], refs.pop()
            refs = refs[1:]
            pair_ref[:tokens, :] = kv_ref[...]
            pair_ref[tokens:, :] = w_ref[:, w_ref.shape[1] - kv_ref.shape[1] :]
        (send_ref,) = refs
        own_row, near_row = own_row_ref[...], near_row_ref[...]
    at = slice(q * cols, (q + 1) * cols)
    local = mm_tn(own_b_ref[:tokens, cols : cols + state], own_w_ref[:tokens, :cols])
    after = own_row[:1, at] * other + local
    beyond = other + near_row[:1, at] * local
    send_ref[:state, :] = jnp.where(left, after, beyond).astype(BF16)


def second_kernel(*refs, q, cols, groups, heads, tokens, state):
    refs = list(refs)
    got_ref, w_ref, b_ref, own_w_ref, own_b_ref, own_row_ref, cc_ref, near_cc_ref = refs[:8]
    refs = refs[8:]
    place = lax.axis_index("seq")
    left, inner = place < 2, (place == 1) | (place == 2)
    width = cols * CHUNKS // heads
    at = slice(q * cols, (q + 1) * cols)
    g = q * groups // CHUNKS
    here = slice(g * state, (g + 1) * state)
    rows = cc_ref.shape[0]
    if q == 0:
        mine_ref, near_ref, later_row_ref, carried_ref, cand_ref, send_ref = refs
        later = jnp.where(left, lines_to_totals(got_ref[state:, :heads]), near_ref[:1, :])
        later_row = as_row(later, width)
        later_row_ref[...] = later_row
        send_ref[rows:, :] = jnp.zeros((16, cols), BF16)
        send_ref[rows:, :heads] = totals_to_lines(later * mine_ref[:1, :])
    else:
        if q == 1:
            kv_ref = refs.pop(0)
            held = kv_ref.shape[0] // (cols // kv_ref.shape[1])
            for i in range(cols // kv_ref.shape[1]):
                part = slice(i * kv_ref.shape[1], (i + 1) * kv_ref.shape[1])
                refs[-1][rows:, part] = kv_ref[i * held : (i + 1) * held, :]
        later_row_ref, carried_ref, cand_ref, send_ref = refs
        later_row = later_row_ref[...]
    got = got_ref[:state, :].astype(F32)
    other = mm_tn(b_ref[:tokens, cols : cols + state], w_ref[:tokens, :cols])
    local = mm_tn(own_b_ref[:tokens, cols : cols + state], own_w_ref[:tokens, :cols])
    start, beyond = jnp.where(left, other, got), jnp.where(left, got, other)
    start = jnp.where(inner, start, 0.0)
    after = own_row_ref[:1, at] * start + local
    lasting = later_row[:1, at]
    state_out = jnp.where(left, beyond + lasting * local, after)
    send_ref[:rows, :] = mm(near_cc_ref[:, here], state_out.astype(BF16)).astype(BF16)
    final = jnp.where(inner, lasting * after + beyond, local)
    carried_ref[...] = mm(cc_ref[:tokens, here], start.astype(BF16))
    cand_ref[...] = mm(cc_ref[tokens:, here], final.astype(BF16))


def third_kernel(*refs, q, cols, heads, tokens):
    refs = list(refs)
    got_ref, carried_ref, cand_ref, base_ref, cum_ref, own_row_ref = refs[:6]
    place = lax.axis_index("seq")
    width = cols * CHUNKS // heads
    at = slice(q * cols, (q + 1) * cols)
    rows = cand_ref.shape[0]
    refs = refs[6:]
    if q == 0:
        later_row_ref = refs[0]
        later_row = as_row(lines_to_totals(got_ref[tokens + rows :, :heads]), width)
        later_row_ref[...] = later_row
    else:
        later_row = refs[0][...]
    refs = refs[1:]
    fade = spread(jnp.exp(-cum_ref[...]), width, q * heads // CHUNKS, heads // CHUNKS)
    got = got_ref[: tokens + rows, :].astype(F32)
    carried = jnp.where(place == 3, got[:tokens], carried_ref[...])
    cand = cand_ref[...]
    cand = jnp.where(
        place == 3,
        own_row_ref[:1, at] * got[tokens:] + cand,
        jnp.where(place == 0, later_row[:1, at] * cand + got[tokens:], cand),
    )
    out = (base_ref[:, at] + fade * carried).astype(BF16)
    if q < CHUNKS - 1:
        out_ref, raw_ref = refs
        out_ref[...] = out
        raw_ref[...] = cand
        return
    outs, raws, (out_ref, keep_ref, give_ref) = refs[: CHUNKS - 1], refs[CHUNKS - 1 : 2 * CHUNKS - 2], refs[-3:]
    rep = lax.axis_index("rep")
    half = rows // 2
    for i in range(CHUNKS):
        at = slice(i * cols, (i + 1) * cols)
        out_ref[:, at] = out if i == q else outs[i][...]
        raw = cand if i == q else raws[i][...]
        keep_ref[:, at] = jnp.where(rep == 0, raw[:half], raw[half:])
        give_ref[:, at] = jnp.where(rep == 0, raw[half:], raw[:half]).astype(BF16)


def intra_kernel(x_ref, b2_ref, c2_ref, cum_ref, skip_ref, base_ref, *, groups):
    tokens, heads = cum_ref.shape
    width = x_ref.shape[1] // heads
    state = c2_ref.shape[1] // groups
    per_group = heads // groups
    first = (lax.axis_index("head") * lax.axis_size("rep") + lax.axis_index("rep")) * heads
    skip = spread(jnp.broadcast_to(skip_ref[...], (8, skip_ref.shape[1])), width, first, heads)[:1]
    cum = cum_ref[...]
    cum_t = cum.T
    shape = (tokens, tokens)
    hidden = jnp.where(iota(shape, 0) >= iota(shape, 1), 0.0, NEG)
    pair = 2 * width
    lane = iota((tokens, pair), 1)
    for g in range(groups):
        here = slice(g * state, (g + 1) * state)
        gram = mm_nt(c2_ref[:tokens, here], b2_ref[:, here])
        for h in range(g * per_group, (g + 1) * per_group, 2):
            mixing = []
            for i in (h, h + 1):
                gap = cum_t[i : i + 1, :] - jnp.broadcast_to(cum[:, i : i + 1], shape)
                mixing.append((jnp.exp(gap + hidden) * gram).astype(BF16))
            at = slice(h * width, (h + 2) * width)
            x = x_ref[:, at]
            zero = jnp.zeros_like(x)
            inputs = jnp.concatenate(
                [jnp.where(lane < width, x, zero), jnp.where(lane < width, zero, x)], axis=0
            )
            base_ref[:, at] = mm(jnp.concatenate(mixing, axis=1), inputs) + skip[:, at] * x.astype(F32)


def cand_kernel(x_ref, b_ref, c_ref, decay_ref, skip_ref, base_ref, fade_ref):
    steps, groups, state = b_ref.shape[1:]
    heads = decay_ref.shape[2]
    width = x_ref.shape[2] // heads
    per_group = heads // groups
    first = lax.axis_index("head") * heads
    skip = spread(jnp.broadcast_to(skip_ref[...], (8, skip_ref.shape[1])), width, first, heads)[:1]
    lower = (iota((steps, steps), 0) >= iota((steps, steps), 1)).astype(F32)
    cum = exact(lower, decay_ref[0])
    fade_ref[...] = spread(jnp.exp(-cum), width)
    wide = (steps, heads * steps)
    cum_t = spread(cum, steps)
    place = iota(wide, 1) % steps
    row = iota(wide, 0)
    cum_s = jnp.sum(jnp.where(row == place, cum_t, 0.0), axis=0, keepdims=True)
    fall = jnp.exp(jnp.where(row >= place, cum_s - cum_t, NEG))
    b = b_ref[0].astype(F32)
    c = c_ref[0].astype(F32)
    quad = 128 // steps
    shape = (quad * steps, quad * width)
    mine = iota(shape, 0) // steps == iota(shape, 1) // width
    for g in range(groups):
        b_g = b[:, g, :].astype(BF16)
        gram = mm_nt(c[:, g, :].astype(BF16), jnp.concatenate([b_g] * quad, axis=0))
        for h in range(g * per_group, (g + 1) * per_group, quad):
            mixing = (fall[:, h * steps : (h + quad) * steps] * gram).astype(BF16)
            at = slice(h * width, (h + quad) * width)
            x = x_ref[0, :, at]
            tall = jnp.concatenate([x] * quad, axis=0)
            inputs = jnp.where(mine, tall, jnp.zeros_like(tall))
            base_ref[:, at] = mm(mixing, inputs) + skip[:, at] * x.astype(F32)


def attend_kernel(length_ref, q_ref, own_k_ref, own_v_ref, k_ref, v_ref, mine_ref, other_ref, *refs):
    out_ref = refs[-1]
    rep = lax.axis_index("rep")
    steps, heads, dim = q_ref.shape[1:]
    kv_heads = own_k_ref.shape[2]
    per_kv = heads // kv_heads
    rows = steps * per_kv
    mine, other = mine_ref[...], other_ref[...]
    keys, values = jnp.where(rep == 0, mine, other), jnp.where(rep == 0, other, mine)
    q = q_ref[0].astype(F32)
    own_k = own_k_ref[0].astype(F32)
    own_v = own_v_ref[0].astype(F32)
    block_k = k_ref[...].astype(F32)
    block_v = v_ref[...].astype(F32)
    scale = dim ** (-0.5)
    step_of = iota((rows, steps), 0) // per_kv
    visible = step_of >= iota((rows, steps), 1)
    live = iota((rows, dim), 0) // per_kv < length_ref[0]
    mixed_of = []
    for j in range(kv_heads):
        query = q[:, j * per_kv : (j + 1) * per_kv, :].reshape(rows, dim).astype(BF16)

        def gather(far, block):
            return jnp.concatenate([far[:, j * dim : (j + 1) * dim], block[:, j, :].astype(BF16)], axis=0)

        far = mm_nt(query, gather(keys, block_k)) * scale
        near = jnp.where(visible, mm_nt(query, own_k[:, j, :].astype(BF16)) * scale, NEG)
        top = jnp.maximum(jnp.max(far, axis=1, keepdims=True), jnp.max(near, axis=1, keepdims=True))
        far = jnp.exp(far - top)
        near = jnp.exp(near - top)
        mass = jnp.sum(far, axis=1, keepdims=True) + jnp.sum(near, axis=1, keepdims=True)
        mixed = mm(far.astype(BF16), gather(values, block_v)) + mm(near.astype(BF16), own_v[:, j, :].astype(BF16))
        mixed = mixed / mass
        mixed = mixed * lax.rsqrt(jnp.mean(mixed * mixed, axis=1, keepdims=True) + EPSILON)
        mixed = jnp.where(live, mixed, 0.0)
        mixed_of.append(mixed.reshape(steps, per_kv, dim))
    out_ref[0] = (jnp.concatenate(mixed_of, axis=1) if kv_heads > 1 else mixed_of[0]).astype(BF16)


def close_kernel(length_ref, base_ref, fade_ref, keep_ref, got_ref, out_ref):
    rep = lax.axis_index("rep")
    keep, got = keep_ref[...], got_ref[...].astype(F32)
    cols = keep.shape[1]
    live = iota(keep.shape, 0) < length_ref[0]
    for i in range(2):
        at = slice(i * cols, (i + 1) * cols)
        carried = jnp.where(rep == i, keep, got)
        result = base_ref[:, at] + fade_ref[:, at] * carried
        out_ref[0, :, at] = jnp.where(live, result, 0.0).astype(BF16)


def call(kernel, name, outs, *args, scalars=0, after=(), cost=0.0, scratch=(), limit=32, gate=()):
    shapes = [jax.ShapeDtypeStruct(shape, dtype) for shape, dtype in outs]
    vmem = pl.BlockSpec(memory_space=pltpu.VMEM)
    smem = pl.BlockSpec(memory_space=pltpu.SMEM)
    count, rest = len(args), len(args) + len(after) + len(gate)
    through = rest + len(shapes)
    out_spec = vmem
    if scratch:
        vmem = pl.BlockSpec(memory_space=pl.ANY)

    def body(*refs):
        kernel(*refs[:count], *refs[rest:through], *refs[through + len(gate) :])

    return pl.pallas_call(
        body,
        out_shape=shapes + [jax.ShapeDtypeStruct(a.shape, a.dtype) for a in gate],
        in_specs=[smem] * scalars
        + [vmem] * (count - scalars)
        + [pl.BlockSpec(memory_space=pl.ANY)] * (len(after) + len(gate)),
        out_specs=[out_spec] * len(shapes) + [pl.BlockSpec(memory_space=pl.ANY)] * len(gate),
        input_output_aliases={count + len(after) + i: len(shapes) + i for i in range(len(gate))},
        scratch_shapes=list(scratch),
        compiler_params=pltpu.CompilerParams(vmem_limit_bytes=limit * 2**20),
        cost_estimate=pl.CostEstimate(flops=int(cost * 10**9), bytes_accessed=0, transcendentals=0),
        name=name,
    )(*args, *after, *gate)


def on_device(
    prefix_x,
    prefix_b,
    prefix_c,
    prefix_decay,
    bypass_weight,
    prefix_key_rows,
    prefix_values,
    cand_x,
    cand_b,
    cand_c,
    cand_decay,
    cand_queries,
    cand_keys,
    cand_values,
    cand_length,
):
    size = lax.axis_size("seq")
    levels = size.bit_length() - 1
    assert size == 2**levels and lax.axis_size("rep") == 2
    tokens, groups, state = prefix_b.shape
    heads = prefix_decay.shape[1]
    wide = prefix_x.shape[1]
    steps = cand_x.shape[1]
    cand_wide = cand_x.shape[2]
    cols = wide // CHUNKS
    skip = bypass_weight.reshape(1, -1)
    plan = payload_plan(groups)

    def to_core(array):
        return lax.ppermute(array, "rep", [(0, 1), (1, 0)])

    def to_neighbour(array):
        return lax.ppermute(array, "seq", [(i, i ^ 1) for i in range(size)])

    def to_mirror(array, level):
        return lax.ppermute(array, "seq", [(i, i ^ (2 ** (level + 1) - 1)) for i in range(size)])

    def between_inner(array):
        far = {1: 2, 2: 1}
        pairs = [(2 * i + r, 2 * far[i] + r if i in far else 2 * i + 1 - r) for i in range(size) for r in range(2)]
        return lax.ppermute(array, ("seq", "rep"), pairs)

    def inward(array):
        return lax.ppermute(array, "seq", [(0, 1), (3, 2)])

    other_c = to_core(cand_c)
    kv_shape = (tokens, prefix_key_rows.shape[1] * prefix_key_rows.shape[2])
    cum, total, b2, kv, *loads = call(
        inputs_kernel,
        "inputs",
        [((tokens, heads), F32), ((8, heads), F32), ((tokens, groups * state), BF16), (kv_shape, BF16)]
        + [
            (
                (
                    tokens + (16 if q == 0 else 0),
                    cols + len(fresh) * state + (kv_shape[1] if q == 1 else 0),
                ),
                BF16,
            )
            for q, fresh in enumerate(plan)
        ],
        prefix_x,
        prefix_b,
        prefix_decay.T,
        prefix_key_rows,
        prefix_values,
        scratch=[
            pltpu.VMEM(prefix_x.shape, BF16),
            pltpu.VMEM(prefix_b.shape, BF16),
            pltpu.VMEM((heads, tokens), F32),
            pltpu.VMEM(prefix_key_rows.shape, BF16),
            pltpu.VMEM(prefix_values.shape, BF16),
            pltpu.SemaphoreType.DMA((5,)),
        ],
        limit=60,
    )
    (cc,) = call(
        projections_kernel,
        "projections",
        [((tokens + 2 * steps, groups * state), BF16)],
        prefix_c,
        cand_c,
        other_c,
        after=(cum,),
    )
    first_of = {g: q for q, fresh in enumerate(plan) for g in fresh}
    def intra(mark, cc):
        return call(
            functools.partial(intra_kernel, groups=groups),
            "intra",
            [((tokens, wide), F32)],
            prefix_x,
            b2,
            cc,
            cum,
            skip,
            after=(mark,),
            gate=(loads[1],),
        )

    def candidates(mark):
        return call(
            cand_kernel,
            "candidates",
            [((steps, cand_wide), F32), ((steps, cand_wide), F32)],
            cand_x,
            cand_b,
            cand_c,
            cand_decay,
            skip,
            after=(mark,),
        )

    def attend(mark, pieces, inner):
        (mine,) = call(
            functools.partial(collect_kernel, inner=inner),
            "collect",
            [((tokens * (size - 1), kv_shape[1]), BF16)],
            *pieces,
            after=(mark,),
        )
        theirs = to_core(mine)

        def finish(mark):
            return call(
                attend_kernel,
                "attend",
                [(cand_queries.shape, BF16)],
                cand_length,
                cand_queries,
                cand_keys,
                cand_values,
                prefix_key_rows,
                prefix_values,
                mine,
                theirs,
                scalars=1,
                after=(mark,),
            )[0]

        return mine, finish

    shared = dict(cols=cols, heads=heads, tokens=tokens)
    if size == 4:
        mark = cc
        middle, carried, cands, outer, outs, raws = {}, {}, {}, {}, [], []
        rows = {"cc": cc}

        def inputs_of(q):
            p = first_of[q * groups // CHUNKS]
            return got[q], got[p], loads[q], loads[p]

        def first(q, mark):
            extra = [((8, wide), F32), ((8, wide), F32), ((8, heads), F32)] if q == 0 else []
            results = call(
                functools.partial(first_kernel, q=q, groups=groups, state=state, **shared),
                "first",
                extra
                + [((state + (16 if q == 0 else 0), cols), BF16)]
                + ([((2 * tokens, kv_shape[1]), BF16)] if q == 1 else []),
                *inputs_of(q),
                *([total] if q == 0 else [rows["own"], rows["near"]]),
                *([kv] if q == 1 else []),
                after=(mark,),
                cost=FIRST_COST if q == 1 else 0.0,
                gate=[(rows["cc"],), loads[2:], (), ()][q],
            )
            if q == 0:
                *results, rows["cc"] = results
                rows["near_cc"] = to_neighbour(rows["cc"])
            elif q == 1:
                *results, loads[2], loads[3] = results
                got.extend((to_neighbour(loads[2]), inward(loads[3])))
            if q == 0:
                rows["own"], rows["near"], rows["near_total"], *results = results
            middle[q] = between_inner(results[0])
            if q == 1:
                rows["kv"] = results[1]
            return results[0]

        def second(q, mark):
            results = call(
                functools.partial(second_kernel, q=q, groups=groups, state=state, **shared),
                "second",
                ([((8, wide), F32)] if q == 0 else [])
                + [
                    ((tokens, cols), F32),
                    ((2 * steps, cols), F32),
                    ((tokens + 2 * steps + [16, 2 * tokens * kv_shape[1] // cols, 0, 0][q], cols), BF16),
                ],
                middle[q],
                *inputs_of(q),
                rows["own"],
                rows["cc"],
                rows["near_cc"],
                *([far_kv] if q == 1 else []),
                *([total, rows["near_total"]] if q == 0 else [rows["later"]]),
                after=(mark,),
                cost=SECOND_COST,
            )
            if q == 0:
                rows["later"], *results = results
            carried[q], cands[q] = results[:2]
            outer[q] = to_neighbour(results[2])
            return results[0]

        def third(q, mark):
            final = q == CHUNKS - 1
            results = call(
                functools.partial(third_kernel, q=q, **shared),
                "third",
                [((tokens, wide), BF16), ((steps, wide), F32), ((steps, wide), BF16)]
                if final
                else ([((8, wide), F32)] if q == 0 else []) + [((tokens, cols), BF16), ((2 * steps, cols), F32)],
                outer[q],
                carried[q],
                cands[q],
                base,
                cum,
                rows["own"],
                *([] if q == 0 else [rows["outer"]]),
                *(outs + raws if final else []),
                after=(mark,),
                cost=THIRD_COST,
            )
            if final:
                return results
            if q == 0:
                rows["outer"], *results = results
            outs.append(results[0])
            raws.append(results[1])
            return results[0]

        base, loads[1] = intra(cc, cc)
        got = [to_neighbour(a) for a in loads[:2]]
        mark = first(0, base)
        mark = first(1, mark)
        far_kv = between_inner(rows["kv"])
        mark = second(0, mark)
        mark = first(2, mark)
        mark = second(1, mark)
        mark = first(3, mark)
        cand_base, cand_fade = candidates(mark)
        mark = third(0, cand_base)
        mark = second(2, mark)
        mark = third(1, mark)
        mark, finish_attend = attend(mark, [rows["kv"], far_kv, outer[1]], True)
        mark = second(3, mark)
        mark = cand_attn = finish_attend(mark)
        mark = third(2, mark)
        results = third(3, mark)
        prefix_out, keep, give = results
    else:
        got = [to_neighbour(a) for a in loads]
        halves = [kv, got[1][:, -kv_shape[1] :]]
        for level in range(1, levels):
            mirrored = to_mirror(halves[0], level)
            halves = [halves[0], halves[1], mirrored, to_neighbour(mirrored)]
            if level < levels - 1:
                halves = [jnp.concatenate([halves[0], halves[2]]), jnp.concatenate([halves[1], halves[3]])]
        base, loads[1] = intra(cc, cc)
        mark = base
        own = call(
            functools.partial(own_kernel, cols=cols, groups=groups, state=state),
            "own",
            [((state, cols), F32)] * CHUNKS,
            *loads,
        )
        own, start = dict(enumerate(own)), {}
        before = None
        near, far = {}, {}
        outs, raws = [], []
        for level in range(levels):
            last = level == levels - 1
            rows = None
            for q in range(CHUNKS):
                final = last and q == CHUNKS - 1
                if level == 0:
                    args, lines = [got[q], got[first_of[q * groups // CHUNKS]]], got[0]
                else:
                    args, lines = [near[q], far[q]], near[0]
                shapes = []
                if q == 0:
                    args += [total, lines] + ([] if level == 0 else [before])
                    shapes += [((8, wide), F32)] * 2 + [((8, heads), F32)] * 2
                else:
                    args += rows
                args += [own[q]] + ([] if level == 0 else [start[q]])
                if final:
                    args += [cc, base, cum] + outs + raws
                    shapes = [((tokens, wide), BF16), ((steps, wide), F32), ((steps, wide), BF16)]
                elif last:
                    args += [cc, base, cum]
                    shapes += [((tokens, cols), BF16), ((2 * steps, cols), F32)]
                else:
                    shapes += [((state, cols), F32)] * 2 + [((state + (16 if q == 0 else 0), cols // 2), BF16)]
                results = call(
                    functools.partial(
                        merge_kernel, level=level, last=last, chunks=[q], groups=groups, state=state, **shared
                    ),
                    "merge",
                    shapes,
                    *args,
                    after=(mark,),
                )
                mark = results[0]
                if final:
                    prefix_out, keep, give = results
                    continue
                if q == 0:
                    rows, (total, before) = list(results[:2]), results[2:4]
                if last:
                    outs.append(results[-2])
                    raws.append(results[-1])
                else:
                    own[q], start[q] = results[-3], results[-2]
                    near[q] = to_mirror(results[-1], level + 1)
                    far[q] = to_neighbour(near[q])
            if level == 0:
                cand_base, cand_fade = candidates(mark)
                pieces = ([halves[0][tokens:]] if levels > 2 else []) + halves[1:]
                mark, finish_attend = attend(cand_base, pieces, False)
                mark = cand_attn = finish_attend(mark)
    (cand_ssm,) = call(
        close_kernel,
        "close",
        [((1, steps, cand_wide), BF16)],
        cand_length,
        cand_base,
        cand_fade,
        keep,
        to_core(give),
        scalars=1,
    )
    return (prefix_out, cand_ssm, cand_attn)


def solution(mesh):
    placed = (
        P(("groups", "seq"), ("head", "rep")),
        P(("groups", "seq"), ("head", "rep"), None),
        P(("groups", "seq"), ("head", "rep"), None),
        P(("groups", "seq"), ("head", "rep")),
        P(),
        P(("groups", "seq"), "head", None),
        P(("groups", "seq"), "head", None),
        P(("groups", "seq", "rep"), None, "head"),
        P(("groups", "seq", "rep"), None, "head", None),
        P(("groups", "seq", "rep"), None, "head", None),
        P(("groups", "seq", "rep"), None, "head"),
        P(("groups", "seq", "rep"), None, "head", None),
        P(("groups", "seq", "rep"), None, "head", None),
        P(("groups", "seq", "rep"), None, "head", None),
        P(("groups", "seq", "rep")),
    )
    return jax.shard_map(
        on_device,
        mesh=mesh,
        in_specs=placed,
        out_specs=(
            P(("groups", "seq"), ("head", "rep")),
            P(("groups", "seq", "rep"), None, "head"),
            P(("groups", "seq", "rep"), None, "head", None),
        ),
        check_vma=False,
    )
```

```python
import functools

import jax
import jax.numpy as jnp
from jax import lax
from jax.experimental import pallas as pl
from jax.experimental.pallas import tpu as pltpu
from jax.sharding import PartitionSpec as P

EPSILON = 1e-06
NEG = -1e30
CHUNKS = 4
SECOND_COST = 1.0
FIRST_COST = 0.0
THIRD_COST = 0.3
F32 = jnp.float32
BF16 = jnp.bfloat16


def mm(a, b):
    return lax.dot_general(a, b, (((1,), (0,)), ((), ())), preferred_element_type=F32)


def mm_nt(a, b):
    return lax.dot_general(a, b, (((1,), (1,)), ((), ())), preferred_element_type=F32)


def mm_tn(a, b):
    return lax.dot_general(a, b, (((0,), (0,)), ((), ())), preferred_element_type=F32)


def exact_nt(a, b):
    return lax.dot_general(
        a, b, (((1,), (1,)), ((), ())), preferred_element_type=F32, precision=lax.Precision.HIGHEST
    )


def exact(a, b):
    return lax.dot_general(
        a, b, (((1,), (0,)), ((), ())), preferred_element_type=F32, precision=lax.Precision.HIGHEST
    )


def iota(shape, dim):
    return lax.broadcasted_iota(jnp.int32, shape, dim)


def split3(a):
    hi = a.astype(BF16)
    rest = a - hi.astype(F32)
    mid = rest.astype(BF16)
    return hi, mid, (rest - mid.astype(F32)).astype(BF16)


def spread(a, width, first=0, count=None):
    rows, cols = a.shape
    count = cols if count is None else count
    parts = jnp.concatenate(split3(a), axis=1)
    shape = (3 * cols, count * width)
    source = iota(shape, 0)
    source = jnp.where(source >= 2 * cols, source - 2 * cols, jnp.where(source >= cols, source - cols, source))
    unit = (source == first + iota(shape, 1) // width).astype(F32).astype(BF16)
    return mm(parts, unit)


def group_of(array, g):
    return array.astype(F32)[:, g, :].astype(BF16)


def payload_plan(groups):
    of = [q * groups // CHUNKS for q in range(CHUNKS)]
    return [([g] if g not in of[:q] else []) for q, g in enumerate(of)]


def totals_to_lines(total):
    hi, mid, lo = [a.astype(F32) for a in split3(jnp.broadcast_to(total, (16, total.shape[1])))]
    line = iota(hi.shape, 0)
    return jnp.where(line == 0, hi, jnp.where(line == 1, mid, jnp.where(line == 2, lo, 0.0))).astype(BF16)


def lines_to_totals(lines):
    lines = lines.astype(F32)
    return lines[0:1] + lines[1:2] + lines[2:3]


def as_row(total, width):
    return spread(jnp.broadcast_to(total, (8, total.shape[1])), width)


def pack(k_ref, v_ref):
    rep = lax.axis_index("rep")
    kv = jnp.where(rep == 0, k_ref[...].astype(F32), v_ref[...].astype(F32))
    return jnp.concatenate([kv[:, j, :] for j in range(kv.shape[1])], axis=1).astype(BF16)


def inputs_kernel(x_any, b_any, decay_t_any, k_any, v_any, cum_ref, total_ref, b2_ref, kv_ref, *refs):
    load_refs, (x_ref, b_ref, decay_t_ref, k_ref, v_ref, sems) = refs[:-6], refs[-6:]
    pairs = ((decay_t_any, decay_t_ref), (b_any, b_ref), (x_any, x_ref), (k_any, k_ref), (v_any, v_ref))
    copies = [pltpu.make_async_copy(source, target, sems.at[i]) for i, (source, target) in enumerate(pairs)]
    for copy in copies:
        copy.start()
    tokens, groups, state = b_ref.shape
    heads = decay_t_ref.shape[0]
    cols = x_ref.shape[1] // CHUNKS
    copies[0].wait()
    lower = (iota((tokens, tokens), 0) >= iota((tokens, tokens), 1)).astype(F32)
    cum = exact_nt(lower, decay_t_ref[...])
    cum_ref[...] = cum
    last = cum[tokens - 1 : tokens, :]
    total = jnp.exp(-last)
    total_ref[...] = jnp.broadcast_to(total, (8, heads))
    load_refs[0][tokens:, :] = jnp.zeros((16, cols + state), BF16)
    load_refs[0][tokens:, :heads] = totals_to_lines(total)
    weights = spread(jnp.exp(last - cum), x_ref.shape[1] // heads)
    for copy in copies[1:]:
        copy.wait()
    b = b_ref[...].astype(F32)
    for g in range(groups):
        b2_ref[:, g * state : (g + 1) * state] = b[:, g, :].astype(BF16)
    kv = pack(k_ref, v_ref)
    kv_ref[...] = kv
    for q, (fresh, load) in enumerate(zip(payload_plan(groups), load_refs)):
        at = slice(q * cols, (q + 1) * cols)
        load[:tokens, :cols] = (x_ref[:, at].astype(F32) * weights[:, at]).astype(BF16)
        if fresh:
            load[:tokens, cols : cols + state] = b2_ref[:, fresh[0] * state : (fresh[0] + 1) * state]
        if q == 1:
            load[:, load.shape[1] - kv.shape[1] :] = kv


def own_kernel(*refs, cols, groups, state):
    load_refs, out_refs = refs[:CHUNKS], refs[CHUNKS:]
    tokens = load_refs[1].shape[0]
    first_of = {g: q for q, fresh in enumerate(payload_plan(groups)) for g in fresh}
    for q in range(CHUNKS):
        b_ref = load_refs[first_of[q * groups // CHUNKS]]
        out_refs[q][...] = mm_tn(b_ref[:tokens, cols : cols + state], load_refs[q][:tokens, :cols])


def collect_kernel(*refs, inner):
    refs, out_ref = list(refs[:-1]), refs[-1]
    place = lax.axis_index("seq")
    pieces = [ref[...] for ref in refs]
    if inner:
        pair, far, outer = pieces
        rows, wide = far.shape
        count = outer.shape[1] // wide
        first = outer.shape[0] - rows // count
        outer = jnp.concatenate([outer[first:, i * wide : (i + 1) * wide] for i in range(count)], axis=0)
        pieces = [pair[pair.shape[0] // 2 :], jnp.where((place == 1) | (place == 2), far, outer)]
    at = 0
    for piece in pieces:
        out_ref[at : at + piece.shape[0], :] = piece
        at += piece.shape[0]


def half_of(place, level):
    odd = lax.rem(place, 2)
    return jnp.where(lax.rem(lax.div(place, 2**level), 2) == 0, 1 - odd, odd)


def merge_kernel(*refs, level, last, chunks, cols, groups, heads, tokens, state):
    refs = list(refs)

    def take(count):
        taken = refs[:count]
        del refs[:count]
        return taken

    place = lax.axis_index("seq")
    right = lax.rem(lax.div(place, 2**level), 2) == 1
    width = cols * CHUNKS // heads
    first = 0 in chunks
    outs = []
    others = []
    if level == 0:
        for q in chunks:
            w_ref, b_ref = take(2)
            others.append(mm_tn(b_ref[:tokens, cols : cols + state], w_ref[:tokens, :cols]))
    else:
        half = half_of(place, level)
        for q in chunks:
            near_ref, far_ref = take(2)
            rows = near_ref.shape[0] - 16 if q == 0 else near_ref.shape[0]
            near, far = near_ref[:rows, :], far_ref[:rows, :]
            pieces = [jnp.where(half == 0, near, far), jnp.where(half == 0, far, near)]
            others.append(jnp.concatenate(pieces, axis=1).astype(F32))
    if first:
        mine_ref, lines_ref = take(2)
        mine = mine_ref[:1, :]
        theirs = lines_to_totals(lines_ref[lines_ref.shape[0] - 16 :, :heads])
        later = as_row(jnp.where(right, mine, theirs), width)
        pair = mine * theirs
        if level == 0:
            before = jnp.ones_like(mine)
        else:
            before = take(1)[0][:1, :]
        before_row = as_row(before, width)
        before = jnp.where(right, before * theirs, before)
        outs += [later, before_row, jnp.broadcast_to(pair, (8, heads)), jnp.broadcast_to(before, (8, heads))]
    else:
        later_ref, before_ref = take(2)
        later, before_row = later_ref[...], before_ref[...]
    for q, other in zip(chunks, others, strict=True):
        at = slice(q * cols, (q + 1) * cols)
        own = take(1)[0][...]
        earlier, following = jnp.where(right, other, own), jnp.where(right, own, other)
        joined = later[:1, at] * earlier + following
        if level == 0:
            start = jnp.where(right, other, 0.0)
        else:
            start = take(1)[0][...]
            start = jnp.where(right, before_row[:1, at] * other + start, start)
        if not last:
            send = jnp.where(half_of(place, level + 1) == 0, joined[:, : cols // 2], joined[:, cols // 2 :]).astype(BF16)
            if q == 0:
                tail = jnp.zeros((16, cols // 2 - heads), BF16)
                lines = jnp.concatenate([totals_to_lines(pair), tail], axis=1)
                send = jnp.concatenate([send, lines], axis=0)
            outs += [joined, start, send]
        else:
            cc_ref, base_ref, cum_ref = take(3)
            g = q * groups // CHUNKS
            here = slice(g * state, (g + 1) * state)
            fade = spread(jnp.exp(-cum_ref[...]), width, q * heads // CHUNKS, heads // CHUNKS)
            carried = mm(cc_ref[:tokens, here], start.astype(BF16))
            outs.append((base_ref[...] + fade * carried).astype(BF16))
            outs.append(mm(cc_ref[tokens:, here], joined.astype(BF16)))
    if last and CHUNKS - 1 in chunks:
        parts = take(2 * (CHUNKS - 1))
        out_parts = [ref[...] for ref in parts[: CHUNKS - 1]] + [outs[-2]]
        raws = [ref[...] for ref in parts[CHUNKS - 1 :]] + [outs[-1]]
        rep = lax.axis_index("rep")
        out_ref, keep_ref, give_ref = refs
        rows = keep_ref.shape[0]
        for q in range(CHUNKS):
            at = slice(q * cols, (q + 1) * cols)
            out_ref[:, at] = out_parts[q]
            keep_ref[:, at] = jnp.where(rep == 0, raws[q][:rows], raws[q][rows:])
            give_ref[:, at] = jnp.where(rep == 0, raws[q][rows:], raws[q][:rows]).astype(BF16)
    else:
        for ref, value in zip(refs, outs, strict=True):
            ref[...] = value


def projections_kernel(c_ref, mine_ref, other_ref, out_ref):
    rep = lax.axis_index("rep")
    tokens, groups, state = c_ref.shape
    steps = mine_ref.shape[1]
    mine, other = mine_ref[0].astype(F32), other_ref[0].astype(F32)
    zero, one = jnp.where(rep == 0, mine, other), jnp.where(rep == 0, other, mine)
    prefix = c_ref[...].astype(F32)
    for g in range(groups):
        at = slice(g * state, (g + 1) * state)
        out_ref[:tokens, at] = prefix[:, g, :].astype(BF16)
        for i, c in enumerate((zero, one)):
            part = jnp.where(rep == 0, c[:, g, :], c[:, groups + g, :])
            out_ref[tokens + i * steps : tokens + (i + 1) * steps, at] = part.astype(BF16)


def first_kernel(*refs, q, cols, groups, heads, tokens, state):
    refs = list(refs)
    w_ref, b_ref, own_w_ref, own_b_ref = refs[:4]
    refs = refs[4:]
    left = lax.axis_index("seq") < 2
    width = cols * CHUNKS // heads
    other = mm_tn(b_ref[:tokens, cols : cols + state], w_ref[:tokens, :cols])
    if q == 0:
        mine_ref, own_row_ref, near_row_ref, near_ref, send_ref = refs
        mine = mine_ref[:1, :]
        near = lines_to_totals(w_ref[tokens:, :heads])
        own_row, near_row = as_row(mine, width), as_row(near, width)
        own_row_ref[...] = own_row
        near_row_ref[...] = near_row
        near_ref[...] = jnp.broadcast_to(near, (8, heads))
        send_ref[state:, :] = jnp.zeros((16, cols), BF16)
        send_ref[state:, :heads] = totals_to_lines(mine * near)
    else:
        own_row_ref, near_row_ref = refs[:2]
        refs = refs[2:]
        if q == 1:
            kv_ref, pair_ref = refs[0], refs.pop()
            refs = refs[1:]
            pair_ref[:tokens, :] = kv_ref[...]
            pair_ref[tokens:, :] = w_ref[:, w_ref.shape[1] - kv_ref.shape[1] :]
        (send_ref,) = refs
        own_row, near_row = own_row_ref[...], near_row_ref[...]
    at = slice(q * cols, (q + 1) * cols)
    local = mm_tn(own_b_ref[:tokens, cols : cols + state], own_w_ref[:tokens, :cols])
    after = own_row[:1, at] * other + local
    beyond = other + near_row[:1, at] * local
    send_ref[:state, :] = jnp.where(left, after, beyond).astype(BF16)


def second_kernel(*refs, q, cols, groups, heads, tokens, state):
    refs = list(refs)
    got_ref, w_ref, b_ref, own_w_ref, own_b_ref, own_row_ref, cc_ref, near_cc_ref = refs[:8]
    refs = refs[8:]
    place = lax.axis_index("seq")
    left, inner = place < 2, (place == 1) | (place == 2)
    width = cols * CHUNKS // heads
    at = slice(q * cols, (q + 1) * cols)
    g = q * groups // CHUNKS
    here = slice(g * state, (g + 1) * state)
    rows = cc_ref.shape[0]
    if q == 0:
        mine_ref, near_ref, later_row_ref, carried_ref, cand_ref, send_ref = refs
        later = jnp.where(left, lines_to_totals(got_ref[state:, :heads]), near_ref[:1, :])
        later_row = as_row(later, width)
        later_row_ref[...] = later_row
        send_ref[rows:, :] = jnp.zeros((16, cols), BF16)
        send_ref[rows:, :heads] = totals_to_lines(later * mine_ref[:1, :])
    else:
        if q == 1:
            kv_ref = refs.pop(0)
            held = kv_ref.shape[0] // (cols // kv_ref.shape[1])
            for i in range(cols // kv_ref.shape[1]):
                part = slice(i * kv_ref.shape[1], (i + 1) * kv_ref.shape[1])
                refs[-1][rows:, part] = kv_ref[i * held : (i + 1) * held, :]
        later_row_ref, carried_ref, cand_ref, send_ref = refs
        later_row = later_row_ref[...]
    got = got_ref[:state, :].astype(F32)
    other = mm_tn(b_ref[:tokens, cols : cols + state], w_ref[:tokens, :cols])
    local = mm_tn(own_b_ref[:tokens, cols : cols + state], own_w_ref[:tokens, :cols])
    start, beyond = jnp.where(left, other, got), jnp.where(left, got, other)
    start = jnp.where(inner, start, 0.0)
    after = own_row_ref[:1, at] * start + local
    lasting = later_row[:1, at]
    state_out = jnp.where(left, beyond + lasting * local, after)
    send_ref[:rows, :] = mm(near_cc_ref[:, here], state_out.astype(BF16)).astype(BF16)
    final = jnp.where(inner, lasting * after + beyond, local)
    carried_ref[...] = mm(cc_ref[:tokens, here], start.astype(BF16))
    cand_ref[...] = mm(cc_ref[tokens:, here], final.astype(BF16))


def third_kernel(*refs, q, cols, heads, tokens):
    refs = list(refs)
    got_ref, cand_ref, own_row_ref = refs[:3]
    place = lax.axis_index("seq")
    width = cols * CHUNKS // heads
    at = slice(q * cols, (q + 1) * cols)
    rows = cand_ref.shape[0]
    refs = refs[3:]
    if q == 0:
        later_row_ref = refs[0]
        later_row = as_row(lines_to_totals(got_ref[tokens + rows :, :heads]), width)
        later_row_ref[...] = later_row
    else:
        later_row = refs[0][...]
    refs = refs[1:]
    cand = cand_ref[...]
    got = got_ref[tokens : tokens + rows, :].astype(F32)
    cand = jnp.where(
        place == 3,
        own_row_ref[:1, at] * got + cand,
        jnp.where(place == 0, later_row[:1, at] * cand + got, cand),
    )
    if q < CHUNKS - 1:
        (raw_ref,) = refs
        raw_ref[...] = cand
        return
    raws, (keep_ref, give_ref) = refs[:-2], refs[-2:]
    rep = lax.axis_index("rep")
    half = rows // 2
    for i in range(CHUNKS):
        at = slice(i * cols, (i + 1) * cols)
        raw = cand if i == q else raws[i][...]
        keep_ref[:, at] = jnp.where(rep == 0, raw[:half], raw[half:])
        give_ref[:, at] = jnp.where(rep == 0, raw[half:], raw[:half]).astype(BF16)


def prefix_kernel(*refs, first, cols, tokens):
    refs, (out_any, buffer, sem) = refs[:-3], refs[-3:]
    last = lax.axis_index("seq") == 3
    count = len(refs) // 4
    if len(refs) % 4:
        refs[-1][...] = jnp.zeros(refs[-1].shape, F32)
        refs = refs[:-1]
    for i in range(count):
        got_ref, carried_ref, base_ref, fade_ref = refs[i::count]
        carried = jnp.where(last, got_ref[:tokens, :].astype(F32), carried_ref[...])
        buffer[:, i * cols : (i + 1) * cols] = (base_ref[...] + fade_ref[...] * carried).astype(BF16)
    copy = pltpu.make_async_copy(buffer, out_any.at[:, pl.ds(first * cols, count * cols)], sem.at[0])
    copy.start()
    copy.wait()


def intra_kernel(x_ref, b2_ref, c2_ref, cum_ref, skip_ref, *base_refs, groups):
    tokens, heads = cum_ref.shape
    width = x_ref.shape[1] // heads
    state = c2_ref.shape[1] // groups
    per_group = heads // groups
    first = (lax.axis_index("head") * lax.axis_size("rep") + lax.axis_index("rep")) * heads
    skip = spread(jnp.broadcast_to(skip_ref[...], (8, skip_ref.shape[1])), width, first, heads)[:1]
    cum = cum_ref[...]
    cum_t = cum.T
    shape = (tokens, tokens)
    hidden = jnp.where(iota(shape, 0) >= iota(shape, 1), 0.0, NEG)
    pair = 2 * width
    lane = iota((tokens, pair), 1)
    for g in range(groups):
        here = slice(g * state, (g + 1) * state)
        gram = mm_nt(c2_ref[:tokens, here], b2_ref[:, here])
        for h in range(g * per_group, (g + 1) * per_group, 2):
            mixing = []
            for i in (h, h + 1):
                gap = cum_t[i : i + 1, :] - jnp.broadcast_to(cum[:, i : i + 1], shape)
                mixing.append((jnp.exp(gap + hidden) * gram).astype(BF16))
            at = slice(h * width, (h + 2) * width)
            x = x_ref[:, at]
            zero = jnp.zeros_like(x)
            inputs = jnp.concatenate(
                [jnp.where(lane < width, x, zero), jnp.where(lane < width, zero, x)], axis=0
            )
            q, start = divmod(h * width, base_refs[0].shape[1])
            base_refs[q][:, start : start + pair] = (
                mm(jnp.concatenate(mixing, axis=1), inputs) + skip[:, at] * x.astype(F32)
            )


def cand_kernel(x_ref, b_ref, c_ref, decay_ref, skip_ref, *refs):
    if len(refs) > 2:
        cum_ref, *fall_refs = refs[:-2]
        cols = fall_refs[0].shape[1]
        fall = spread(jnp.exp(-cum_ref[...]), cols * len(fall_refs) // cum_ref.shape[1])
        for i, ref in enumerate(fall_refs):
            ref[...] = fall[:, i * cols : (i + 1) * cols]
    base_ref, fade_ref = refs[-2:]
    steps, groups, state = b_ref.shape[1:]
    heads = decay_ref.shape[2]
    width = x_ref.shape[2] // heads
    per_group = heads // groups
    first = lax.axis_index("head") * heads
    skip = spread(jnp.broadcast_to(skip_ref[...], (8, skip_ref.shape[1])), width, first, heads)[:1]
    lower = (iota((steps, steps), 0) >= iota((steps, steps), 1)).astype(F32)
    cum = exact(lower, decay_ref[0])
    fade_ref[...] = spread(jnp.exp(-cum), width)
    wide = (steps, heads * steps)
    cum_t = spread(cum, steps)
    place = iota(wide, 1) % steps
    row = iota(wide, 0)
    cum_s = jnp.sum(jnp.where(row == place, cum_t, 0.0), axis=0, keepdims=True)
    fall = jnp.exp(jnp.where(row >= place, cum_s - cum_t, NEG))
    b = b_ref[0].astype(F32)
    c = c_ref[0].astype(F32)
    quad = 128 // steps
    shape = (quad * steps, quad * width)
    mine = iota(shape, 0) // steps == iota(shape, 1) // width
    for g in range(groups):
        b_g = b[:, g, :].astype(BF16)
        gram = mm_nt(c[:, g, :].astype(BF16), jnp.concatenate([b_g] * quad, axis=0))
        for h in range(g * per_group, (g + 1) * per_group, quad):
            mixing = (fall[:, h * steps : (h + quad) * steps] * gram).astype(BF16)
            at = slice(h * width, (h + quad) * width)
            x = x_ref[0, :, at]
            tall = jnp.concatenate([x] * quad, axis=0)
            inputs = jnp.where(mine, tall, jnp.zeros_like(tall))
            base_ref[:, at] = mm(mixing, inputs) + skip[:, at] * x.astype(F32)


def attend_kernel(length_ref, q_ref, own_k_ref, own_v_ref, k_ref, v_ref, mine_ref, other_ref, mark_ref, out_any, out_ref, sem):
    mark_ref[...] = jnp.zeros(mark_ref.shape, F32)
    rep = lax.axis_index("rep")
    steps, heads, dim = q_ref.shape[1:]
    kv_heads = own_k_ref.shape[2]
    per_kv = heads // kv_heads
    rows = steps * per_kv
    mine, other = mine_ref[...], other_ref[...]
    keys, values = jnp.where(rep == 0, mine, other), jnp.where(rep == 0, other, mine)
    q = q_ref[0].astype(F32)
    own_k = own_k_ref[0].astype(F32)
    own_v = own_v_ref[0].astype(F32)
    block_k = k_ref[...].astype(F32)
    block_v = v_ref[...].astype(F32)
    scale = dim ** (-0.5)
    step_of = iota((rows, steps), 0) // per_kv
    visible = step_of >= iota((rows, steps), 1)
    live = iota((rows, dim), 0) // per_kv < length_ref[0]
    mixed_of = []
    for j in range(kv_heads):
        query = q[:, j * per_kv : (j + 1) * per_kv, :].reshape(rows, dim).astype(BF16)

        def gather(far, block):
            return jnp.concatenate([far[:, j * dim : (j + 1) * dim], block[:, j, :].astype(BF16)], axis=0)

        far = mm_nt(query, gather(keys, block_k)) * scale
        near = jnp.where(visible, mm_nt(query, own_k[:, j, :].astype(BF16)) * scale, NEG)
        top = jnp.maximum(jnp.max(far, axis=1, keepdims=True), jnp.max(near, axis=1, keepdims=True))
        far = jnp.exp(far - top)
        near = jnp.exp(near - top)
        mass = jnp.sum(far, axis=1, keepdims=True) + jnp.sum(near, axis=1, keepdims=True)
        mixed = mm(far.astype(BF16), gather(values, block_v)) + mm(near.astype(BF16), own_v[:, j, :].astype(BF16))
        mixed = mixed / mass
        mixed = mixed * lax.rsqrt(jnp.mean(mixed * mixed, axis=1, keepdims=True) + EPSILON)
        mixed = jnp.where(live, mixed, 0.0)
        mixed_of.append(mixed.reshape(steps, per_kv, dim))
    out_ref[0] = (jnp.concatenate(mixed_of, axis=1) if kv_heads > 1 else mixed_of[0]).astype(BF16)
    copy = pltpu.make_async_copy(out_ref, out_any, sem.at[0])
    copy.start()
    copy.wait()


def close_kernel(length_ref, base_ref, fade_ref, keep_ref, got_ref, out_ref):
    rep = lax.axis_index("rep")
    keep, got = keep_ref[...], got_ref[...].astype(F32)
    cols = keep.shape[1]
    live = iota(keep.shape, 0) < length_ref[0]
    for i in range(2):
        at = slice(i * cols, (i + 1) * cols)
        carried = jnp.where(rep == i, keep, got)
        result = base_ref[:, at] + fade_ref[:, at] * carried
        out_ref[0, :, at] = jnp.where(live, result, 0.0).astype(BF16)


def call(kernel, name, outs, *args, scalars=0, after=(), cost=0.0, scratch=(), limit=32, gate=(), into=(), raw=False):
    shapes = [jax.ShapeDtypeStruct(shape, dtype) for shape, dtype in outs]
    vmem = pl.BlockSpec(memory_space=pltpu.VMEM)
    smem = pl.BlockSpec(memory_space=pltpu.SMEM)
    anywhere = pl.BlockSpec(memory_space=pl.ANY)
    given = [a for a in into if hasattr(a, "dtype")]
    passed = [*gate, *given]
    count = len(args)
    rest = count + len(after) + len(passed)
    through = rest + len(shapes)
    shapes += [jax.ShapeDtypeStruct(a.shape, a.dtype) for a in gate]
    shapes += [jax.ShapeDtypeStruct(a.shape, a.dtype) if hasattr(a, "dtype") else jax.ShapeDtypeStruct(*a) for a in into]
    aliases = {count + len(after) + i: len(outs) + i for i in range(len(passed))}

    def body(*refs):
        kernel(*refs[:count], *refs[rest:through], *refs[through + len(gate) :])

    return pl.pallas_call(
        body,
        out_shape=shapes,
        in_specs=[smem] * scalars
        + [anywhere if raw else vmem] * (count - scalars)
        + [anywhere] * (len(after) + len(passed)),
        out_specs=[vmem] * len(outs) + [anywhere] * (len(gate) + len(into)),
        input_output_aliases=aliases,
        scratch_shapes=list(scratch),
        compiler_params=pltpu.CompilerParams(vmem_limit_bytes=limit * 2**20),
        cost_estimate=pl.CostEstimate(flops=int(cost * 10**9), bytes_accessed=0, transcendentals=0),
        name=name,
    )(*args, *after, *passed)


def on_device(
    prefix_x,
    prefix_b,
    prefix_c,
    prefix_decay,
    bypass_weight,
    prefix_key_rows,
    prefix_values,
    cand_x,
    cand_b,
    cand_c,
    cand_decay,
    cand_queries,
    cand_keys,
    cand_values,
    cand_length,
):
    size = lax.axis_size("seq")
    levels = size.bit_length() - 1
    assert size == 2**levels and lax.axis_size("rep") == 2
    tokens, groups, state = prefix_b.shape
    heads = prefix_decay.shape[1]
    wide = prefix_x.shape[1]
    steps = cand_x.shape[1]
    cand_wide = cand_x.shape[2]
    cols = wide // CHUNKS
    skip = bypass_weight.reshape(1, -1)
    plan = payload_plan(groups)

    def to_core(array):
        return lax.ppermute(array, "rep", [(0, 1), (1, 0)])

    def to_neighbour(array):
        return lax.ppermute(array, "seq", [(i, i ^ 1) for i in range(size)])

    def to_mirror(array, level):
        return lax.ppermute(array, "seq", [(i, i ^ (2 ** (level + 1) - 1)) for i in range(size)])

    def between_inner(array):
        far = {1: 2, 2: 1}
        pairs = [(2 * i + r, 2 * far[i] + r if i in far else 2 * i + 1 - r) for i in range(size) for r in range(2)]
        return lax.ppermute(array, ("seq", "rep"), pairs)

    def inward(array):
        return lax.ppermute(array, "seq", [(0, 1), (3, 2)])

    other_c = to_core(cand_c)
    kv_shape = (tokens, prefix_key_rows.shape[1] * prefix_key_rows.shape[2])
    cum, total, b2, kv, *loads = call(
        inputs_kernel,
        "inputs",
        [((tokens, heads), F32), ((8, heads), F32), ((tokens, groups * state), BF16), (kv_shape, BF16)]
        + [
            (
                (
                    tokens + (16 if q == 0 else 0),
                    cols + len(fresh) * state + (kv_shape[1] if q == 1 else 0),
                ),
                BF16,
            )
            for q, fresh in enumerate(plan)
        ],
        prefix_x,
        prefix_b,
        prefix_decay.T,
        prefix_key_rows,
        prefix_values,
        scratch=[
            pltpu.VMEM(prefix_x.shape, BF16),
            pltpu.VMEM(prefix_b.shape, BF16),
            pltpu.VMEM((heads, tokens), F32),
            pltpu.VMEM(prefix_key_rows.shape, BF16),
            pltpu.VMEM(prefix_values.shape, BF16),
            pltpu.SemaphoreType.DMA((5,)),
        ],
        raw=True,
        limit=60,
    )
    (cc,) = call(
        projections_kernel,
        "projections",
        [((tokens + 2 * steps, groups * state), BF16)],
        prefix_c,
        cand_c,
        other_c,
        after=(cum,),
    )
    first_of = {g: q for q, fresh in enumerate(plan) for g in fresh}
    def intra(mark, cc):
        return call(
            functools.partial(intra_kernel, groups=groups),
            "intra",
            [((tokens, cols), F32)] * CHUNKS,
            prefix_x,
            b2,
            cc,
            cum,
            skip,
            after=(mark,),
            gate=(loads[1],),
        )

    def candidates(mark, *more):
        return call(
            cand_kernel,
            "candidates",
            [((tokens, cols), F32)] * (CHUNKS * len(more)) + [((steps, cand_wide), F32), ((steps, cand_wide), F32)],
            cand_x,
            cand_b,
            cand_c,
            cand_decay,
            skip,
            *more,
            after=(mark,),
        )

    def attend(mark, pieces, inner):
        (mine,) = call(
            functools.partial(collect_kernel, inner=inner),
            "collect",
            [((tokens * (size - 1), kv_shape[1]), BF16)],
            *pieces,
            after=(mark,),
        )
        theirs = to_core(mine)

        def finish(mark):
            return call(
                attend_kernel,
                "attend",
                [((8, 128), F32)],
                cand_length,
                cand_queries,
                cand_keys,
                cand_values,
                prefix_key_rows,
                prefix_values,
                mine,
                theirs,
                scalars=1,
                after=(mark,),
                into=((cand_queries.shape, BF16),),
                scratch=[pltpu.VMEM(cand_queries.shape, BF16), pltpu.SemaphoreType.DMA((1,))],
            )

        return mine, finish

    shared = dict(cols=cols, heads=heads, tokens=tokens)
    if size == 4:
        mark = cc
        middle, carried, cands, outer, outs, raws = {}, {}, {}, {}, [], []
        rows = {"cc": cc}

        def inputs_of(q):
            p = first_of[q * groups // CHUNKS]
            return got[q], got[p], loads[q], loads[p]

        def first(q, mark):
            extra = [((8, wide), F32), ((8, wide), F32), ((8, heads), F32)] if q == 0 else []
            results = call(
                functools.partial(first_kernel, q=q, groups=groups, state=state, **shared),
                "first",
                extra
                + [((state + (16 if q == 0 else 0), cols), BF16)]
                + ([((2 * tokens, kv_shape[1]), BF16)] if q == 1 else []),
                *inputs_of(q),
                *([total] if q == 0 else [rows["own"], rows["near"]]),
                *([kv] if q == 1 else []),
                after=(mark,),
                cost=FIRST_COST if q == 1 else 0.0,
                gate=[(rows["cc"],), loads[2:], (), ()][q],
            )
            if q == 0:
                *results, rows["cc"] = results
                rows["near_cc"] = to_neighbour(rows["cc"])
            elif q == 1:
                *results, loads[2], loads[3] = results
                got.extend((to_neighbour(loads[2]), inward(loads[3])))
            if q == 0:
                rows["own"], rows["near"], rows["near_total"], *results = results
            middle[q] = between_inner(results[0])
            if q == 1:
                rows["kv"] = results[1]
            return results[0]

        def second(q, mark):
            results = call(
                functools.partial(second_kernel, q=q, groups=groups, state=state, **shared),
                "second",
                ([((8, wide), F32)] if q == 0 else [])
                + [
                    ((tokens, cols), F32),
                    ((2 * steps, cols), F32),
                    ((tokens + 2 * steps + [16, 2 * tokens * kv_shape[1] // cols, 0, 0][q], cols), BF16),
                ],
                middle[q],
                *inputs_of(q),
                rows["own"],
                rows["cc"],
                rows["near_cc"],
                *([far_kv] if q == 1 else []),
                *([total, rows["near_total"]] if q == 0 else [rows["later"]]),
                after=(mark,),
                cost=SECOND_COST,
            )
            if q == 0:
                rows["later"], *results = results
            carried[q], cands[q] = results[:2]
            outer[q] = to_neighbour(results[2])
            return results[0]

        def third(q, mark):
            final = q == CHUNKS - 1
            results = call(
                functools.partial(third_kernel, q=q, **shared),
                "third",
                [((steps, wide), F32), ((steps, wide), BF16)]
                if final
                else ([((8, wide), F32)] if q == 0 else []) + [((2 * steps, cols), F32)],
                outer[q],
                cands[q],
                rows["own"],
                *([] if q == 0 else [rows["outer"]]),
                *(raws if final else []),
                after=(mark,),
                cost=THIRD_COST,
            )
            if q == 0:
                rows["outer"], *results = results
            if final:
                return results
            raws.append(results[0])
            return results[0]

        def prefix(start, count, mark, into):
            span = range(start, start + count)
            return call(
                functools.partial(prefix_kernel, first=start, cols=cols, tokens=tokens),
                "prefix",
                [((8, 128), F32)] if start == 0 else [],
                *[each[q] for each in (outer, carried, base, fade) for q in span],
                after=(mark,),
                into=(into,),
                scratch=[pltpu.VMEM((tokens, count * cols), BF16), pltpu.SemaphoreType.DMA((1,))],
            )

        *base, loads[1] = intra(cc, cc)
        got = [to_neighbour(a) for a in loads[:2]]
        mark = first(0, base[0])
        mark = first(1, mark)
        far_kv = between_inner(rows["kv"])
        mark = second(0, mark)
        mark = first(2, mark)
        mark = second(1, mark)
        mark = first(3, mark)
        *fade, cand_base, cand_fade = candidates(mark, cum)
        mark = third(0, cand_base)
        mark = second(2, mark)
        mark = third(1, mark)
        mark, finish_attend = attend(mark, [rows["kv"], far_kv, outer[1]], True)
        mark = second(3, mark)
        mark, cand_attn = finish_attend(mark)
        mark = third(2, mark)
        mark, prefix_out = prefix(0, CHUNKS - 1, mark, (prefix_x.shape, BF16))
        keep, give = third(3, mark)
        (prefix_out,) = prefix(CHUNKS - 1, 1, keep, prefix_out)
    else:
        got = [to_neighbour(a) for a in loads]
        halves = [kv, got[1][:, -kv_shape[1] :]]
        for level in range(1, levels):
            mirrored = to_mirror(halves[0], level)
            halves = [halves[0], halves[1], mirrored, to_neighbour(mirrored)]
            if level < levels - 1:
                halves = [jnp.concatenate([halves[0], halves[2]]), jnp.concatenate([halves[1], halves[3]])]
        *base, loads[1] = intra(cc, cc)
        mark = base[0]
        own = call(
            functools.partial(own_kernel, cols=cols, groups=groups, state=state),
            "own",
            [((state, cols), F32)] * CHUNKS,
            *loads,
        )
        own, start = dict(enumerate(own)), {}
        before = None
        near, far = {}, {}
        outs, raws = [], []
        for level in range(levels):
            last = level == levels - 1
            rows = None
            for q in range(CHUNKS):
                final = last and q == CHUNKS - 1
                if level == 0:
                    args, lines = [got[q], got[first_of[q * groups // CHUNKS]]], got[0]
                else:
                    args, lines = [near[q], far[q]], near[0]
                shapes = []
                if q == 0:
                    args += [total, lines] + ([] if level == 0 else [before])
                    shapes += [((8, wide), F32)] * 2 + [((8, heads), F32)] * 2
                else:
                    args += rows
                args += [own[q]] + ([] if level == 0 else [start[q]])
                if final:
                    args += [cc, base[q], cum] + outs + raws
                    shapes = [((tokens, wide), BF16), ((steps, wide), F32), ((steps, wide), BF16)]
                elif last:
                    args += [cc, base[q], cum]
                    shapes += [((tokens, cols), BF16), ((2 * steps, cols), F32)]
                else:
                    shapes += [((state, cols), F32)] * 2 + [((state + (16 if q == 0 else 0), cols // 2), BF16)]
                results = call(
                    functools.partial(
                        merge_kernel, level=level, last=last, chunks=[q], groups=groups, state=state, **shared
                    ),
                    "merge",
                    shapes,
                    *args,
                    after=(mark,),
                )
                mark = results[0]
                if final:
                    prefix_out, keep, give = results
                    continue
                if q == 0:
                    rows, (total, before) = list(results[:2]), results[2:4]
                if last:
                    outs.append(results[-2])
                    raws.append(results[-1])
                else:
                    own[q], start[q] = results[-3], results[-2]
                    near[q] = to_mirror(results[-1], level + 1)
                    far[q] = to_neighbour(near[q])
            if level == 0:
                cand_base, cand_fade = candidates(mark)
                pieces = ([halves[0][tokens:]] if levels > 2 else []) + halves[1:]
                mark, finish_attend = attend(cand_base, pieces, False)
                mark, cand_attn = finish_attend(mark)
    (cand_ssm,) = call(
        close_kernel,
        "close",
        [((1, steps, cand_wide), BF16)],
        cand_length,
        cand_base,
        cand_fade,
        keep,
        to_core(give),
        scalars=1,
    )
    return (prefix_out, cand_ssm, cand_attn)


def solution(mesh):
    placed = (
        P(("groups", "seq"), ("head", "rep")),
        P(("groups", "seq"), ("head", "rep"), None),
        P(("groups", "seq"), ("head", "rep"), None),
        P(("groups", "seq"), ("head", "rep")),
        P(),
        P(("groups", "seq"), "head", None),
        P(("groups", "seq"), "head", None),
        P(("groups", "seq", "rep"), None, "head"),
        P(("groups", "seq", "rep"), None, "head", None),
        P(("groups", "seq", "rep"), None, "head", None),
        P(("groups", "seq", "rep"), None, "head"),
        P(("groups", "seq", "rep"), None, "head", None),
        P(("groups", "seq", "rep"), None, "head", None),
        P(("groups", "seq", "rep"), None, "head", None),
        P(("groups", "seq", "rep")),
    )
    return jax.shard_map(
        on_device,
        mesh=mesh,
        in_specs=placed,
        out_specs=(
            P(("groups", "seq"), ("head", "rep")),
            P(("groups", "seq", "rep"), None, "head"),
            P(("groups", "seq", "rep"), None, "head", None),
        ),
        check_vma=False,
    )
```

```python
import functools

import jax
import jax.numpy as jnp
from jax import lax
from jax.experimental import pallas as pl
from jax.experimental.pallas import tpu as pltpu
from jax.sharding import PartitionSpec as P

EPSILON = 1e-06
NEG = -1e30
LARGEST = 3.38e38
CHUNKS = 4
PARTS = (8, 8, 8, 8)
SECOND_COST = 1.0
FIRST_COST = 0.0
THIRD_COST = 0.3
F32 = jnp.float32
BF16 = jnp.bfloat16


def mm(a, b):
    return lax.dot_general(a, b, (((1,), (0,)), ((), ())), preferred_element_type=F32)


def mm_nt(a, b):
    return lax.dot_general(a, b, (((1,), (1,)), ((), ())), preferred_element_type=F32)


def mm_tn(a, b):
    return lax.dot_general(a, b, (((0,), (0,)), ((), ())), preferred_element_type=F32)


def exact_nt(a, b):
    return lax.dot_general(
        a, b, (((1,), (1,)), ((), ())), preferred_element_type=F32, precision=lax.Precision.HIGHEST
    )


def exact(a, b):
    return lax.dot_general(
        a, b, (((1,), (0,)), ((), ())), preferred_element_type=F32, precision=lax.Precision.HIGHEST
    )


def iota(shape, dim):
    return lax.broadcasted_iota(jnp.int32, shape, dim)


def split3(a):
    hi = jnp.clip(a, -LARGEST, LARGEST).astype(BF16)
    rest = a - hi.astype(F32)
    mid = rest.astype(BF16)
    return hi, mid, (rest - mid.astype(F32)).astype(BF16)


def spread(a, width, first=0, count=None):
    rows, cols = a.shape
    count = cols if count is None else count
    parts = jnp.concatenate(split3(a), axis=1)
    shape = (3 * cols, count * width)
    source = iota(shape, 0)
    source = jnp.where(source >= 2 * cols, source - 2 * cols, jnp.where(source >= cols, source - cols, source))
    unit = (source == first + iota(shape, 1) // width).astype(F32).astype(BF16)
    return mm(parts, unit)


def group_of(array, g):
    return array.astype(F32)[:, g, :].astype(BF16)


def cut(heads, size):
    if size == 4 and heads % sum(PARTS) == 0:
        return tuple(heads // sum(PARTS) * part for part in PARTS)
    return (heads // CHUNKS,) * CHUNKS


def groups_of(groups, counts):
    of = [sum(counts[:q]) * groups // sum(counts) for q in range(CHUNKS)]
    return of, {g: of.index(g) for g in of}


def columns(q, counts, width):
    return slice(sum(counts[:q]) * width, sum(counts[: q + 1]) * width)


def payload_plan(groups, counts):
    of, first_of = groups_of(groups, counts)
    return [[g] if first_of[g] == q else [] for q, g in enumerate(of)]


def totals_to_lines(total):
    hi, mid, lo = [a.astype(F32) for a in split3(jnp.broadcast_to(total, (16, total.shape[1])))]
    line = iota(hi.shape, 0)
    return jnp.where(line == 0, hi, jnp.where(line == 1, mid, jnp.where(line == 2, lo, 0.0))).astype(BF16)


def lines_to_totals(lines):
    lines = lines.astype(F32)
    return lines[0:1] + lines[1:2] + lines[2:3]


def as_row(total, width):
    return spread(jnp.broadcast_to(total, (8, total.shape[1])), width)


def pack(k_ref, v_ref):
    rep = lax.axis_index("rep")
    kv = jnp.where(rep == 0, k_ref[...].astype(F32), v_ref[...].astype(F32))
    return jnp.concatenate([kv[:, j, :] for j in range(kv.shape[1])], axis=1).astype(BF16)


def inputs_kernel(x_any, b_any, decay_t_any, k_any, v_any, cum_ref, total_ref, b2_ref, kv_ref, *refs, counts):
    load_refs, (x_ref, b_ref, decay_t_ref, k_ref, v_ref, sems) = refs[:-6], refs[-6:]
    pairs = ((decay_t_any, decay_t_ref), (b_any, b_ref), (x_any, x_ref), (k_any, k_ref), (v_any, v_ref))
    copies = [pltpu.make_async_copy(source, target, sems.at[i]) for i, (source, target) in enumerate(pairs)]
    for copy in copies:
        copy.start()
    tokens, groups, state = b_ref.shape
    heads = decay_t_ref.shape[0]
    width = x_ref.shape[1] // heads
    copies[0].wait()
    lower = (iota((tokens, tokens), 0) >= iota((tokens, tokens), 1)).astype(F32)
    cum = exact_nt(lower, decay_t_ref[...])
    cum_ref[...] = cum
    last = cum[tokens - 1 : tokens, :]
    total = jnp.exp(-last)
    total_ref[...] = jnp.broadcast_to(total, (8, heads))
    load_refs[0][tokens:, :] = jnp.zeros((16, load_refs[0].shape[1]), BF16)
    load_refs[0][tokens:, :heads] = totals_to_lines(total)
    weights = spread(jnp.exp(last - cum), width)
    for copy in copies[1:]:
        copy.wait()
    b = b_ref[...].astype(F32)
    for g in range(groups):
        b2_ref[:, g * state : (g + 1) * state] = b[:, g, :].astype(BF16)
    kv = pack(k_ref, v_ref)
    kv_ref[...] = kv
    for q, (fresh, load) in enumerate(zip(payload_plan(groups, counts), load_refs)):
        at = columns(q, counts, width)
        cols = counts[q] * width
        load[:tokens, :cols] = (x_ref[:, at].astype(F32) * weights[:, at]).astype(BF16)
        if fresh:
            load[:tokens, cols : cols + state] = b2_ref[:, fresh[0] * state : (fresh[0] + 1) * state]
        if q == 1:
            load[:, load.shape[1] - kv.shape[1] :] = kv


def own_kernel(*refs, cols, groups, state, counts):
    load_refs, out_refs = refs[:CHUNKS], refs[CHUNKS:]
    tokens = load_refs[1].shape[0]
    of, first_of = groups_of(groups, counts)
    for q in range(CHUNKS):
        b_ref = load_refs[first_of[of[q]]]
        out_refs[q][...] = mm_tn(b_ref[:tokens, cols : cols + state], load_refs[q][:tokens, :cols])


def collect_kernel(*refs, inner):
    refs, out_ref = list(refs[:-1]), refs[-1]
    place = lax.axis_index("seq")
    pieces = [ref[...] for ref in refs]
    if inner:
        pair, far, outer = pieces
        rows, wide = far.shape
        count = outer.shape[1] // wide
        first = outer.shape[0] - rows // count
        outer = jnp.concatenate([outer[first:, i * wide : (i + 1) * wide] for i in range(count)], axis=0)
        pieces = [pair[pair.shape[0] // 2 :], jnp.where((place == 1) | (place == 2), far, outer)]
    at = 0
    for piece in pieces:
        out_ref[at : at + piece.shape[0], :] = piece
        at += piece.shape[0]


def half_of(place, level):
    odd = lax.rem(place, 2)
    return jnp.where(lax.rem(lax.div(place, 2**level), 2) == 0, 1 - odd, odd)


def merge_kernel(*refs, level, last, chunks, cols, groups, heads, tokens, state):
    refs = list(refs)

    def take(count):
        taken = refs[:count]
        del refs[:count]
        return taken

    place = lax.axis_index("seq")
    right = lax.rem(lax.div(place, 2**level), 2) == 1
    width = cols * CHUNKS // heads
    first = 0 in chunks
    outs = []
    others = []
    if level == 0:
        for q in chunks:
            w_ref, b_ref = take(2)
            others.append(mm_tn(b_ref[:tokens, cols : cols + state], w_ref[:tokens, :cols]))
    else:
        half = half_of(place, level)
        for q in chunks:
            near_ref, far_ref = take(2)
            rows = near_ref.shape[0] - 16 if q == 0 else near_ref.shape[0]
            near, far = near_ref[:rows, :], far_ref[:rows, :]
            pieces = [jnp.where(half == 0, near, far), jnp.where(half == 0, far, near)]
            others.append(jnp.concatenate(pieces, axis=1).astype(F32))
    if first:
        mine_ref, lines_ref = take(2)
        mine = mine_ref[:1, :]
        theirs = lines_to_totals(lines_ref[lines_ref.shape[0] - 16 :, :heads])
        later = as_row(jnp.where(right, mine, theirs), width)
        pair = mine * theirs
        if level == 0:
            before = jnp.ones_like(mine)
        else:
            before = take(1)[0][:1, :]
        before_row = as_row(before, width)
        before = jnp.where(right, before * theirs, before)
        outs += [later, before_row, jnp.broadcast_to(pair, (8, heads)), jnp.broadcast_to(before, (8, heads))]
    else:
        later_ref, before_ref = take(2)
        later, before_row = later_ref[...], before_ref[...]
    for q, other in zip(chunks, others, strict=True):
        at = slice(q * cols, (q + 1) * cols)
        own = take(1)[0][...]
        earlier, following = jnp.where(right, other, own), jnp.where(right, own, other)
        joined = later[:1, at] * earlier + following
        if level == 0:
            start = jnp.where(right, other, 0.0)
        else:
            start = take(1)[0][...]
            start = jnp.where(right, before_row[:1, at] * other + start, start)
        if not last:
            send = jnp.where(half_of(place, level + 1) == 0, joined[:, : cols // 2], joined[:, cols // 2 :]).astype(BF16)
            if q == 0:
                tail = jnp.zeros((16, cols // 2 - heads), BF16)
                lines = jnp.concatenate([totals_to_lines(pair), tail], axis=1)
                send = jnp.concatenate([send, lines], axis=0)
            outs += [joined, start, send]
        else:
            cc_ref, base_ref, cum_ref = take(3)
            g = q * groups // CHUNKS
            here = slice(g * state, (g + 1) * state)
            fade = spread(jnp.exp(-cum_ref[...]), width, q * heads // CHUNKS, heads // CHUNKS)
            carried = mm(cc_ref[:tokens, here], start.astype(BF16))
            outs.append((base_ref[...] + fade * carried).astype(BF16))
            outs.append(mm(cc_ref[tokens:, here], joined.astype(BF16)))
    if last and CHUNKS - 1 in chunks:
        parts = take(2 * (CHUNKS - 1))
        out_parts = [ref[...] for ref in parts[: CHUNKS - 1]] + [outs[-2]]
        raws = [ref[...] for ref in parts[CHUNKS - 1 :]] + [outs[-1]]
        rep = lax.axis_index("rep")
        out_ref, keep_ref, give_ref = refs
        rows = keep_ref.shape[0]
        for q in range(CHUNKS):
            at = slice(q * cols, (q + 1) * cols)
            out_ref[:, at] = out_parts[q]
            keep_ref[:, at] = jnp.where(rep == 0, raws[q][:rows], raws[q][rows:])
            give_ref[:, at] = jnp.where(rep == 0, raws[q][rows:], raws[q][:rows]).astype(BF16)
    else:
        for ref, value in zip(refs, outs, strict=True):
            ref[...] = value


def projections_kernel(c_ref, mine_ref, other_ref, out_ref):
    rep = lax.axis_index("rep")
    tokens, groups, state = c_ref.shape
    steps = mine_ref.shape[1]
    mine, other = mine_ref[0].astype(F32), other_ref[0].astype(F32)
    zero, one = jnp.where(rep == 0, mine, other), jnp.where(rep == 0, other, mine)
    prefix = c_ref[...].astype(F32)
    for g in range(groups):
        at = slice(g * state, (g + 1) * state)
        out_ref[:tokens, at] = prefix[:, g, :].astype(BF16)
        for i, c in enumerate((zero, one)):
            part = jnp.where(rep == 0, c[:, g, :], c[:, groups + g, :])
            out_ref[tokens + i * steps : tokens + (i + 1) * steps, at] = part.astype(BF16)


def first_kernel(*refs, q, counts, width, groups, heads, tokens, state):
    refs = list(refs)
    w_ref, b_ref, own_w_ref, own_b_ref = refs[:4]
    refs = refs[4:]
    left = lax.axis_index("seq") < 2
    cols = counts[q] * width
    of, first_of = groups_of(groups, counts)
    at_b = slice(counts[first_of[of[q]]] * width, counts[first_of[of[q]]] * width + state)
    other = mm_tn(b_ref[:tokens, at_b], w_ref[:tokens, :cols])
    if q == 0:
        mine_ref, own_row_ref, near_row_ref, near_ref, send_ref = refs
        mine = mine_ref[:1, :]
        near = lines_to_totals(w_ref[tokens:, :heads])
        own_row, near_row = as_row(mine, width), as_row(near, width)
        own_row_ref[...] = own_row
        near_row_ref[...] = near_row
        near_ref[...] = jnp.broadcast_to(near, (8, heads))
        send_ref[state:, :] = jnp.zeros((16, cols), BF16)
        send_ref[state:, :heads] = totals_to_lines(mine * near)
    else:
        own_row_ref, near_row_ref = refs[:2]
        refs = refs[2:]
        if q == 1:
            kv_ref, pair_ref = refs[0], refs.pop()
            refs = refs[1:]
            pair_ref[:tokens, :] = kv_ref[...]
            pair_ref[tokens:, :] = w_ref[:, w_ref.shape[1] - kv_ref.shape[1] :]
        (send_ref,) = refs
        own_row, near_row = own_row_ref[...], near_row_ref[...]
    at = columns(q, counts, width)
    local = mm_tn(own_b_ref[:tokens, at_b], own_w_ref[:tokens, :cols])
    after = own_row[:1, at] * other + local
    beyond = other + near_row[:1, at] * local
    send_ref[:state, :] = jnp.where(left, after, beyond).astype(BF16)


def second_kernel(*refs, q, counts, width, groups, heads, tokens, state, make):
    refs = list(refs)
    got_ref, w_ref, b_ref, own_w_ref, own_b_ref, own_row_ref, cc_ref, near_cc_ref = refs[:8]
    refs = refs[8:]
    if make == "send":
        refs[-1:] = [None, None, refs[-1]]
    elif make == "keep":
        refs.append(None)
    place = lax.axis_index("seq")
    left, inner = place < 2, (place == 1) | (place == 2)
    cols = counts[q] * width
    at = columns(q, counts, width)
    of, first_of = groups_of(groups, counts)
    at_b = slice(counts[first_of[of[q]]] * width, counts[first_of[of[q]]] * width + state)
    here = slice(of[q] * state, (of[q] + 1) * state)
    rows = cc_ref.shape[0]
    if q == 0:
        mine_ref, near_ref, later_row_ref, carried_ref, cand_ref, send_ref = refs
        later = jnp.where(left, lines_to_totals(got_ref[state:, :heads]), near_ref[:1, :])
        later_row = as_row(later, width)
        later_row_ref[...] = later_row
        send_ref[rows:, :] = jnp.zeros((16, cols), BF16)
        send_ref[rows:, :heads] = totals_to_lines(later * mine_ref[:1, :])
    else:
        if q == 1:
            kv_ref = refs.pop(0)
            held = kv_ref.shape[0] // (cols // kv_ref.shape[1])
            for i in range(cols // kv_ref.shape[1]):
                part = slice(i * kv_ref.shape[1], (i + 1) * kv_ref.shape[1])
                refs[-1][rows:, part] = kv_ref[i * held : (i + 1) * held, :]
        later_row_ref, carried_ref, cand_ref, send_ref = refs
        later_row = later_row_ref[...]
    got = got_ref[:state, :].astype(F32)
    other = mm_tn(b_ref[:tokens, at_b], w_ref[:tokens, :cols])
    local = mm_tn(own_b_ref[:tokens, at_b], own_w_ref[:tokens, :cols])
    start, beyond = jnp.where(left, other, got), jnp.where(left, got, other)
    start = jnp.where(inner, start, 0.0)
    after = own_row_ref[:1, at] * start + local
    lasting = later_row[:1, at]
    if make != "keep":
        state_out = jnp.where(left, beyond + lasting * local, after)
        send_ref[:rows, :] = mm(near_cc_ref[:, here], state_out.astype(BF16)).astype(BF16)
    if make == "send":
        return
    final = jnp.where(inner, lasting * after + beyond, local)
    carried_ref[...] = mm(cc_ref[:tokens, here], start.astype(BF16))
    cand_ref[...] = mm(cc_ref[tokens:, here], final.astype(BF16))


def third_kernel(*refs, q, counts, width, heads, tokens):
    refs = list(refs)
    got_ref, cand_ref, own_row_ref = refs[:3]
    place = lax.axis_index("seq")
    at = columns(q, counts, width)
    rows = cand_ref.shape[0]
    refs = refs[3:]
    if q == 0:
        later_row_ref = refs[0]
        later_row = as_row(lines_to_totals(got_ref[tokens + rows :, :heads]), width)
        later_row_ref[...] = later_row
    else:
        later_row = refs[0][...]
    refs = refs[1:]
    cand = cand_ref[...]
    got = got_ref[tokens : tokens + rows, :].astype(F32)
    cand = jnp.where(
        place == 3,
        own_row_ref[:1, at] * got + cand,
        jnp.where(place == 0, later_row[:1, at] * cand + got, cand),
    )
    if q < CHUNKS - 1:
        (raw_ref,) = refs
        raw_ref[...] = cand
        return
    raws, (keep_ref, give_ref) = refs[:-2], refs[-2:]
    rep = lax.axis_index("rep")
    half = rows // 2
    for i in range(CHUNKS):
        at = columns(i, counts, width)
        raw = cand if i == q else raws[i][...]
        keep_ref[:, at] = jnp.where(rep == 0, raw[:half], raw[half:])
        give_ref[:, at] = jnp.where(rep == 0, raw[half:], raw[:half]).astype(BF16)


def prefix_kernel(*refs, first, tokens):
    refs, (out_any, buffer, sem) = refs[:-3], refs[-3:]
    last = lax.axis_index("seq") == 3
    count = len(refs) // 4
    if len(refs) % 4:
        refs[-1][...] = jnp.zeros(refs[-1].shape, F32)
        refs = refs[:-1]
    at = 0
    for i in range(count):
        got_ref, carried_ref, base_ref, fade_ref = refs[i::count]
        carried = jnp.where(last, got_ref[:tokens, :].astype(F32), carried_ref[...])
        buffer[:, at : at + base_ref.shape[1]] = (base_ref[...] + fade_ref[...] * carried).astype(BF16)
        at += base_ref.shape[1]
    copy = pltpu.make_async_copy(buffer, out_any.at[:, pl.ds(first, at)], sem.at[0])
    copy.start()
    copy.wait()


def intra_kernel(x_ref, b2_ref, c2_ref, cum_ref, skip_ref, *base_refs, groups):
    tokens, heads = cum_ref.shape
    width = x_ref.shape[1] // heads
    state = c2_ref.shape[1] // groups
    per_group = heads // groups
    first = (lax.axis_index("head") * lax.axis_size("rep") + lax.axis_index("rep")) * heads
    skip = spread(jnp.broadcast_to(skip_ref[...], (8, skip_ref.shape[1])), width, first, heads)[:1]
    cum = cum_ref[...]
    cum_t = cum.T
    shape = (tokens, tokens)
    hidden = jnp.where(iota(shape, 0) >= iota(shape, 1), 0.0, NEG)
    pair = 2 * width
    lane = iota((tokens, pair), 1)
    for g in range(groups):
        here = slice(g * state, (g + 1) * state)
        gram = mm_nt(c2_ref[:tokens, here], b2_ref[:, here])
        for h in range(g * per_group, (g + 1) * per_group, 2):
            mixing = []
            for i in (h, h + 1):
                gap = cum_t[i : i + 1, :] - jnp.broadcast_to(cum[:, i : i + 1], shape)
                mixing.append((jnp.exp(gap + hidden) * gram).astype(BF16))
            at = slice(h * width, (h + 2) * width)
            x = x_ref[:, at]
            zero = jnp.zeros_like(x)
            inputs = jnp.concatenate(
                [jnp.where(lane < width, x, zero), jnp.where(lane < width, zero, x)], axis=0
            )
            q, start = 0, h * width
            while start >= base_refs[q].shape[1]:
                start -= base_refs[q].shape[1]
                q += 1
            base_refs[q][:, start : start + pair] = (
                mm(jnp.concatenate(mixing, axis=1), inputs) + skip[:, at] * x.astype(F32)
            )


def cand_kernel(x_ref, b_ref, c_ref, decay_ref, skip_ref, *refs):
    if len(refs) > 2:
        cum_ref, *fall_refs = refs[:-2]
        fall = spread(jnp.exp(-cum_ref[...]), sum(ref.shape[1] for ref in fall_refs) // cum_ref.shape[1])
        at = 0
        for ref in fall_refs:
            ref[...] = fall[:, at : at + ref.shape[1]]
            at += ref.shape[1]
    base_ref, fade_ref = refs[-2:]
    steps, groups, state = b_ref.shape[1:]
    heads = decay_ref.shape[2]
    width = x_ref.shape[2] // heads
    per_group = heads // groups
    first = lax.axis_index("head") * heads
    skip = spread(jnp.broadcast_to(skip_ref[...], (8, skip_ref.shape[1])), width, first, heads)[:1]
    lower = (iota((steps, steps), 0) >= iota((steps, steps), 1)).astype(F32)
    cum = exact(lower, decay_ref[0])
    fade_ref[...] = spread(jnp.exp(-cum), width)
    wide = (steps, heads * steps)
    cum_t = spread(cum, steps)
    place = iota(wide, 1) % steps
    row = iota(wide, 0)
    cum_s = jnp.sum(jnp.where(row == place, cum_t, 0.0), axis=0, keepdims=True)
    fall = jnp.exp(jnp.where(row >= place, cum_s - cum_t, NEG))
    b = b_ref[0].astype(F32)
    c = c_ref[0].astype(F32)
    quad = 128 // steps
    shape = (quad * steps, quad * width)
    mine = iota(shape, 0) // steps == iota(shape, 1) // width
    for g in range(groups):
        b_g = b[:, g, :].astype(BF16)
        gram = mm_nt(c[:, g, :].astype(BF16), jnp.concatenate([b_g] * quad, axis=0))
        for h in range(g * per_group, (g + 1) * per_group, quad):
            mixing = (fall[:, h * steps : (h + quad) * steps] * gram).astype(BF16)
            at = slice(h * width, (h + quad) * width)
            x = x_ref[0, :, at]
            tall = jnp.concatenate([x] * quad, axis=0)
            inputs = jnp.where(mine, tall, jnp.zeros_like(tall))
            base_ref[:, at] = mm(mixing, inputs) + skip[:, at] * x.astype(F32)


def attend_kernel(length_ref, q_ref, own_k_ref, own_v_ref, k_ref, v_ref, mine_ref, other_ref, mark_ref, out_any, out_ref, sem):
    mark_ref[...] = jnp.zeros(mark_ref.shape, F32)
    rep = lax.axis_index("rep")
    steps, heads, dim = q_ref.shape[1:]
    kv_heads = own_k_ref.shape[2]
    per_kv = heads // kv_heads
    rows = steps * per_kv
    mine, other = mine_ref[...], other_ref[...]
    keys, values = jnp.where(rep == 0, mine, other), jnp.where(rep == 0, other, mine)
    q = q_ref[0].astype(F32)
    own_k = own_k_ref[0].astype(F32)
    own_v = own_v_ref[0].astype(F32)
    block_k = k_ref[...].astype(F32)
    block_v = v_ref[...].astype(F32)
    scale = dim ** (-0.5)
    step_of = iota((rows, steps), 0) // per_kv
    visible = step_of >= iota((rows, steps), 1)
    live = iota((rows, dim), 0) // per_kv < length_ref[0]
    mixed_of = []
    for j in range(kv_heads):
        query = q[:, j * per_kv : (j + 1) * per_kv, :].reshape(rows, dim).astype(BF16)

        def gather(far, block):
            return jnp.concatenate([far[:, j * dim : (j + 1) * dim], block[:, j, :].astype(BF16)], axis=0)

        far = mm_nt(query, gather(keys, block_k)) * scale
        near = jnp.where(visible, mm_nt(query, own_k[:, j, :].astype(BF16)) * scale, NEG)
        top = jnp.maximum(jnp.max(far, axis=1, keepdims=True), jnp.max(near, axis=1, keepdims=True))
        far = jnp.exp(far - top)
        near = jnp.exp(near - top)
        mass = jnp.sum(far, axis=1, keepdims=True) + jnp.sum(near, axis=1, keepdims=True)
        mixed = mm(far.astype(BF16), gather(values, block_v)) + mm(near.astype(BF16), own_v[:, j, :].astype(BF16))
        mixed = mixed / mass
        mixed = mixed * lax.rsqrt(jnp.mean(mixed * mixed, axis=1, keepdims=True) + EPSILON)
        mixed = jnp.where(live, mixed, 0.0)
        mixed_of.append(mixed.reshape(steps, per_kv, dim))
    out_ref[0] = (jnp.concatenate(mixed_of, axis=1) if kv_heads > 1 else mixed_of[0]).astype(BF16)
    copy = pltpu.make_async_copy(out_ref, out_any, sem.at[0])
    copy.start()
    copy.wait()


def close_kernel(length_ref, base_ref, fade_ref, keep_ref, got_ref, out_ref):
    rep = lax.axis_index("rep")
    keep, got = keep_ref[...], got_ref[...].astype(F32)
    cols = keep.shape[1]
    live = iota(keep.shape, 0) < length_ref[0]
    for i in range(2):
        at = slice(i * cols, (i + 1) * cols)
        carried = jnp.where(rep == i, keep, got)
        result = base_ref[:, at] + fade_ref[:, at] * carried
        out_ref[0, :, at] = jnp.where(live, result, 0.0).astype(BF16)


def call(kernel, name, outs, *args, scalars=0, after=(), cost=0.0, scratch=(), limit=32, gate=(), into=(), raw=False):
    shapes = [jax.ShapeDtypeStruct(shape, dtype) for shape, dtype in outs]
    vmem = pl.BlockSpec(memory_space=pltpu.VMEM)
    smem = pl.BlockSpec(memory_space=pltpu.SMEM)
    anywhere = pl.BlockSpec(memory_space=pl.ANY)
    given = [a for a in into if hasattr(a, "dtype")]
    passed = [*gate, *given]
    count = len(args)
    rest = count + len(after) + len(passed)
    through = rest + len(shapes)
    shapes += [jax.ShapeDtypeStruct(a.shape, a.dtype) for a in gate]
    shapes += [jax.ShapeDtypeStruct(a.shape, a.dtype) if hasattr(a, "dtype") else jax.ShapeDtypeStruct(*a) for a in into]
    aliases = {count + len(after) + i: len(outs) + i for i in range(len(passed))}

    def body(*refs):
        kernel(*refs[:count], *refs[rest:through], *refs[through + len(gate) :])

    return pl.pallas_call(
        body,
        out_shape=shapes,
        in_specs=[smem] * scalars
        + [anywhere if raw else vmem] * (count - scalars)
        + [anywhere] * (len(after) + len(passed)),
        out_specs=[vmem] * len(outs) + [anywhere] * (len(gate) + len(into)),
        input_output_aliases=aliases,
        scratch_shapes=list(scratch),
        compiler_params=pltpu.CompilerParams(vmem_limit_bytes=limit * 2**20),
        cost_estimate=pl.CostEstimate(flops=int(cost * 10**9), bytes_accessed=0, transcendentals=0),
        name=name,
    )(*args, *after, *passed)


def on_device(
    prefix_x,
    prefix_b,
    prefix_c,
    prefix_decay,
    bypass_weight,
    prefix_key_rows,
    prefix_values,
    cand_x,
    cand_b,
    cand_c,
    cand_decay,
    cand_queries,
    cand_keys,
    cand_values,
    cand_length,
):
    size = lax.axis_size("seq")
    levels = size.bit_length() - 1
    assert size == 2**levels and lax.axis_size("rep") == 2
    tokens, groups, state = prefix_b.shape
    heads = prefix_decay.shape[1]
    wide = prefix_x.shape[1]
    steps = cand_x.shape[1]
    cand_wide = cand_x.shape[2]
    cols = wide // CHUNKS
    skip = bypass_weight.reshape(1, -1)
    counts = cut(heads, size)
    width = wide // heads
    plan = payload_plan(groups, counts)

    def to_core(array):
        return lax.ppermute(array, "rep", [(0, 1), (1, 0)])

    def to_neighbour(array):
        return lax.ppermute(array, "seq", [(i, i ^ 1) for i in range(size)])

    def to_mirror(array, level):
        return lax.ppermute(array, "seq", [(i, i ^ (2 ** (level + 1) - 1)) for i in range(size)])

    def between_inner(array):
        far = {1: 2, 2: 1}
        pairs = [(2 * i + r, 2 * far[i] + r if i in far else 2 * i + 1 - r) for i in range(size) for r in range(2)]
        return lax.ppermute(array, ("seq", "rep"), pairs)

    def inward(array):
        return lax.ppermute(array, "seq", [(0, 1), (3, 2)])

    other_c = to_core(cand_c)
    kv_shape = (tokens, prefix_key_rows.shape[1] * prefix_key_rows.shape[2])
    cum, total, b2, kv, *loads = call(
        functools.partial(inputs_kernel, counts=counts),
        "inputs",
        [((tokens, heads), F32), ((8, heads), F32), ((tokens, groups * state), BF16), (kv_shape, BF16)]
        + [
            (
                (
                    tokens + (16 if q == 0 else 0),
                    counts[q] * width + len(fresh) * state + (kv_shape[1] if q == 1 else 0),
                ),
                BF16,
            )
            for q, fresh in enumerate(plan)
        ],
        prefix_x,
        prefix_b,
        prefix_decay.T,
        prefix_key_rows,
        prefix_values,
        scratch=[
            pltpu.VMEM(prefix_x.shape, BF16),
            pltpu.VMEM(prefix_b.shape, BF16),
            pltpu.VMEM((heads, tokens), F32),
            pltpu.VMEM(prefix_key_rows.shape, BF16),
            pltpu.VMEM(prefix_values.shape, BF16),
            pltpu.SemaphoreType.DMA((5,)),
        ],
        raw=True,
        limit=60,
    )
    (cc,) = call(
        projections_kernel,
        "projections",
        [((tokens + 2 * steps, groups * state), BF16)],
        prefix_c,
        cand_c,
        other_c,
        after=(cum,),
    )
    group_of, first_of = groups_of(groups, counts)
    def intra(mark, cc):
        return call(
            functools.partial(intra_kernel, groups=groups),
            "intra",
            [((tokens, count * width), F32) for count in counts],
            prefix_x,
            b2,
            cc,
            cum,
            skip,
            after=(mark,),
            gate=(loads[1],),
        )

    def candidates(mark, *more):
        return call(
            cand_kernel,
            "candidates",
            [((tokens, count * width), F32) for count in counts if more] + [((steps, cand_wide), F32), ((steps, cand_wide), F32)],
            cand_x,
            cand_b,
            cand_c,
            cand_decay,
            skip,
            *more,
            after=(mark,),
        )

    def attend(mark, pieces, inner):
        (mine,) = call(
            functools.partial(collect_kernel, inner=inner),
            "collect",
            [((tokens * (size - 1), kv_shape[1]), BF16)],
            *pieces,
            after=(mark,),
        )
        theirs = to_core(mine)

        def finish(mark):
            return call(
                attend_kernel,
                "attend",
                [((8, 128), F32)],
                cand_length,
                cand_queries,
                cand_keys,
                cand_values,
                prefix_key_rows,
                prefix_values,
                mine,
                theirs,
                scalars=1,
                after=(mark,),
                into=((cand_queries.shape, BF16),),
                scratch=[pltpu.VMEM(cand_queries.shape, BF16), pltpu.SemaphoreType.DMA((1,))],
            )

        return mine, finish

    shared = dict(cols=cols, heads=heads, tokens=tokens)
    if size == 4:
        shared = dict(counts=counts, width=width, heads=heads, tokens=tokens)
        mark = cc
        middle, carried, cands, outer, outs, raws = {}, {}, {}, {}, [], []
        rows = {"cc": cc}
        below = (16, 2 * tokens // (counts[1] * width // kv_shape[1]), 0, 0)

        def inputs_of(q):
            p = first_of[group_of[q]]
            return got[q], got[p], loads[q], loads[p]

        def first(q, mark):
            extra = [((8, wide), F32), ((8, wide), F32), ((8, heads), F32)] if q == 0 else []
            results = call(
                functools.partial(first_kernel, q=q, groups=groups, state=state, **shared),
                "first",
                extra
                + [((state + (16 if q == 0 else 0), counts[q] * width), BF16)]
                + ([((2 * tokens, kv_shape[1]), BF16)] if q == 1 else []),
                *inputs_of(q),
                *([total] if q == 0 else [rows["own"], rows["near"]]),
                *([kv] if q == 1 else []),
                after=(mark,),
                cost=FIRST_COST if q == 1 else 0.0,
                gate=[(rows["cc"],), loads[2:], (), ()][q],
            )
            if q == 0:
                *results, rows["cc"] = results
                rows["near_cc"] = to_neighbour(rows["cc"])
            elif q == 1:
                *results, loads[2], loads[3] = results
                got.extend((to_neighbour(loads[2]), inward(loads[3])))
            if q == 0:
                rows["own"], rows["near"], rows["near_total"], *results = results
            middle[q] = between_inner(results[0])
            if q == 1:
                rows["kv"] = results[1]
            return results[0]

        def second(q, mark, make="all"):
            results = call(
                functools.partial(second_kernel, q=q, groups=groups, state=state, make=make, **shared),
                "second",
                ([((8, wide), F32)] if q == 0 else [])
                + [((tokens, counts[q] * width), F32), ((2 * steps, counts[q] * width), F32)] * (make != "send")
                + [((tokens + 2 * steps + below[q], counts[q] * width), BF16)] * (make != "keep"),
                middle[q],
                *inputs_of(q),
                rows["own"],
                rows["cc"],
                rows["near_cc"],
                *([far_kv] if q == 1 else []),
                *([total, rows["near_total"]] if q == 0 else [rows["later"]]),
                after=(mark,),
                cost=SECOND_COST,
            )
            if q == 0:
                rows["later"], *results = results
            if make != "keep":
                outer[q] = to_neighbour(results[-1])
            if make != "send":
                carried[q], cands[q] = results[:2]
            return results[0]

        def third(q, mark):
            final = q == CHUNKS - 1
            results = call(
                functools.partial(third_kernel, q=q, **shared),
                "third",
                [((steps, wide), F32), ((steps, wide), BF16)]
                if final
                else ([((8, wide), F32)] if q == 0 else []) + [((2 * steps, counts[q] * width), F32)],
                outer[q],
                cands[q],
                rows["own"],
                *([] if q == 0 else [rows["outer"]]),
                *(raws if final else []),
                after=(mark,),
                cost=THIRD_COST,
            )
            if q == 0:
                rows["outer"], *results = results
            if final:
                return results
            raws.append(results[0])
            return results[0]

        def prefix(start, count, mark, into):
            span = range(start, start + count)
            return call(
                functools.partial(prefix_kernel, first=sum(counts[:start]) * width, tokens=tokens),
                "prefix",
                [((8, 128), F32)] if start == 0 else [],
                *[each[q] for each in (outer, carried, base, fade) for q in span],
                after=(mark,),
                into=(into,),
                scratch=[
                    pltpu.VMEM((tokens, sum(counts[start : start + count]) * width), BF16),
                    pltpu.SemaphoreType.DMA((1,)),
                ],
            )

        *base, loads[1] = intra(cc, cc)
        got = [to_neighbour(a) for a in loads[:2]]
        mark = first(0, base[0])
        mark = first(1, mark)
        far_kv = between_inner(rows["kv"])
        mark = second(0, mark)
        mark = first(2, mark)
        mark = second(1, mark)
        mark = first(3, mark)
        *fade, cand_base, cand_fade = candidates(mark, cum)
        mark = third(0, cand_base)
        mark = second(2, mark)
        mark = third(1, mark)
        mark, finish_attend = attend(mark, [rows["kv"], far_kv, outer[1]], True)
        mark = second(3, mark, "send")
        mark = second(3, mark, "keep")
        mark, cand_attn = finish_attend(mark)
        mark = third(2, mark)
        mark, prefix_out = prefix(0, CHUNKS - 1, mark, (prefix_x.shape, BF16))
        keep, give = third(3, mark)
        (prefix_out,) = prefix(CHUNKS - 1, 1, keep, prefix_out)
    else:
        got = [to_neighbour(a) for a in loads]
        halves = [kv, got[1][:, -kv_shape[1] :]]
        for level in range(1, levels):
            mirrored = to_mirror(halves[0], level)
            halves = [halves[0], halves[1], mirrored, to_neighbour(mirrored)]
            if level < levels - 1:
                halves = [jnp.concatenate([halves[0], halves[2]]), jnp.concatenate([halves[1], halves[3]])]
        *base, loads[1] = intra(cc, cc)
        mark = base[0]
        own = call(
            functools.partial(own_kernel, cols=cols, groups=groups, state=state, counts=counts),
            "own",
            [((state, cols), F32)] * CHUNKS,
            *loads,
        )
        own, start = dict(enumerate(own)), {}
        before = None
        near, far = {}, {}
        outs, raws = [], []
        for level in range(levels):
            last = level == levels - 1
            rows = None
            for q in range(CHUNKS):
                final = last and q == CHUNKS - 1
                if level == 0:
                    args, lines = [got[q], got[first_of[group_of[q]]]], got[0]
                else:
                    args, lines = [near[q], far[q]], near[0]
                shapes = []
                if q == 0:
                    args += [total, lines] + ([] if level == 0 else [before])
                    shapes += [((8, wide), F32)] * 2 + [((8, heads), F32)] * 2
                else:
                    args += rows
                args += [own[q]] + ([] if level == 0 else [start[q]])
                if final:
                    args += [cc, base[q], cum] + outs + raws
                    shapes = [((tokens, wide), BF16), ((steps, wide), F32), ((steps, wide), BF16)]
                elif last:
                    args += [cc, base[q], cum]
                    shapes += [((tokens, cols), BF16), ((2 * steps, cols), F32)]
                else:
                    shapes += [((state, cols), F32)] * 2 + [((state + (16 if q == 0 else 0), cols // 2), BF16)]
                results = call(
                    functools.partial(
                        merge_kernel, level=level, last=last, chunks=[q], groups=groups, state=state, **shared
                    ),
                    "merge",
                    shapes,
                    *args,
                    after=(mark,),
                )
                mark = results[0]
                if final:
                    prefix_out, keep, give = results
                    continue
                if q == 0:
                    rows, (total, before) = list(results[:2]), results[2:4]
                if last:
                    outs.append(results[-2])
                    raws.append(results[-1])
                else:
                    own[q], start[q] = results[-3], results[-2]
                    near[q] = to_mirror(results[-1], level + 1)
                    far[q] = to_neighbour(near[q])
            if level == 0:
                cand_base, cand_fade = candidates(mark)
                pieces = ([halves[0][tokens:]] if levels > 2 else []) + halves[1:]
                mark, finish_attend = attend(cand_base, pieces, False)
                mark, cand_attn = finish_attend(mark)
    (cand_ssm,) = call(
        close_kernel,
        "close",
        [((1, steps, cand_wide), BF16)],
        cand_length,
        cand_base,
        cand_fade,
        keep,
        to_core(give),
        scalars=1,
    )
    return (prefix_out, cand_ssm, cand_attn)


def solution(mesh):
    placed = (
        P(("groups", "seq"), ("head", "rep")),
        P(("groups", "seq"), ("head", "rep"), None),
        P(("groups", "seq"), ("head", "rep"), None),
        P(("groups", "seq"), ("head", "rep")),
        P(),
        P(("groups", "seq"), "head", None),
        P(("groups", "seq"), "head", None),
        P(("groups", "seq", "rep"), None, "head"),
        P(("groups", "seq", "rep"), None, "head", None),
        P(("groups", "seq", "rep"), None, "head", None),
        P(("groups", "seq", "rep"), None, "head"),
        P(("groups", "seq", "rep"), None, "head", None),
        P(("groups", "seq", "rep"), None, "head", None),
        P(("groups", "seq", "rep"), None, "head", None),
        P(("groups", "seq", "rep")),
    )
    return jax.shard_map(
        on_device,
        mesh=mesh,
        in_specs=placed,
        out_specs=(
            P(("groups", "seq"), ("head", "rep")),
            P(("groups", "seq", "rep"), None, "head"),
            P(("groups", "seq", "rep"), None, "head", None),
        ),
        check_vma=False,
    )
```

```python
import functools

import jax
import jax.numpy as jnp
from jax import lax
from jax.experimental import pallas as pl
from jax.experimental.pallas import tpu as pltpu
from jax.sharding import PartitionSpec as P

EPSILON = 1e-06
NEG = -1e30
LARGEST = 3.38e38
CHUNKS = 4
PARTS = (8, 8, 8, 8)
SECOND_COST = 1.0
FIRST_COST = 1.0
THIRD_COST = 0.3
F32 = jnp.float32
BF16 = jnp.bfloat16


def mm(a, b):
    return lax.dot_general(a, b, (((1,), (0,)), ((), ())), preferred_element_type=F32)


def mm_nt(a, b):
    return lax.dot_general(a, b, (((1,), (1,)), ((), ())), preferred_element_type=F32)


def mm_tn(a, b):
    return lax.dot_general(a, b, (((0,), (0,)), ((), ())), preferred_element_type=F32)


def exact_nt(a, b):
    return lax.dot_general(
        a, b, (((1,), (1,)), ((), ())), preferred_element_type=F32, precision=lax.Precision.HIGHEST
    )


def exact(a, b):
    return lax.dot_general(
        a, b, (((1,), (0,)), ((), ())), preferred_element_type=F32, precision=lax.Precision.HIGHEST
    )


def iota(shape, dim):
    return lax.broadcasted_iota(jnp.int32, shape, dim)


def split3(a):
    hi = jnp.clip(a, -LARGEST, LARGEST).astype(BF16)
    rest = a - hi.astype(F32)
    mid = rest.astype(BF16)
    return hi, mid, (rest - mid.astype(F32)).astype(BF16)


def spread(a, width, first=0, count=None):
    rows, cols = a.shape
    count = cols if count is None else count
    parts = jnp.concatenate(split3(a), axis=1)
    shape = (3 * cols, count * width)
    source = iota(shape, 0)
    source = jnp.where(source >= 2 * cols, source - 2 * cols, jnp.where(source >= cols, source - cols, source))
    unit = (source == first + iota(shape, 1) // width).astype(F32).astype(BF16)
    return mm(parts, unit)


def group_of(array, g):
    return array.astype(F32)[:, g, :].astype(BF16)


def cut(heads, size):
    if size == 4 and heads % sum(PARTS) == 0:
        return tuple(heads // sum(PARTS) * part for part in PARTS)
    return (heads // CHUNKS,) * CHUNKS


def groups_of(groups, counts):
    of = [sum(counts[:q]) * groups // sum(counts) for q in range(CHUNKS)]
    return of, {g: of.index(g) for g in of}


def columns(q, counts, width):
    return slice(sum(counts[:q]) * width, sum(counts[: q + 1]) * width)


def payload_plan(groups, counts):
    of, first_of = groups_of(groups, counts)
    return [[g] if first_of[g] == q else [] for q, g in enumerate(of)]


def totals_to_lines(total):
    hi, mid, lo = [a.astype(F32) for a in split3(jnp.broadcast_to(total, (16, total.shape[1])))]
    line = iota(hi.shape, 0)
    return jnp.where(line == 0, hi, jnp.where(line == 1, mid, jnp.where(line == 2, lo, 0.0))).astype(BF16)


def lines_to_totals(lines):
    lines = lines.astype(F32)
    return lines[0:1] + lines[1:2] + lines[2:3]


def as_row(total, width):
    return spread(jnp.broadcast_to(total, (8, total.shape[1])), width)


def pack(k_ref, v_ref):
    rep = lax.axis_index("rep")
    kv = jnp.where(rep == 0, k_ref[...].astype(F32), v_ref[...].astype(F32))
    return jnp.concatenate([kv[:, j, :] for j in range(kv.shape[1])], axis=1).astype(BF16)


def inputs_kernel(x_any, b_any, decay_t_any, k_any, v_any, cum_ref, total_ref, b2_ref, kv_ref, *refs, counts):
    load_refs, (x_ref, b_ref, decay_t_ref, k_ref, v_ref, sems) = refs[:-6], refs[-6:]
    pairs = ((decay_t_any, decay_t_ref), (b_any, b_ref), (x_any, x_ref), (k_any, k_ref), (v_any, v_ref))
    copies = [pltpu.make_async_copy(source, target, sems.at[i]) for i, (source, target) in enumerate(pairs)]
    for copy in copies:
        copy.start()
    tokens, groups, state = b_ref.shape
    heads = decay_t_ref.shape[0]
    width = x_ref.shape[1] // heads
    copies[0].wait()
    lower = (iota((tokens, tokens), 0) >= iota((tokens, tokens), 1)).astype(F32)
    cum = exact_nt(lower, decay_t_ref[...])
    cum_ref[...] = cum
    last = cum[tokens - 1 : tokens, :]
    total = jnp.exp(-last)
    total_ref[...] = jnp.broadcast_to(total, (8, heads))
    load_refs[0][tokens:, :] = jnp.zeros((16, load_refs[0].shape[1]), BF16)
    load_refs[0][tokens:, :heads] = totals_to_lines(total)
    weights = spread(jnp.exp(last - cum), width)
    for copy in copies[1:]:
        copy.wait()
    b = b_ref[...].astype(F32)
    for g in range(groups):
        b2_ref[:, g * state : (g + 1) * state] = b[:, g, :].astype(BF16)
    kv = pack(k_ref, v_ref)
    kv_ref[...] = kv
    for q, (fresh, load) in enumerate(zip(payload_plan(groups, counts), load_refs)):
        at = columns(q, counts, width)
        cols = counts[q] * width
        load[:tokens, :cols] = (x_ref[:, at].astype(F32) * weights[:, at]).astype(BF16)
        if fresh:
            load[:tokens, cols : cols + state] = b2_ref[:, fresh[0] * state : (fresh[0] + 1) * state]
        if q == 1:
            load[:, load.shape[1] - kv.shape[1] :] = kv


def own_kernel(*refs, cols, groups, state, counts):
    load_refs, out_refs = refs[:CHUNKS], refs[CHUNKS:]
    tokens = load_refs[1].shape[0]
    of, first_of = groups_of(groups, counts)
    for q in range(CHUNKS):
        b_ref = load_refs[first_of[of[q]]]
        out_refs[q][...] = mm_tn(b_ref[:tokens, cols : cols + state], load_refs[q][:tokens, :cols])


def collect_kernel(*refs, inner):
    refs, out_ref = list(refs[:-1]), refs[-1]
    place = lax.axis_index("seq")
    pieces = [ref[...] for ref in refs]
    if inner:
        pair, far, outer = pieces
        rows, wide = far.shape
        count = outer.shape[1] // wide
        first = outer.shape[0] - rows // count
        outer = jnp.concatenate([outer[first:, i * wide : (i + 1) * wide] for i in range(count)], axis=0)
        pieces = [pair[pair.shape[0] // 2 :], jnp.where((place == 1) | (place == 2), far, outer)]
    at = 0
    for piece in pieces:
        out_ref[at : at + piece.shape[0], :] = piece
        at += piece.shape[0]


def half_of(place, level):
    odd = lax.rem(place, 2)
    return jnp.where(lax.rem(lax.div(place, 2**level), 2) == 0, 1 - odd, odd)


def merge_kernel(*refs, level, last, chunks, cols, groups, heads, tokens, state):
    refs = list(refs)

    def take(count):
        taken = refs[:count]
        del refs[:count]
        return taken

    place = lax.axis_index("seq")
    right = lax.rem(lax.div(place, 2**level), 2) == 1
    width = cols * CHUNKS // heads
    first = 0 in chunks
    outs = []
    others = []
    if level == 0:
        for q in chunks:
            w_ref, b_ref = take(2)
            others.append(mm_tn(b_ref[:tokens, cols : cols + state], w_ref[:tokens, :cols]))
    else:
        half = half_of(place, level)
        for q in chunks:
            near_ref, far_ref = take(2)
            rows = near_ref.shape[0] - 16 if q == 0 else near_ref.shape[0]
            near, far = near_ref[:rows, :], far_ref[:rows, :]
            pieces = [jnp.where(half == 0, near, far), jnp.where(half == 0, far, near)]
            others.append(jnp.concatenate(pieces, axis=1).astype(F32))
    if first:
        mine_ref, lines_ref = take(2)
        mine = mine_ref[:1, :]
        theirs = lines_to_totals(lines_ref[lines_ref.shape[0] - 16 :, :heads])
        later = as_row(jnp.where(right, mine, theirs), width)
        pair = mine * theirs
        if level == 0:
            before = jnp.ones_like(mine)
        else:
            before = take(1)[0][:1, :]
        before_row = as_row(before, width)
        before = jnp.where(right, before * theirs, before)
        outs += [later, before_row, jnp.broadcast_to(pair, (8, heads)), jnp.broadcast_to(before, (8, heads))]
    else:
        later_ref, before_ref = take(2)
        later, before_row = later_ref[...], before_ref[...]
    for q, other in zip(chunks, others, strict=True):
        at = slice(q * cols, (q + 1) * cols)
        own = take(1)[0][...]
        earlier, following = jnp.where(right, other, own), jnp.where(right, own, other)
        joined = later[:1, at] * earlier + following
        if level == 0:
            start = jnp.where(right, other, 0.0)
        else:
            start = take(1)[0][...]
            start = jnp.where(right, before_row[:1, at] * other + start, start)
        if not last:
            send = jnp.where(half_of(place, level + 1) == 0, joined[:, : cols // 2], joined[:, cols // 2 :]).astype(BF16)
            if q == 0:
                tail = jnp.zeros((16, cols // 2 - heads), BF16)
                lines = jnp.concatenate([totals_to_lines(pair), tail], axis=1)
                send = jnp.concatenate([send, lines], axis=0)
            outs += [joined, start, send]
        else:
            cc_ref, base_ref, cum_ref = take(3)
            g = q * groups // CHUNKS
            here = slice(g * state, (g + 1) * state)
            fade = spread(jnp.exp(-cum_ref[...]), width, q * heads // CHUNKS, heads // CHUNKS)
            carried = mm(cc_ref[:tokens, here], start.astype(BF16))
            outs.append((base_ref[...] + fade * carried).astype(BF16))
            outs.append(mm(cc_ref[tokens:, here], joined.astype(BF16)))
    if last and CHUNKS - 1 in chunks:
        parts = take(2 * (CHUNKS - 1))
        out_parts = [ref[...] for ref in parts[: CHUNKS - 1]] + [outs[-2]]
        raws = [ref[...] for ref in parts[CHUNKS - 1 :]] + [outs[-1]]
        rep = lax.axis_index("rep")
        out_ref, keep_ref, give_ref = refs
        rows = keep_ref.shape[0]
        for q in range(CHUNKS):
            at = slice(q * cols, (q + 1) * cols)
            out_ref[:, at] = out_parts[q]
            keep_ref[:, at] = jnp.where(rep == 0, raws[q][:rows], raws[q][rows:])
            give_ref[:, at] = jnp.where(rep == 0, raws[q][rows:], raws[q][:rows]).astype(BF16)
    else:
        for ref, value in zip(refs, outs, strict=True):
            ref[...] = value


def projections_kernel(c_ref, mine_ref, other_ref, out_ref):
    rep = lax.axis_index("rep")
    tokens, groups, state = c_ref.shape
    steps = mine_ref.shape[1]
    mine, other = mine_ref[0].astype(F32), other_ref[0].astype(F32)
    zero, one = jnp.where(rep == 0, mine, other), jnp.where(rep == 0, other, mine)
    prefix = c_ref[...].astype(F32)
    for g in range(groups):
        at = slice(g * state, (g + 1) * state)
        out_ref[:tokens, at] = prefix[:, g, :].astype(BF16)
        for i, c in enumerate((zero, one)):
            part = jnp.where(rep == 0, c[:, g, :], c[:, groups + g, :])
            out_ref[tokens + i * steps : tokens + (i + 1) * steps, at] = part.astype(BF16)


def first_kernel(*refs, q, counts, width, groups, heads, tokens, state):
    refs = list(refs)
    w_ref, b_ref, own_w_ref, own_b_ref = refs[:4]
    refs = refs[4:]
    left = lax.axis_index("seq") < 2
    cols = counts[q] * width
    of, first_of = groups_of(groups, counts)
    at_b = slice(counts[first_of[of[q]]] * width, counts[first_of[of[q]]] * width + state)
    other = mm_tn(b_ref[:tokens, at_b], w_ref[:tokens, :cols])
    if q == 0:
        mine_ref, own_row_ref, near_row_ref, near_ref, send_ref = refs
        mine = mine_ref[:1, :]
        near = lines_to_totals(w_ref[tokens:, :heads])
        own_row, near_row = as_row(mine, width), as_row(near, width)
        own_row_ref[...] = own_row
        near_row_ref[...] = near_row
        near_ref[...] = jnp.broadcast_to(near, (8, heads))
        send_ref[state:, :] = jnp.zeros((16, cols), BF16)
        send_ref[state:, :heads] = totals_to_lines(mine * near)
    else:
        own_row_ref, near_row_ref = refs[:2]
        refs = refs[2:]
        if q == 1:
            kv_ref, pair_ref = refs[0], refs.pop()
            refs = refs[1:]
            pair_ref[:tokens, :] = kv_ref[...]
            pair_ref[tokens:, :] = w_ref[:, w_ref.shape[1] - kv_ref.shape[1] :]
        (send_ref,) = refs
        own_row, near_row = own_row_ref[...], near_row_ref[...]
    at = columns(q, counts, width)
    local = mm_tn(own_b_ref[:tokens, at_b], own_w_ref[:tokens, :cols])
    after = own_row[:1, at] * other + local
    beyond = other + near_row[:1, at] * local
    send_ref[:state, :] = jnp.where(left, after, beyond).astype(BF16)


def second_kernel(*refs, q, counts, width, groups, heads, tokens, state, make):
    refs = list(refs)
    got_ref, w_ref, b_ref, own_w_ref, own_b_ref, own_row_ref, cc_ref, near_cc_ref = refs[:8]
    refs = refs[8:]
    if make == "send":
        refs[-1:] = [None, None, refs[-1]]
    elif make == "keep":
        refs.append(None)
    place = lax.axis_index("seq")
    left, inner = place < 2, (place == 1) | (place == 2)
    cols = counts[q] * width
    at = columns(q, counts, width)
    of, first_of = groups_of(groups, counts)
    at_b = slice(counts[first_of[of[q]]] * width, counts[first_of[of[q]]] * width + state)
    here = slice(of[q] * state, (of[q] + 1) * state)
    rows = cc_ref.shape[0]
    if q == 0:
        mine_ref, near_ref, later_row_ref, carried_ref, cand_ref, send_ref = refs
        later = jnp.where(left, lines_to_totals(got_ref[state:, :heads]), near_ref[:1, :])
        later_row = as_row(later, width)
        later_row_ref[...] = later_row
        send_ref[rows:, :] = jnp.zeros((16, cols), BF16)
        send_ref[rows:, :heads] = totals_to_lines(later * mine_ref[:1, :])
    else:
        if q == 1:
            kv_ref = refs.pop(0)
            held = kv_ref.shape[0] // (cols // kv_ref.shape[1])
            for i in range(cols // kv_ref.shape[1]):
                part = slice(i * kv_ref.shape[1], (i + 1) * kv_ref.shape[1])
                refs[-1][rows:, part] = kv_ref[i * held : (i + 1) * held, :]
        later_row_ref, carried_ref, cand_ref, send_ref = refs
        later_row = later_row_ref[...]
    got = got_ref[:state, :].astype(F32)
    other = mm_tn(b_ref[:tokens, at_b], w_ref[:tokens, :cols])
    local = mm_tn(own_b_ref[:tokens, at_b], own_w_ref[:tokens, :cols])
    start, beyond = jnp.where(left, other, got), jnp.where(left, got, other)
    start = jnp.where(inner, start, 0.0)
    after = own_row_ref[:1, at] * start + local
    lasting = later_row[:1, at]
    if make != "keep":
        state_out = jnp.where(left, beyond + lasting * local, after)
        send_ref[:rows, :] = mm(near_cc_ref[:, here], state_out.astype(BF16)).astype(BF16)
    if make == "send":
        return
    final = jnp.where(inner, lasting * after + beyond, local)
    carried_ref[...] = mm(cc_ref[:tokens, here], start.astype(BF16))
    cand_ref[...] = mm(cc_ref[tokens:, here], final.astype(BF16))


def third_kernel(*refs, q, counts, width, heads, tokens):
    refs = list(refs)
    got_ref, cand_ref, own_row_ref = refs[:3]
    place = lax.axis_index("seq")
    at = columns(q, counts, width)
    rows = cand_ref.shape[0]
    refs = refs[3:]
    if q == 0:
        later_row_ref = refs[0]
        later_row = as_row(lines_to_totals(got_ref[tokens + rows :, :heads]), width)
        later_row_ref[...] = later_row
    else:
        later_row = refs[0][...]
    refs = refs[1:]
    cand = cand_ref[...]
    got = got_ref[tokens : tokens + rows, :].astype(F32)
    cand = jnp.where(
        place == 3,
        own_row_ref[:1, at] * got + cand,
        jnp.where(place == 0, later_row[:1, at] * cand + got, cand),
    )
    if q < CHUNKS - 1:
        (raw_ref,) = refs
        raw_ref[...] = cand
        return
    raws, (keep_ref, give_ref) = refs[:-2], refs[-2:]
    rep = lax.axis_index("rep")
    half = rows // 2
    for i in range(CHUNKS):
        at = columns(i, counts, width)
        raw = cand if i == q else raws[i][...]
        keep_ref[:, at] = jnp.where(rep == 0, raw[:half], raw[half:])
        give_ref[:, at] = jnp.where(rep == 0, raw[half:], raw[:half]).astype(BF16)


def prefix_kernel(*refs, first, tokens):
    refs, (out_any, buffer, sem) = refs[:-3], refs[-3:]
    last = lax.axis_index("seq") == 3
    count = len(refs) // 4
    if len(refs) % 4:
        refs[-1][...] = jnp.zeros(refs[-1].shape, F32)
        refs = refs[:-1]
    at = 0
    for i in range(count):
        got_ref, carried_ref, base_ref, fade_ref = refs[i::count]
        carried = jnp.where(last, got_ref[:tokens, :].astype(F32), carried_ref[...])
        buffer[:, at : at + base_ref.shape[1]] = (base_ref[...] + fade_ref[...] * carried).astype(BF16)
        at += base_ref.shape[1]
    copy = pltpu.make_async_copy(buffer, out_any.at[:, pl.ds(first, at)], sem.at[0])
    copy.start()
    copy.wait()


def intra_kernel(x_ref, b2_ref, c2_ref, cum_ref, skip_ref, *base_refs, groups):
    tokens, heads = cum_ref.shape
    width = x_ref.shape[1] // heads
    state = c2_ref.shape[1] // groups
    per_group = heads // groups
    first = (lax.axis_index("head") * lax.axis_size("rep") + lax.axis_index("rep")) * heads
    skip = spread(jnp.broadcast_to(skip_ref[...], (8, skip_ref.shape[1])), width, first, heads)[:1]
    cum = cum_ref[...]
    cum_t = cum.T
    shape = (tokens, tokens)
    hidden = jnp.where(iota(shape, 0) >= iota(shape, 1), 0.0, NEG)
    pair = 2 * width
    lane = iota((tokens, pair), 1)
    for g in range(groups):
        here = slice(g * state, (g + 1) * state)
        gram = mm_nt(c2_ref[:tokens, here], b2_ref[:, here])
        for h in range(g * per_group, (g + 1) * per_group, 2):
            mixing = []
            for i in (h, h + 1):
                gap = cum_t[i : i + 1, :] - jnp.broadcast_to(cum[:, i : i + 1], shape)
                mixing.append((jnp.exp(gap + hidden) * gram).astype(BF16))
            at = slice(h * width, (h + 2) * width)
            x = x_ref[:, at]
            zero = jnp.zeros_like(x)
            inputs = jnp.concatenate(
                [jnp.where(lane < width, x, zero), jnp.where(lane < width, zero, x)], axis=0
            )
            q, start = 0, h * width
            while start >= base_refs[q].shape[1]:
                start -= base_refs[q].shape[1]
                q += 1
            base_refs[q][:, start : start + pair] = (
                mm(jnp.concatenate(mixing, axis=1), inputs) + skip[:, at] * x.astype(F32)
            )


def cand_kernel(x_ref, b_ref, c_ref, decay_ref, skip_ref, *refs):
    if len(refs) > 2:
        cum_ref, *fall_refs = refs[:-2]
        fall = spread(jnp.exp(-cum_ref[...]), sum(ref.shape[1] for ref in fall_refs) // cum_ref.shape[1])
        at = 0
        for ref in fall_refs:
            ref[...] = fall[:, at : at + ref.shape[1]]
            at += ref.shape[1]
    base_ref, fade_ref = refs[-2:]
    steps, groups, state = b_ref.shape[1:]
    heads = decay_ref.shape[2]
    width = x_ref.shape[2] // heads
    per_group = heads // groups
    first = lax.axis_index("head") * heads
    skip = spread(jnp.broadcast_to(skip_ref[...], (8, skip_ref.shape[1])), width, first, heads)[:1]
    lower = (iota((steps, steps), 0) >= iota((steps, steps), 1)).astype(F32)
    cum = exact(lower, decay_ref[0])
    fade_ref[...] = spread(jnp.exp(-cum), width)
    wide = (steps, heads * steps)
    cum_t = spread(cum, steps)
    place = iota(wide, 1) % steps
    row = iota(wide, 0)
    cum_s = jnp.sum(jnp.where(row == place, cum_t, 0.0), axis=0, keepdims=True)
    fall = jnp.exp(jnp.where(row >= place, cum_s - cum_t, NEG))
    b = b_ref[0].astype(F32)
    c = c_ref[0].astype(F32)
    quad = 128 // steps
    shape = (quad * steps, quad * width)
    mine = iota(shape, 0) // steps == iota(shape, 1) // width
    for g in range(groups):
        b_g = b[:, g, :].astype(BF16)
        gram = mm_nt(c[:, g, :].astype(BF16), jnp.concatenate([b_g] * quad, axis=0))
        for h in range(g * per_group, (g + 1) * per_group, quad):
            mixing = (fall[:, h * steps : (h + quad) * steps] * gram).astype(BF16)
            at = slice(h * width, (h + quad) * width)
            x = x_ref[0, :, at]
            tall = jnp.concatenate([x] * quad, axis=0)
            inputs = jnp.where(mine, tall, jnp.zeros_like(tall))
            base_ref[:, at] = mm(mixing, inputs) + skip[:, at] * x.astype(F32)


def attend_kernel(length_ref, q_ref, own_k_ref, own_v_ref, k_ref, v_ref, mine_ref, other_ref, mark_ref, out_any, out_ref, sem):
    mark_ref[...] = jnp.zeros(mark_ref.shape, F32)
    rep = lax.axis_index("rep")
    steps, heads, dim = q_ref.shape[1:]
    kv_heads = own_k_ref.shape[2]
    per_kv = heads // kv_heads
    rows = steps * per_kv
    mine, other = mine_ref[...], other_ref[...]
    keys, values = jnp.where(rep == 0, mine, other), jnp.where(rep == 0, other, mine)
    q = q_ref[0].astype(F32)
    own_k = own_k_ref[0].astype(F32)
    own_v = own_v_ref[0].astype(F32)
    block_k = k_ref[...].astype(F32)
    block_v = v_ref[...].astype(F32)
    scale = dim ** (-0.5)
    step_of = iota((rows, steps), 0) // per_kv
    visible = step_of >= iota((rows, steps), 1)
    live = iota((rows, dim), 0) // per_kv < length_ref[0]
    mixed_of = []
    for j in range(kv_heads):
        query = q[:, j * per_kv : (j + 1) * per_kv, :].reshape(rows, dim).astype(BF16)

        def gather(far, block):
            return jnp.concatenate([far[:, j * dim : (j + 1) * dim], block[:, j, :].astype(BF16)], axis=0)

        far = mm_nt(query, gather(keys, block_k)) * scale
        near = jnp.where(visible, mm_nt(query, own_k[:, j, :].astype(BF16)) * scale, NEG)
        top = jnp.maximum(jnp.max(far, axis=1, keepdims=True), jnp.max(near, axis=1, keepdims=True))
        far = jnp.exp(far - top)
        near = jnp.exp(near - top)
        mass = jnp.sum(far, axis=1, keepdims=True) + jnp.sum(near, axis=1, keepdims=True)
        mixed = mm(far.astype(BF16), gather(values, block_v)) + mm(near.astype(BF16), own_v[:, j, :].astype(BF16))
        mixed = mixed / mass
        mixed = mixed * lax.rsqrt(jnp.mean(mixed * mixed, axis=1, keepdims=True) + EPSILON)
        mixed = jnp.where(live, mixed, 0.0)
        mixed_of.append(mixed.reshape(steps, per_kv, dim))
    out_ref[0] = (jnp.concatenate(mixed_of, axis=1) if kv_heads > 1 else mixed_of[0]).astype(BF16)
    copy = pltpu.make_async_copy(out_ref, out_any, sem.at[0])
    copy.start()
    copy.wait()


def close_kernel(length_ref, base_ref, fade_ref, keep_ref, got_ref, out_ref):
    rep = lax.axis_index("rep")
    keep, got = keep_ref[...], got_ref[...].astype(F32)
    cols = keep.shape[1]
    live = iota(keep.shape, 0) < length_ref[0]
    for i in range(2):
        at = slice(i * cols, (i + 1) * cols)
        carried = jnp.where(rep == i, keep, got)
        result = base_ref[:, at] + fade_ref[:, at] * carried
        out_ref[0, :, at] = jnp.where(live, result, 0.0).astype(BF16)


def call(kernel, name, outs, *args, scalars=0, after=(), cost=0.0, scratch=(), limit=32, gate=(), into=(), raw=False):
    shapes = [jax.ShapeDtypeStruct(shape, dtype) for shape, dtype in outs]
    vmem = pl.BlockSpec(memory_space=pltpu.VMEM)
    smem = pl.BlockSpec(memory_space=pltpu.SMEM)
    anywhere = pl.BlockSpec(memory_space=pl.ANY)
    given = [a for a in into if hasattr(a, "dtype")]
    passed = [*gate, *given]
    count = len(args)
    rest = count + len(after) + len(passed)
    through = rest + len(shapes)
    shapes += [jax.ShapeDtypeStruct(a.shape, a.dtype) for a in gate]
    shapes += [jax.ShapeDtypeStruct(a.shape, a.dtype) if hasattr(a, "dtype") else jax.ShapeDtypeStruct(*a) for a in into]
    aliases = {count + len(after) + i: len(outs) + i for i in range(len(passed))}

    def body(*refs):
        kernel(*refs[:count], *refs[rest:through], *refs[through + len(gate) :])

    return pl.pallas_call(
        body,
        out_shape=shapes,
        in_specs=[smem] * scalars
        + [anywhere if raw else vmem] * (count - scalars)
        + [anywhere] * (len(after) + len(passed)),
        out_specs=[vmem] * len(outs) + [anywhere] * (len(gate) + len(into)),
        input_output_aliases=aliases,
        scratch_shapes=list(scratch),
        compiler_params=pltpu.CompilerParams(vmem_limit_bytes=limit * 2**20),
        cost_estimate=pl.CostEstimate(flops=int(cost * 10**9), bytes_accessed=0, transcendentals=0),
        name=name,
    )(*args, *after, *passed)


def on_device(
    prefix_x,
    prefix_b,
    prefix_c,
    prefix_decay,
    bypass_weight,
    prefix_key_rows,
    prefix_values,
    cand_x,
    cand_b,
    cand_c,
    cand_decay,
    cand_queries,
    cand_keys,
    cand_values,
    cand_length,
):
    size = lax.axis_size("seq")
    levels = size.bit_length() - 1
    assert size == 2**levels and lax.axis_size("rep") == 2
    tokens, groups, state = prefix_b.shape
    heads = prefix_decay.shape[1]
    wide = prefix_x.shape[1]
    steps = cand_x.shape[1]
    cand_wide = cand_x.shape[2]
    cols = wide // CHUNKS
    skip = bypass_weight.reshape(1, -1)
    counts = cut(heads, size)
    width = wide // heads
    plan = payload_plan(groups, counts)

    def to_core(array):
        return lax.ppermute(array, "rep", [(0, 1), (1, 0)])

    def to_neighbour(array):
        return lax.ppermute(array, "seq", [(i, i ^ 1) for i in range(size)])

    def to_mirror(array, level):
        return lax.ppermute(array, "seq", [(i, i ^ (2 ** (level + 1) - 1)) for i in range(size)])

    def between_inner(array):
        far = {1: 2, 2: 1}
        pairs = [(2 * i + r, 2 * far[i] + r if i in far else 2 * i + 1 - r) for i in range(size) for r in range(2)]
        return lax.ppermute(array, ("seq", "rep"), pairs)

    def inward(array):
        return lax.ppermute(array, "seq", [(0, 1), (3, 2)])

    other_c = to_core(cand_c)
    kv_shape = (tokens, prefix_key_rows.shape[1] * prefix_key_rows.shape[2])
    cum, total, b2, kv, *loads = call(
        functools.partial(inputs_kernel, counts=counts),
        "inputs",
        [((tokens, heads), F32), ((8, heads), F32), ((tokens, groups * state), BF16), (kv_shape, BF16)]
        + [
            (
                (
                    tokens + (16 if q == 0 else 0),
                    counts[q] * width + len(fresh) * state + (kv_shape[1] if q == 1 else 0),
                ),
                BF16,
            )
            for q, fresh in enumerate(plan)
        ],
        prefix_x,
        prefix_b,
        prefix_decay.T,
        prefix_key_rows,
        prefix_values,
        scratch=[
            pltpu.VMEM(prefix_x.shape, BF16),
            pltpu.VMEM(prefix_b.shape, BF16),
            pltpu.VMEM((heads, tokens), F32),
            pltpu.VMEM(prefix_key_rows.shape, BF16),
            pltpu.VMEM(prefix_values.shape, BF16),
            pltpu.SemaphoreType.DMA((5,)),
        ],
        raw=True,
        limit=60,
    )
    (cc,) = call(
        projections_kernel,
        "projections",
        [((tokens + 2 * steps, groups * state), BF16)],
        prefix_c,
        cand_c,
        other_c,
        after=(cum,),
    )
    group_of, first_of = groups_of(groups, counts)
    def intra(mark, cc):
        return call(
            functools.partial(intra_kernel, groups=groups),
            "intra",
            [((tokens, count * width), F32) for count in counts],
            prefix_x,
            b2,
            cc,
            cum,
            skip,
            after=(mark,),
            gate=(loads[1],),
        )

    def candidates(mark, *more):
        return call(
            cand_kernel,
            "candidates",
            [((tokens, count * width), F32) for count in counts if more] + [((steps, cand_wide), F32), ((steps, cand_wide), F32)],
            cand_x,
            cand_b,
            cand_c,
            cand_decay,
            skip,
            *more,
            after=(mark,),
        )

    def attend(mark, pieces, inner):
        (mine,) = call(
            functools.partial(collect_kernel, inner=inner),
            "collect",
            [((tokens * (size - 1), kv_shape[1]), BF16)],
            *pieces,
            after=(mark,),
        )
        theirs = to_core(mine)

        def finish(mark):
            return call(
                attend_kernel,
                "attend",
                [((8, 128), F32)],
                cand_length,
                cand_queries,
                cand_keys,
                cand_values,
                prefix_key_rows,
                prefix_values,
                mine,
                theirs,
                scalars=1,
                after=(mark,),
                into=((cand_queries.shape, BF16),),
                scratch=[pltpu.VMEM(cand_queries.shape, BF16), pltpu.SemaphoreType.DMA((1,))],
            )

        return mine, finish

    shared = dict(cols=cols, heads=heads, tokens=tokens)
    if size == 4:
        shared = dict(counts=counts, width=width, heads=heads, tokens=tokens)
        mark = cc
        middle, carried, cands, outer, outs, raws = {}, {}, {}, {}, [], []
        rows = {"cc": cc}
        below = (16, 2 * tokens // (counts[1] * width // kv_shape[1]), 0, 0)

        def inputs_of(q):
            p = first_of[group_of[q]]
            return got[q], got[p], loads[q], loads[p]

        def first(q, mark):
            extra = [((8, wide), F32), ((8, wide), F32), ((8, heads), F32)] if q == 0 else []
            results = call(
                functools.partial(first_kernel, q=q, groups=groups, state=state, **shared),
                "first",
                extra
                + [((state + (16 if q == 0 else 0), counts[q] * width), BF16)]
                + ([((2 * tokens, kv_shape[1]), BF16)] if q == 1 else []),
                *inputs_of(q),
                *([total] if q == 0 else [rows["own"], rows["near"]]),
                *([kv] if q == 1 else []),
                after=(mark,),
                cost=FIRST_COST if q == 1 else 0.0,
                gate=[(rows["cc"],), loads[2:], (), ()][q],
            )
            if q == 0:
                *results, rows["cc"] = results
                rows["near_cc"] = to_neighbour(rows["cc"])
            elif q == 1:
                *results, loads[2], loads[3] = results
                got.extend((to_neighbour(loads[2]), inward(loads[3])))
            if q == 0:
                rows["own"], rows["near"], rows["near_total"], *results = results
            middle[q] = between_inner(results[0])
            if q == 1:
                rows["kv"] = results[1]
            return results[0]

        def second(q, mark, make="all"):
            results = call(
                functools.partial(second_kernel, q=q, groups=groups, state=state, make=make, **shared),
                "second",
                ([((8, wide), F32)] if q == 0 else [])
                + [((tokens, counts[q] * width), F32), ((2 * steps, counts[q] * width), F32)] * (make != "send")
                + [((tokens + 2 * steps + below[q], counts[q] * width), BF16)] * (make != "keep"),
                middle[q],
                *inputs_of(q),
                rows["own"],
                rows["cc"],
                rows["near_cc"],
                *([far_kv] if q == 1 else []),
                *([total, rows["near_total"]] if q == 0 else [rows["later"]]),
                after=(mark,),
                cost=SECOND_COST,
            )
            if q == 0:
                rows["later"], *results = results
            if make != "keep":
                outer[q] = to_neighbour(results[-1])
            if make != "send":
                carried[q], cands[q] = results[:2]
            return results[0]

        def third(q, mark):
            final = q == CHUNKS - 1
            results = call(
                functools.partial(third_kernel, q=q, **shared),
                "third",
                [((steps, wide), F32), ((steps, wide), BF16)]
                if final
                else ([((8, wide), F32)] if q == 0 else []) + [((2 * steps, counts[q] * width), F32)],
                outer[q],
                cands[q],
                rows["own"],
                *([] if q == 0 else [rows["outer"]]),
                *(raws if final else []),
                after=(mark,),
                cost=THIRD_COST,
            )
            if q == 0:
                rows["outer"], *results = results
            if final:
                return results
            raws.append(results[0])
            return results[0]

        def prefix(start, count, mark, into):
            span = range(start, start + count)
            return call(
                functools.partial(prefix_kernel, first=sum(counts[:start]) * width, tokens=tokens),
                "prefix",
                [((8, 128), F32)] if start == 0 else [],
                *[each[q] for each in (outer, carried, base, fade) for q in span],
                after=(mark,),
                into=(into,),
                scratch=[
                    pltpu.VMEM((tokens, sum(counts[start : start + count]) * width), BF16),
                    pltpu.SemaphoreType.DMA((1,)),
                ],
            )

        *base, loads[1] = intra(cc, cc)
        got = [to_neighbour(a) for a in loads[:2]]
        mark = first(0, base[0])
        mark = first(1, mark)
        far_kv = between_inner(rows["kv"])
        mark = second(0, mark)
        mark = first(2, mark)
        mark = second(1, mark)
        mark = first(3, mark)
        *fade, cand_base, cand_fade = candidates(mark, cum)
        mark = third(0, cand_base)
        mark = second(2, mark)
        mark = third(1, mark)
        mark, finish_attend = attend(mark, [rows["kv"], far_kv, outer[1]], True)
        mark = second(3, mark, "send")
        mark = second(3, mark, "keep")
        mark, cand_attn = finish_attend(mark)
        mark = third(2, mark)
        mark, prefix_out = prefix(0, CHUNKS - 1, mark, (prefix_x.shape, BF16))
        keep, give = third(3, mark)
        (prefix_out,) = prefix(CHUNKS - 1, 1, keep, prefix_out)
    else:
        got = [to_neighbour(a) for a in loads]
        halves = [kv, got[1][:, -kv_shape[1] :]]
        for level in range(1, levels):
            mirrored = to_mirror(halves[0], level)
            halves = [halves[0], halves[1], mirrored, to_neighbour(mirrored)]
            if level < levels - 1:
                halves = [jnp.concatenate([halves[0], halves[2]]), jnp.concatenate([halves[1], halves[3]])]
        *base, loads[1] = intra(cc, cc)
        mark = base[0]
        own = call(
            functools.partial(own_kernel, cols=cols, groups=groups, state=state, counts=counts),
            "own",
            [((state, cols), F32)] * CHUNKS,
            *loads,
        )
        own, start = dict(enumerate(own)), {}
        before = None
        near, far = {}, {}
        outs, raws = [], []
        for level in range(levels):
            last = level == levels - 1
            rows = None
            for q in range(CHUNKS):
                final = last and q == CHUNKS - 1
                if level == 0:
                    args, lines = [got[q], got[first_of[group_of[q]]]], got[0]
                else:
                    args, lines = [near[q], far[q]], near[0]
                shapes = []
                if q == 0:
                    args += [total, lines] + ([] if level == 0 else [before])
                    shapes += [((8, wide), F32)] * 2 + [((8, heads), F32)] * 2
                else:
                    args += rows
                args += [own[q]] + ([] if level == 0 else [start[q]])
                if final:
                    args += [cc, base[q], cum] + outs + raws
                    shapes = [((tokens, wide), BF16), ((steps, wide), F32), ((steps, wide), BF16)]
                elif last:
                    args += [cc, base[q], cum]
                    shapes += [((tokens, cols), BF16), ((2 * steps, cols), F32)]
                else:
                    shapes += [((state, cols), F32)] * 2 + [((state + (16 if q == 0 else 0), cols // 2), BF16)]
                results = call(
                    functools.partial(
                        merge_kernel, level=level, last=last, chunks=[q], groups=groups, state=state, **shared
                    ),
                    "merge",
                    shapes,
                    *args,
                    after=(mark,),
                )
                mark = results[0]
                if final:
                    prefix_out, keep, give = results
                    continue
                if q == 0:
                    rows, (total, before) = list(results[:2]), results[2:4]
                if last:
                    outs.append(results[-2])
                    raws.append(results[-1])
                else:
                    own[q], start[q] = results[-3], results[-2]
                    near[q] = to_mirror(results[-1], level + 1)
                    far[q] = to_neighbour(near[q])
            if level == 0:
                cand_base, cand_fade = candidates(mark)
                pieces = ([halves[0][tokens:]] if levels > 2 else []) + halves[1:]
                mark, finish_attend = attend(cand_base, pieces, False)
                mark, cand_attn = finish_attend(mark)
    (cand_ssm,) = call(
        close_kernel,
        "close",
        [((1, steps, cand_wide), BF16)],
        cand_length,
        cand_base,
        cand_fade,
        keep,
        to_core(give),
        scalars=1,
    )
    return (prefix_out, cand_ssm, cand_attn)


def solution(mesh):
    placed = (
        P(("groups", "seq"), ("head", "rep")),
        P(("groups", "seq"), ("head", "rep"), None),
        P(("groups", "seq"), ("head", "rep"), None),
        P(("groups", "seq"), ("head", "rep")),
        P(),
        P(("groups", "seq"), "head", None),
        P(("groups", "seq"), "head", None),
        P(("groups", "seq", "rep"), None, "head"),
        P(("groups", "seq", "rep"), None, "head", None),
        P(("groups", "seq", "rep"), None, "head", None),
        P(("groups", "seq", "rep"), None, "head"),
        P(("groups", "seq", "rep"), None, "head", None),
        P(("groups", "seq", "rep"), None, "head", None),
        P(("groups", "seq", "rep"), None, "head", None),
        P(("groups", "seq", "rep")),
    )
    return jax.shard_map(
        on_device,
        mesh=mesh,
        in_specs=placed,
        out_specs=(
            P(("groups", "seq"), ("head", "rep")),
            P(("groups", "seq", "rep"), None, "head"),
            P(("groups", "seq", "rep"), None, "head", None),
        ),
        check_vma=False,
    )
```

```python
import functools

import jax
import jax.numpy as jnp
from jax import lax
from jax.experimental import pallas as pl
from jax.experimental.pallas import tpu as pltpu
from jax.sharding import PartitionSpec as P

EPSILON = 1e-06
NEG = -1e30
LARGEST = 3.38e38
CHUNKS = 4
PARTS = (8, 8, 8, 8)
SECOND_COST = 1.0
FIRST_COST = 1.0
THIRD_COST = 0.3
F32 = jnp.float32
BF16 = jnp.bfloat16


def mm(a, b):
    return lax.dot_general(a, b, (((1,), (0,)), ((), ())), preferred_element_type=F32)


def mm_nt(a, b):
    return lax.dot_general(a, b, (((1,), (1,)), ((), ())), preferred_element_type=F32)


def mm_tn(a, b):
    return lax.dot_general(a, b, (((0,), (0,)), ((), ())), preferred_element_type=F32)


def exact_nt(a, b):
    return lax.dot_general(
        a, b, (((1,), (1,)), ((), ())), preferred_element_type=F32, precision=lax.Precision.HIGHEST
    )


def exact(a, b):
    return lax.dot_general(
        a, b, (((1,), (0,)), ((), ())), preferred_element_type=F32, precision=lax.Precision.HIGHEST
    )


def iota(shape, dim):
    return lax.broadcasted_iota(jnp.int32, shape, dim)


def split3(a):
    hi = jnp.clip(a, -LARGEST, LARGEST).astype(BF16)
    rest = a - hi.astype(F32)
    mid = rest.astype(BF16)
    return hi, mid, (rest - mid.astype(F32)).astype(BF16)


def spread(a, width, first=0, count=None):
    rows, cols = a.shape
    count = cols if count is None else count
    parts = jnp.concatenate(split3(a), axis=1)
    shape = (3 * cols, count * width)
    source = iota(shape, 0)
    source = jnp.where(source >= 2 * cols, source - 2 * cols, jnp.where(source >= cols, source - cols, source))
    unit = (source == first + iota(shape, 1) // width).astype(F32).astype(BF16)
    return mm(parts, unit)


def group_of(array, g):
    return array.astype(F32)[:, g, :].astype(BF16)


def cut(heads, size):
    if size == 4 and heads % sum(PARTS) == 0:
        return tuple(heads // sum(PARTS) * part for part in PARTS)
    return (heads // CHUNKS,) * CHUNKS


def groups_of(groups, counts):
    of = [sum(counts[:q]) * groups // sum(counts) for q in range(CHUNKS)]
    return of, {g: of.index(g) for g in of}


def columns(q, counts, width):
    return slice(sum(counts[:q]) * width, sum(counts[: q + 1]) * width)


def payload_plan(groups, counts):
    of, first_of = groups_of(groups, counts)
    return [[g] if first_of[g] == q else [] for q, g in enumerate(of)]


def totals_to_lines(total):
    hi, mid, lo = [a.astype(F32) for a in split3(jnp.broadcast_to(total, (16, total.shape[1])))]
    line = iota(hi.shape, 0)
    return jnp.where(line == 0, hi, jnp.where(line == 1, mid, jnp.where(line == 2, lo, 0.0))).astype(BF16)


def lines_to_totals(lines):
    lines = lines.astype(F32)
    return lines[0:1] + lines[1:2] + lines[2:3]


def as_row(total, width):
    return spread(jnp.broadcast_to(total, (8, total.shape[1])), width)


def pack(k_ref, v_ref):
    rep = lax.axis_index("rep")
    kv = jnp.where(rep == 0, k_ref[...].astype(F32), v_ref[...].astype(F32))
    return jnp.concatenate([kv[:, j, :] for j in range(kv.shape[1])], axis=1).astype(BF16)


def inputs_kernel(x_any, b_any, decay_t_any, k_any, v_any, cum_ref, total_ref, b2_ref, kv_ref, *refs, counts):
    load_refs, (x_ref, b_ref, decay_t_ref, k_ref, v_ref, sems) = refs[:-6], refs[-6:]
    pairs = ((decay_t_any, decay_t_ref), (b_any, b_ref), (x_any, x_ref), (k_any, k_ref), (v_any, v_ref))
    copies = [pltpu.make_async_copy(source, target, sems.at[i]) for i, (source, target) in enumerate(pairs)]
    for copy in copies:
        copy.start()
    tokens, groups, state = b_ref.shape
    heads = decay_t_ref.shape[0]
    width = x_ref.shape[1] // heads
    copies[0].wait()
    lower = (iota((tokens, tokens), 0) >= iota((tokens, tokens), 1)).astype(F32)
    cum = exact_nt(lower, decay_t_ref[...])
    cum_ref[...] = cum
    last = cum[tokens - 1 : tokens, :]
    total = jnp.exp(-last)
    total_ref[...] = jnp.broadcast_to(total, (8, heads))
    load_refs[0][tokens:, :] = jnp.zeros((16, load_refs[0].shape[1]), BF16)
    load_refs[0][tokens:, :heads] = totals_to_lines(total)
    weights = spread(jnp.exp(last - cum), width)
    for copy in copies[1:]:
        copy.wait()
    b = b_ref[...].astype(F32)
    for g in range(groups):
        b2_ref[:, g * state : (g + 1) * state] = b[:, g, :].astype(BF16)
    kv = pack(k_ref, v_ref)
    kv_ref[...] = kv
    for q, (fresh, load) in enumerate(zip(payload_plan(groups, counts), load_refs)):
        at = columns(q, counts, width)
        cols = counts[q] * width
        load[:tokens, :cols] = (x_ref[:, at].astype(F32) * weights[:, at]).astype(BF16)
        if fresh:
            load[:tokens, cols : cols + state] = b2_ref[:, fresh[0] * state : (fresh[0] + 1) * state]
        if q == 1:
            load[:, load.shape[1] - kv.shape[1] :] = kv


def own_kernel(*refs, cols, groups, state, counts):
    load_refs, out_refs = refs[:CHUNKS], refs[CHUNKS:]
    tokens = load_refs[1].shape[0]
    of, first_of = groups_of(groups, counts)
    for q in range(CHUNKS):
        b_ref = load_refs[first_of[of[q]]]
        out_refs[q][...] = mm_tn(b_ref[:tokens, cols : cols + state], load_refs[q][:tokens, :cols])


def collect_kernel(*refs, inner):
    refs, out_ref = list(refs[:-1]), refs[-1]
    place = lax.axis_index("seq")
    pieces = [ref[...] for ref in refs]
    if inner:
        pair, far, outer = pieces
        rows, wide = far.shape
        count = outer.shape[1] // wide
        first = outer.shape[0] - rows // count
        outer = jnp.concatenate([outer[first:, i * wide : (i + 1) * wide] for i in range(count)], axis=0)
        pieces = [pair[pair.shape[0] // 2 :], jnp.where((place == 1) | (place == 2), far, outer)]
    at = 0
    for piece in pieces:
        out_ref[at : at + piece.shape[0], :] = piece
        at += piece.shape[0]


def half_of(place, level):
    odd = lax.rem(place, 2)
    return jnp.where(lax.rem(lax.div(place, 2**level), 2) == 0, 1 - odd, odd)


def merge_kernel(*refs, level, last, chunks, cols, groups, heads, tokens, state):
    refs = list(refs)

    def take(count):
        taken = refs[:count]
        del refs[:count]
        return taken

    place = lax.axis_index("seq")
    right = lax.rem(lax.div(place, 2**level), 2) == 1
    width = cols * CHUNKS // heads
    first = 0 in chunks
    outs = []
    others = []
    if level == 0:
        for q in chunks:
            w_ref, b_ref = take(2)
            others.append(mm_tn(b_ref[:tokens, cols : cols + state], w_ref[:tokens, :cols]))
    else:
        half = half_of(place, level)
        for q in chunks:
            near_ref, far_ref = take(2)
            rows = near_ref.shape[0] - 16 if q == 0 else near_ref.shape[0]
            near, far = near_ref[:rows, :], far_ref[:rows, :]
            pieces = [jnp.where(half == 0, near, far), jnp.where(half == 0, far, near)]
            others.append(jnp.concatenate(pieces, axis=1).astype(F32))
    if first:
        mine_ref, lines_ref = take(2)
        mine = mine_ref[:1, :]
        theirs = lines_to_totals(lines_ref[lines_ref.shape[0] - 16 :, :heads])
        later = as_row(jnp.where(right, mine, theirs), width)
        pair = mine * theirs
        if level == 0:
            before = jnp.ones_like(mine)
        else:
            before = take(1)[0][:1, :]
        before_row = as_row(before, width)
        before = jnp.where(right, before * theirs, before)
        outs += [later, before_row, jnp.broadcast_to(pair, (8, heads)), jnp.broadcast_to(before, (8, heads))]
    else:
        later_ref, before_ref = take(2)
        later, before_row = later_ref[...], before_ref[...]
    for q, other in zip(chunks, others, strict=True):
        at = slice(q * cols, (q + 1) * cols)
        own = take(1)[0][...]
        earlier, following = jnp.where(right, other, own), jnp.where(right, own, other)
        joined = later[:1, at] * earlier + following
        if level == 0:
            start = jnp.where(right, other, 0.0)
        else:
            start = take(1)[0][...]
            start = jnp.where(right, before_row[:1, at] * other + start, start)
        if not last:
            send = jnp.where(half_of(place, level + 1) == 0, joined[:, : cols // 2], joined[:, cols // 2 :]).astype(BF16)
            if q == 0:
                tail = jnp.zeros((16, cols // 2 - heads), BF16)
                lines = jnp.concatenate([totals_to_lines(pair), tail], axis=1)
                send = jnp.concatenate([send, lines], axis=0)
            outs += [joined, start, send]
        else:
            cc_ref, base_ref, cum_ref = take(3)
            g = q * groups // CHUNKS
            here = slice(g * state, (g + 1) * state)
            fade = spread(jnp.exp(-cum_ref[...]), width, q * heads // CHUNKS, heads // CHUNKS)
            carried = mm(cc_ref[:tokens, here], start.astype(BF16))
            outs.append((base_ref[...] + fade * carried).astype(BF16))
            outs.append(mm(cc_ref[tokens:, here], joined.astype(BF16)))
    if last and CHUNKS - 1 in chunks:
        parts = take(2 * (CHUNKS - 1))
        out_parts = [ref[...] for ref in parts[: CHUNKS - 1]] + [outs[-2]]
        raws = [ref[...] for ref in parts[CHUNKS - 1 :]] + [outs[-1]]
        rep = lax.axis_index("rep")
        out_ref, keep_ref, give_ref = refs
        rows = keep_ref.shape[0]
        for q in range(CHUNKS):
            at = slice(q * cols, (q + 1) * cols)
            out_ref[:, at] = out_parts[q]
            keep_ref[:, at] = jnp.where(rep == 0, raws[q][:rows], raws[q][rows:])
            give_ref[:, at] = jnp.where(rep == 0, raws[q][rows:], raws[q][:rows]).astype(BF16)
    else:
        for ref, value in zip(refs, outs, strict=True):
            ref[...] = value


def projections_kernel(c_ref, mine_ref, other_ref, out_ref):
    rep = lax.axis_index("rep")
    tokens, groups, state = c_ref.shape
    steps = mine_ref.shape[1]
    mine, other = mine_ref[0].astype(F32), other_ref[0].astype(F32)
    zero, one = jnp.where(rep == 0, mine, other), jnp.where(rep == 0, other, mine)
    prefix = c_ref[...].astype(F32)
    for g in range(groups):
        at = slice(g * state, (g + 1) * state)
        out_ref[:tokens, at] = prefix[:, g, :].astype(BF16)
        for i, c in enumerate((zero, one)):
            part = jnp.where(rep == 0, c[:, g, :], c[:, groups + g, :])
            out_ref[tokens + i * steps : tokens + (i + 1) * steps, at] = part.astype(BF16)


def first_kernel(*refs, q, counts, width, groups, heads, tokens, state):
    refs = list(refs)
    w_ref, b_ref, own_w_ref, own_b_ref = refs[:4]
    refs = refs[4:]
    left = lax.axis_index("seq") < 2
    cols = counts[q] * width
    of, first_of = groups_of(groups, counts)
    at_b = slice(counts[first_of[of[q]]] * width, counts[first_of[of[q]]] * width + state)
    other = mm_tn(b_ref[:tokens, at_b], w_ref[:tokens, :cols])
    if q == 0:
        mine_ref, own_row_ref, near_row_ref, near_ref, send_ref = refs
        mine = mine_ref[:1, :]
        near = lines_to_totals(w_ref[tokens:, :heads])
        own_row, near_row = own_row_ref[...], as_row(near, width)
        near_row_ref[...] = near_row
        near_ref[...] = jnp.broadcast_to(near, (8, heads))
        send_ref[state:, :] = jnp.zeros((16, cols), BF16)
        send_ref[state:, :heads] = totals_to_lines(mine * near)
    else:
        own_row_ref, near_row_ref = refs[:2]
        refs = refs[2:]
        if q == 1:
            kv_ref, pair_ref = refs[0], refs.pop()
            refs = refs[1:]
            pair_ref[:tokens, :] = kv_ref[...]
            pair_ref[tokens:, :] = w_ref[:, w_ref.shape[1] - kv_ref.shape[1] :]
        (send_ref,) = refs
        own_row, near_row = own_row_ref[...], near_row_ref[...]
    at = columns(q, counts, width)
    local = mm_tn(own_b_ref[:tokens, at_b], own_w_ref[:tokens, :cols])
    after = own_row[:1, at] * other + local
    beyond = other + near_row[:1, at] * local
    send_ref[:state, :] = jnp.where(left, after, beyond).astype(BF16)


def second_kernel(*refs, q, counts, width, groups, heads, tokens, state, make):
    refs = list(refs)
    got_ref, w_ref, b_ref, own_w_ref, own_b_ref, own_row_ref, cc_ref, near_cc_ref = refs[:8]
    refs = refs[8:]
    if make == "send":
        refs[-1:] = [None, None, refs[-1]]
    elif make == "keep":
        refs.append(None)
    place = lax.axis_index("seq")
    left, inner = place < 2, (place == 1) | (place == 2)
    cols = counts[q] * width
    at = columns(q, counts, width)
    of, first_of = groups_of(groups, counts)
    at_b = slice(counts[first_of[of[q]]] * width, counts[first_of[of[q]]] * width + state)
    here = slice(of[q] * state, (of[q] + 1) * state)
    rows = cc_ref.shape[0]
    if q == 0:
        mine_ref, near_ref, later_row_ref, carried_ref, cand_ref, send_ref = refs
        later = jnp.where(left, lines_to_totals(got_ref[state:, :heads]), near_ref[:1, :])
        later_row = as_row(later, width)
        later_row_ref[...] = later_row
        send_ref[rows:, :] = jnp.zeros((16, cols), BF16)
        send_ref[rows:, :heads] = totals_to_lines(later * mine_ref[:1, :])
    else:
        if q == 1:
            kv_ref = refs.pop(0)
            held = kv_ref.shape[0] // (cols // kv_ref.shape[1])
            for i in range(cols // kv_ref.shape[1]):
                part = slice(i * kv_ref.shape[1], (i + 1) * kv_ref.shape[1])
                refs[-1][rows:, part] = kv_ref[i * held : (i + 1) * held, :]
        later_row_ref, carried_ref, cand_ref, send_ref = refs
        later_row = later_row_ref[...]
    got = got_ref[:state, :].astype(F32)
    other = mm_tn(b_ref[:tokens, at_b], w_ref[:tokens, :cols])
    local = mm_tn(own_b_ref[:tokens, at_b], own_w_ref[:tokens, :cols])
    start, beyond = jnp.where(left, other, got), jnp.where(left, got, other)
    start = jnp.where(inner, start, 0.0)
    after = own_row_ref[:1, at] * start + local
    lasting = later_row[:1, at]
    if make != "keep":
        state_out = jnp.where(left, beyond + lasting * local, after)
        send_ref[:rows, :] = mm(near_cc_ref[:, here], state_out.astype(BF16)).astype(BF16)
    if make == "send":
        return
    final = jnp.where(inner, lasting * after + beyond, local)
    carried_ref[...] = mm(cc_ref[:tokens, here], start.astype(BF16))
    cand_ref[...] = mm(cc_ref[tokens:, here], final.astype(BF16))


def third_kernel(*refs, q, counts, width, heads, tokens):
    refs = list(refs)
    got_ref, cand_ref, own_row_ref = refs[:3]
    place = lax.axis_index("seq")
    at = columns(q, counts, width)
    rows = cand_ref.shape[0]
    refs = refs[3:]
    if q == 0:
        later_row_ref = refs[0]
        later_row = as_row(lines_to_totals(got_ref[tokens + rows :, :heads]), width)
        later_row_ref[...] = later_row
    else:
        later_row = refs[0][...]
    refs = refs[1:]
    cand = cand_ref[...]
    got = got_ref[tokens : tokens + rows, :].astype(F32)
    cand = jnp.where(
        place == 3,
        own_row_ref[:1, at] * got + cand,
        jnp.where(place == 0, later_row[:1, at] * cand + got, cand),
    )
    if q < CHUNKS - 1:
        (raw_ref,) = refs
        raw_ref[...] = cand
        return
    raws, (keep_ref, give_ref) = refs[:-2], refs[-2:]
    rep = lax.axis_index("rep")
    half = rows // 2
    for i in range(CHUNKS):
        at = columns(i, counts, width)
        raw = cand if i == q else raws[i][...]
        keep_ref[:, at] = jnp.where(rep == 0, raw[:half], raw[half:])
        give_ref[:, at] = jnp.where(rep == 0, raw[half:], raw[:half]).astype(BF16)


def prefix_kernel(*refs, first, tokens):
    refs, (out_any, buffer, sem) = refs[:-3], refs[-3:]
    last = lax.axis_index("seq") == 3
    count = len(refs) // 4
    if len(refs) % 4:
        refs[-1][...] = jnp.zeros(refs[-1].shape, F32)
        refs = refs[:-1]
    at = 0
    for i in range(count):
        got_ref, carried_ref, base_ref, fade_ref = refs[i::count]
        carried = jnp.where(last, got_ref[:tokens, :].astype(F32), carried_ref[...])
        buffer[:, at : at + base_ref.shape[1]] = (base_ref[...] + fade_ref[...] * carried).astype(BF16)
        at += base_ref.shape[1]
    copy = pltpu.make_async_copy(buffer, out_any.at[:, pl.ds(first, at)], sem.at[0])
    copy.start()
    copy.wait()


def intra_kernel(x_ref, b2_ref, c2_ref, cum_ref, skip_ref, *refs, groups):
    *base_refs, row_ref = refs
    tokens, heads = cum_ref.shape
    width = x_ref.shape[1] // heads
    state = c2_ref.shape[1] // groups
    per_group = heads // groups
    first = (lax.axis_index("head") * lax.axis_size("rep") + lax.axis_index("rep")) * heads
    skip = spread(jnp.broadcast_to(skip_ref[...], (8, skip_ref.shape[1])), width, first, heads)[:1]
    cum = cum_ref[...]
    row_ref[...] = as_row(jnp.exp(-cum[tokens - 1 : tokens, :]), width)
    cum_t = cum.T
    shape = (tokens, tokens)
    hidden = jnp.where(iota(shape, 0) >= iota(shape, 1), 0.0, NEG)
    pair = 2 * width
    lane = iota((tokens, pair), 1)
    for g in range(groups):
        here = slice(g * state, (g + 1) * state)
        gram = mm_nt(c2_ref[:tokens, here], b2_ref[:, here])
        for h in range(g * per_group, (g + 1) * per_group, 2):
            mixing = []
            for i in (h, h + 1):
                gap = cum_t[i : i + 1, :] - jnp.broadcast_to(cum[:, i : i + 1], shape)
                mixing.append((jnp.exp(gap + hidden) * gram).astype(BF16))
            at = slice(h * width, (h + 2) * width)
            x = x_ref[:, at]
            zero = jnp.zeros_like(x)
            inputs = jnp.concatenate(
                [jnp.where(lane < width, x, zero), jnp.where(lane < width, zero, x)], axis=0
            )
            q, start = 0, h * width
            while start >= base_refs[q].shape[1]:
                start -= base_refs[q].shape[1]
                q += 1
            base_refs[q][:, start : start + pair] = (
                mm(jnp.concatenate(mixing, axis=1), inputs) + skip[:, at] * x.astype(F32)
            )


def cand_kernel(x_ref, b_ref, c_ref, decay_ref, skip_ref, *refs):
    if len(refs) > 2:
        cum_ref, *fall_refs = refs[:-2]
        fall = spread(jnp.exp(-cum_ref[...]), sum(ref.shape[1] for ref in fall_refs) // cum_ref.shape[1])
        at = 0
        for ref in fall_refs:
            ref[...] = fall[:, at : at + ref.shape[1]]
            at += ref.shape[1]
    base_ref, fade_ref = refs[-2:]
    steps, groups, state = b_ref.shape[1:]
    heads = decay_ref.shape[2]
    width = x_ref.shape[2] // heads
    per_group = heads // groups
    first = lax.axis_index("head") * heads
    skip = spread(jnp.broadcast_to(skip_ref[...], (8, skip_ref.shape[1])), width, first, heads)[:1]
    lower = (iota((steps, steps), 0) >= iota((steps, steps), 1)).astype(F32)
    cum = exact(lower, decay_ref[0])
    fade_ref[...] = spread(jnp.exp(-cum), width)
    wide = (steps, heads * steps)
    cum_t = spread(cum, steps)
    place = iota(wide, 1) % steps
    row = iota(wide, 0)
    cum_s = jnp.sum(jnp.where(row == place, cum_t, 0.0), axis=0, keepdims=True)
    fall = jnp.exp(jnp.where(row >= place, cum_s - cum_t, NEG))
    b = b_ref[0].astype(F32)
    c = c_ref[0].astype(F32)
    quad = 128 // steps
    shape = (quad * steps, quad * width)
    mine = iota(shape, 0) // steps == iota(shape, 1) // width
    for g in range(groups):
        b_g = b[:, g, :].astype(BF16)
        gram = mm_nt(c[:, g, :].astype(BF16), jnp.concatenate([b_g] * quad, axis=0))
        for h in range(g * per_group, (g + 1) * per_group, quad):
            mixing = (fall[:, h * steps : (h + quad) * steps] * gram).astype(BF16)
            at = slice(h * width, (h + quad) * width)
            x = x_ref[0, :, at]
            tall = jnp.concatenate([x] * quad, axis=0)
            inputs = jnp.where(mine, tall, jnp.zeros_like(tall))
            base_ref[:, at] = mm(mixing, inputs) + skip[:, at] * x.astype(F32)


def attend_kernel(length_ref, q_ref, own_k_ref, own_v_ref, k_ref, v_ref, mine_ref, other_ref, mark_ref, out_any, out_ref, sem):
    mark_ref[...] = jnp.zeros(mark_ref.shape, F32)
    rep = lax.axis_index("rep")
    steps, heads, dim = q_ref.shape[1:]
    kv_heads = own_k_ref.shape[2]
    per_kv = heads // kv_heads
    rows = steps * per_kv
    mine, other = mine_ref[...], other_ref[...]
    keys, values = jnp.where(rep == 0, mine, other), jnp.where(rep == 0, other, mine)
    q = q_ref[0].astype(F32)
    own_k = own_k_ref[0].astype(F32)
    own_v = own_v_ref[0].astype(F32)
    block_k = k_ref[...].astype(F32)
    block_v = v_ref[...].astype(F32)
    scale = dim ** (-0.5)
    step_of = iota((rows, steps), 0) // per_kv
    visible = step_of >= iota((rows, steps), 1)
    live = iota((rows, dim), 0) // per_kv < length_ref[0]
    mixed_of = []
    for j in range(kv_heads):
        query = q[:, j * per_kv : (j + 1) * per_kv, :].reshape(rows, dim).astype(BF16)

        def gather(far, block):
            return jnp.concatenate([far[:, j * dim : (j + 1) * dim], block[:, j, :].astype(BF16)], axis=0)

        far = mm_nt(query, gather(keys, block_k)) * scale
        near = jnp.where(visible, mm_nt(query, own_k[:, j, :].astype(BF16)) * scale, NEG)
        top = jnp.maximum(jnp.max(far, axis=1, keepdims=True), jnp.max(near, axis=1, keepdims=True))
        far = jnp.exp(far - top)
        near = jnp.exp(near - top)
        mass = jnp.sum(far, axis=1, keepdims=True) + jnp.sum(near, axis=1, keepdims=True)
        mixed = mm(far.astype(BF16), gather(values, block_v)) + mm(near.astype(BF16), own_v[:, j, :].astype(BF16))
        mixed = mixed / mass
        mixed = mixed * lax.rsqrt(jnp.mean(mixed * mixed, axis=1, keepdims=True) + EPSILON)
        mixed = jnp.where(live, mixed, 0.0)
        mixed_of.append(mixed.reshape(steps, per_kv, dim))
    out_ref[0] = (jnp.concatenate(mixed_of, axis=1) if kv_heads > 1 else mixed_of[0]).astype(BF16)
    copy = pltpu.make_async_copy(out_ref, out_any, sem.at[0])
    copy.start()
    copy.wait()


def close_kernel(length_ref, base_ref, fade_ref, keep_ref, got_ref, out_ref):
    rep = lax.axis_index("rep")
    keep, got = keep_ref[...], got_ref[...].astype(F32)
    cols = keep.shape[1]
    live = iota(keep.shape, 0) < length_ref[0]
    for i in range(2):
        at = slice(i * cols, (i + 1) * cols)
        carried = jnp.where(rep == i, keep, got)
        result = base_ref[:, at] + fade_ref[:, at] * carried
        out_ref[0, :, at] = jnp.where(live, result, 0.0).astype(BF16)


def call(kernel, name, outs, *args, scalars=0, after=(), cost=0.0, scratch=(), limit=32, gate=(), into=(), raw=False):
    shapes = [jax.ShapeDtypeStruct(shape, dtype) for shape, dtype in outs]
    vmem = pl.BlockSpec(memory_space=pltpu.VMEM)
    smem = pl.BlockSpec(memory_space=pltpu.SMEM)
    anywhere = pl.BlockSpec(memory_space=pl.ANY)
    given = [a for a in into if hasattr(a, "dtype")]
    passed = [*gate, *given]
    count = len(args)
    rest = count + len(after) + len(passed)
    through = rest + len(shapes)
    shapes += [jax.ShapeDtypeStruct(a.shape, a.dtype) for a in gate]
    shapes += [jax.ShapeDtypeStruct(a.shape, a.dtype) if hasattr(a, "dtype") else jax.ShapeDtypeStruct(*a) for a in into]
    aliases = {count + len(after) + i: len(outs) + i for i in range(len(passed))}

    def body(*refs):
        kernel(*refs[:count], *refs[rest:through], *refs[through + len(gate) :])

    return pl.pallas_call(
        body,
        out_shape=shapes,
        in_specs=[smem] * scalars
        + [anywhere if raw else vmem] * (count - scalars)
        + [anywhere] * (len(after) + len(passed)),
        out_specs=[vmem] * len(outs) + [anywhere] * (len(gate) + len(into)),
        input_output_aliases=aliases,
        scratch_shapes=list(scratch),
        compiler_params=pltpu.CompilerParams(vmem_limit_bytes=limit * 2**20),
        cost_estimate=pl.CostEstimate(flops=int(cost * 10**9), bytes_accessed=0, transcendentals=0),
        name=name,
    )(*args, *after, *passed)


def on_device(
    prefix_x,
    prefix_b,
    prefix_c,
    prefix_decay,
    bypass_weight,
    prefix_key_rows,
    prefix_values,
    cand_x,
    cand_b,
    cand_c,
    cand_decay,
    cand_queries,
    cand_keys,
    cand_values,
    cand_length,
):
    size = lax.axis_size("seq")
    levels = size.bit_length() - 1
    assert size == 2**levels and lax.axis_size("rep") == 2
    tokens, groups, state = prefix_b.shape
    heads = prefix_decay.shape[1]
    wide = prefix_x.shape[1]
    steps = cand_x.shape[1]
    cand_wide = cand_x.shape[2]
    cols = wide // CHUNKS
    skip = bypass_weight.reshape(1, -1)
    counts = cut(heads, size)
    width = wide // heads
    plan = payload_plan(groups, counts)

    def to_core(array):
        return lax.ppermute(array, "rep", [(0, 1), (1, 0)])

    def to_neighbour(array):
        return lax.ppermute(array, "seq", [(i, i ^ 1) for i in range(size)])

    def to_mirror(array, level):
        return lax.ppermute(array, "seq", [(i, i ^ (2 ** (level + 1) - 1)) for i in range(size)])

    def between_inner(array):
        far = {1: 2, 2: 1}
        pairs = [(2 * i + r, 2 * far[i] + r if i in far else 2 * i + 1 - r) for i in range(size) for r in range(2)]
        return lax.ppermute(array, ("seq", "rep"), pairs)

    def inward(array):
        return lax.ppermute(array, "seq", [(0, 1), (3, 2)])

    other_c = to_core(cand_c)
    kv_shape = (tokens, prefix_key_rows.shape[1] * prefix_key_rows.shape[2])
    cum, total, b2, kv, *loads = call(
        functools.partial(inputs_kernel, counts=counts),
        "inputs",
        [((tokens, heads), F32), ((8, heads), F32), ((tokens, groups * state), BF16), (kv_shape, BF16)]
        + [
            (
                (
                    tokens + (16 if q == 0 else 0),
                    counts[q] * width + len(fresh) * state + (kv_shape[1] if q == 1 else 0),
                ),
                BF16,
            )
            for q, fresh in enumerate(plan)
        ],
        prefix_x,
        prefix_b,
        prefix_decay.T,
        prefix_key_rows,
        prefix_values,
        scratch=[
            pltpu.VMEM(prefix_x.shape, BF16),
            pltpu.VMEM(prefix_b.shape, BF16),
            pltpu.VMEM((heads, tokens), F32),
            pltpu.VMEM(prefix_key_rows.shape, BF16),
            pltpu.VMEM(prefix_values.shape, BF16),
            pltpu.SemaphoreType.DMA((5,)),
        ],
        raw=True,
        limit=60,
    )
    (cc,) = call(
        projections_kernel,
        "projections",
        [((tokens + 2 * steps, groups * state), BF16)],
        prefix_c,
        cand_c,
        other_c,
        after=(cum,),
    )
    group_of, first_of = groups_of(groups, counts)
    def intra(mark, cc):
        return call(
            functools.partial(intra_kernel, groups=groups),
            "intra",
            [((tokens, count * width), F32) for count in counts] + [((8, wide), F32)],
            prefix_x,
            b2,
            cc,
            cum,
            skip,
            after=(mark,),
            gate=(loads[1],),
        )

    def candidates(mark, *more):
        return call(
            cand_kernel,
            "candidates",
            [((tokens, count * width), F32) for count in counts if more] + [((steps, cand_wide), F32), ((steps, cand_wide), F32)],
            cand_x,
            cand_b,
            cand_c,
            cand_decay,
            skip,
            *more,
            after=(mark,),
        )

    def attend(mark, pieces, inner):
        (mine,) = call(
            functools.partial(collect_kernel, inner=inner),
            "collect",
            [((tokens * (size - 1), kv_shape[1]), BF16)],
            *pieces,
            after=(mark,),
        )
        theirs = to_core(mine)

        def finish(mark):
            return call(
                attend_kernel,
                "attend",
                [((8, 128), F32)],
                cand_length,
                cand_queries,
                cand_keys,
                cand_values,
                prefix_key_rows,
                prefix_values,
                mine,
                theirs,
                scalars=1,
                after=(mark,),
                into=((cand_queries.shape, BF16),),
                scratch=[pltpu.VMEM(cand_queries.shape, BF16), pltpu.SemaphoreType.DMA((1,))],
            )

        return mine, finish

    shared = dict(cols=cols, heads=heads, tokens=tokens)
    if size == 4:
        shared = dict(counts=counts, width=width, heads=heads, tokens=tokens)
        mark = cc
        middle, carried, cands, outer, outs, raws = {}, {}, {}, {}, [], []
        rows = {"cc": cc}
        below = (16, 2 * tokens // (counts[1] * width // kv_shape[1]), 0, 0)

        def inputs_of(q):
            p = first_of[group_of[q]]
            return got[q], got[p], loads[q], loads[p]

        def first(q, mark):
            extra = [((8, wide), F32), ((8, heads), F32)] if q == 0 else []
            results = call(
                functools.partial(first_kernel, q=q, groups=groups, state=state, **shared),
                "first",
                extra
                + [((state + (16 if q == 0 else 0), counts[q] * width), BF16)]
                + ([((2 * tokens, kv_shape[1]), BF16)] if q == 1 else []),
                *inputs_of(q),
                *([total, rows["own"]] if q == 0 else [rows["own"], rows["near"]]),
                *([kv] if q == 1 else []),
                after=(mark,),
                cost=FIRST_COST if q == 1 else 0.0,
                gate=[(rows["cc"],), loads[2:], (), ()][q],
            )
            if q == 0:
                *results, rows["cc"] = results
                rows["near_cc"] = to_neighbour(rows["cc"])
            elif q == 1:
                *results, loads[2], loads[3] = results
                got.extend((to_neighbour(loads[2]), inward(loads[3])))
            if q == 0:
                rows["near"], rows["near_total"], *results = results
            middle[q] = between_inner(results[0])
            if q == 1:
                rows["kv"] = results[1]
            return results[0]

        def second(q, mark, make="all"):
            results = call(
                functools.partial(second_kernel, q=q, groups=groups, state=state, make=make, **shared),
                "second",
                ([((8, wide), F32)] if q == 0 else [])
                + [((tokens, counts[q] * width), F32), ((2 * steps, counts[q] * width), F32)] * (make != "send")
                + [((tokens + 2 * steps + below[q], counts[q] * width), BF16)] * (make != "keep"),
                middle[q],
                *inputs_of(q),
                rows["own"],
                rows["cc"],
                rows["near_cc"],
                *([far_kv] if q == 1 else []),
                *([total, rows["near_total"]] if q == 0 else [rows["later"]]),
                after=(mark,),
                cost=SECOND_COST,
            )
            if q == 0:
                rows["later"], *results = results
            if make != "keep":
                outer[q] = to_neighbour(results[-1])
            if make != "send":
                carried[q], cands[q] = results[:2]
            return results[0]

        def third(q, mark):
            final = q == CHUNKS - 1
            results = call(
                functools.partial(third_kernel, q=q, **shared),
                "third",
                [((steps, wide), F32), ((steps, wide), BF16)]
                if final
                else ([((8, wide), F32)] if q == 0 else []) + [((2 * steps, counts[q] * width), F32)],
                outer[q],
                cands[q],
                rows["own"],
                *([] if q == 0 else [rows["outer"]]),
                *(raws if final else []),
                after=(mark,),
                cost=THIRD_COST,
            )
            if q == 0:
                rows["outer"], *results = results
            if final:
                return results
            raws.append(results[0])
            return results[0]

        def prefix(start, count, mark, into):
            span = range(start, start + count)
            return call(
                functools.partial(prefix_kernel, first=sum(counts[:start]) * width, tokens=tokens),
                "prefix",
                [((8, 128), F32)] if start == 0 else [],
                *[each[q] for each in (outer, carried, base, fade) for q in span],
                after=(mark,),
                into=(into,),
                scratch=[
                    pltpu.VMEM((tokens, sum(counts[start : start + count]) * width), BF16),
                    pltpu.SemaphoreType.DMA((1,)),
                ],
            )

        *base, rows["own"], loads[1] = intra(cc, cc)
        got = [to_neighbour(a) for a in loads[:2]]
        mark = first(0, base[0])
        mark = first(1, mark)
        far_kv = between_inner(rows["kv"])
        mark = second(0, mark)
        mark = first(2, mark)
        mark = second(1, mark)
        mark = first(3, mark)
        *fade, cand_base, cand_fade = candidates(mark, cum)
        mark = third(0, cand_base)
        mark = second(2, mark)
        mark = third(1, mark)
        mark, finish_attend = attend(mark, [rows["kv"], far_kv, outer[1]], True)
        mark = second(3, mark, "send")
        mark = second(3, mark, "keep")
        mark, cand_attn = finish_attend(mark)
        mark = third(2, mark)
        mark, prefix_out = prefix(0, CHUNKS - 1, mark, (prefix_x.shape, BF16))
        keep, give = third(3, mark)
        (prefix_out,) = prefix(CHUNKS - 1, 1, keep, prefix_out)
    else:
        got = [to_neighbour(a) for a in loads]
        halves = [kv, got[1][:, -kv_shape[1] :]]
        for level in range(1, levels):
            mirrored = to_mirror(halves[0], level)
            halves = [halves[0], halves[1], mirrored, to_neighbour(mirrored)]
            if level < levels - 1:
                halves = [jnp.concatenate([halves[0], halves[2]]), jnp.concatenate([halves[1], halves[3]])]
        *base, _, loads[1] = intra(cc, cc)
        mark = base[0]
        own = call(
            functools.partial(own_kernel, cols=cols, groups=groups, state=state, counts=counts),
            "own",
            [((state, cols), F32)] * CHUNKS,
            *loads,
        )
        own, start = dict(enumerate(own)), {}
        before = None
        near, far = {}, {}
        outs, raws = [], []
        for level in range(levels):
            last = level == levels - 1
            rows = None
            for q in range(CHUNKS):
                final = last and q == CHUNKS - 1
                if level == 0:
                    args, lines = [got[q], got[first_of[group_of[q]]]], got[0]
                else:
                    args, lines = [near[q], far[q]], near[0]
                shapes = []
                if q == 0:
                    args += [total, lines] + ([] if level == 0 else [before])
                    shapes += [((8, wide), F32)] * 2 + [((8, heads), F32)] * 2
                else:
                    args += rows
                args += [own[q]] + ([] if level == 0 else [start[q]])
                if final:
                    args += [cc, base[q], cum] + outs + raws
                    shapes = [((tokens, wide), BF16), ((steps, wide), F32), ((steps, wide), BF16)]
                elif last:
                    args += [cc, base[q], cum]
                    shapes += [((tokens, cols), BF16), ((2 * steps, cols), F32)]
                else:
                    shapes += [((state, cols), F32)] * 2 + [((state + (16 if q == 0 else 0), cols // 2), BF16)]
                results = call(
                    functools.partial(
                        merge_kernel, level=level, last=last, chunks=[q], groups=groups, state=state, **shared
                    ),
                    "merge",
                    shapes,
                    *args,
                    after=(mark,),
                )
                mark = results[0]
                if final:
                    prefix_out, keep, give = results
                    continue
                if q == 0:
                    rows, (total, before) = list(results[:2]), results[2:4]
                if last:
                    outs.append(results[-2])
                    raws.append(results[-1])
                else:
                    own[q], start[q] = results[-3], results[-2]
                    near[q] = to_mirror(results[-1], level + 1)
                    far[q] = to_neighbour(near[q])
            if level == 0:
                cand_base, cand_fade = candidates(mark)
                pieces = ([halves[0][tokens:]] if levels > 2 else []) + halves[1:]
                mark, finish_attend = attend(cand_base, pieces, False)
                mark, cand_attn = finish_attend(mark)
    (cand_ssm,) = call(
        close_kernel,
        "close",
        [((1, steps, cand_wide), BF16)],
        cand_length,
        cand_base,
        cand_fade,
        keep,
        to_core(give),
        scalars=1,
    )
    return (prefix_out, cand_ssm, cand_attn)


def solution(mesh):
    placed = (
        P(("groups", "seq"), ("head", "rep")),
        P(("groups", "seq"), ("head", "rep"), None),
        P(("groups", "seq"), ("head", "rep"), None),
        P(("groups", "seq"), ("head", "rep")),
        P(),
        P(("groups", "seq"), "head", None),
        P(("groups", "seq"), "head", None),
        P(("groups", "seq", "rep"), None, "head"),
        P(("groups", "seq", "rep"), None, "head", None),
        P(("groups", "seq", "rep"), None, "head", None),
        P(("groups", "seq", "rep"), None, "head"),
        P(("groups", "seq", "rep"), None, "head", None),
        P(("groups", "seq", "rep"), None, "head", None),
        P(("groups", "seq", "rep"), None, "head", None),
        P(("groups", "seq", "rep")),
    )
    return jax.shard_map(
        on_device,
        mesh=mesh,
        in_specs=placed,
        out_specs=(
            P(("groups", "seq"), ("head", "rep")),
            P(("groups", "seq", "rep"), None, "head"),
            P(("groups", "seq", "rep"), None, "head", None),
        ),
        check_vma=False,
    )
```
